128 devices in a mesh: gx: 32 (over y, x, core), gy: 4 (over z).
Axes of the slice: x: 4, y: 4, z: 4, core: 2. Of those that a mesh axis runs over, the one named last changes fastest.
Arguments:
- head_start: float32 [32, 256, 512], P(None, 'gx', 'gy'), may hold values from -6 to -0.5
- sat_conduct: float32 [32, 256, 512], P(None, 'gx', 'gy'), may hold values from 0.5 to 5
- alpha_dry: float32 [32, 256, 512], P(None, 'gx', 'gy'), may hold values from 0.5 to 3
- wet_flag: int32 [32, 256, 512], P(None, 'gx', 'gy'), may hold values 0 or 1
- reversal_head: float32 [32, 256, 512], P(None, 'gx', 'gy'), may hold values from -8 to -1
- send_row: int32 [128, 9, 1024], P(('gx', 'gy')), may hold values from 0 to 255
- send_col: int32 [128, 9, 1024], P(('gx', 'gy')), may hold values from 0 to 127
- root_radial: float32 [16384, 128], P(('gx', 'gy')), may hold values from 0.02 to 0.2
- root_axial: float32 [16384, 128], P(('gx', 'gy')), may hold values from 1 to 10
- stem_link: float32 [16384], P(('gx', 'gy')), may hold values from 1 to 10
- entry_seg: int32 [16384], P(('gx', 'gy')), may hold values from 0 to 127
- source_dev: int32 [16384, 128], P(('gx', 'gy')), may hold values from 0 to 127, as said below
- source_slot: int32 [16384, 128], P(('gx', 'gy')), may hold values from 0 to 1023
- demand: float32 [2048], P(('gx', 'gy')), may hold values from 16 to 128
Outputs:
- head_end: float32 [32, 256, 512], P(None, 'gx', 'gy')
- collar_head: float32 [2048], P(('gx', 'gy'))
The draws below stay inside these ranges and needn't reach their ends.
Inputs may be any that keep to these rules, and one draw needn't show every extreme that they name: source_dev[b, i] is the device o = b // 128 that holds the block, or one of the eight devices whose tile coordinates differ from o's by at most 1 in each direction, periodically.
All inputs are finite; a program needn't handle non-finite values. No bound on the sum of `wet_flag` on one device may be relied on, other than what follows from the above.
Results may differ from the reference program's by a relative error of at most 0.0003.
Values sent between devices are 32-bit elements; how exact they have to be, the bound alone decides.
No kernel may reach another device: no remote copies, remote signals or barrier semaphores. Data moves between devices by JAX's collectives and lax.ppermute only.
A program may use at most 64 MiB of HBM per device.

```python
import math
import jax
import jax.numpy as jnp
from jax import lax

NZ = 32
CX = 8
CY = 128
SEG = 128
SLOT = 1024
PICARD = 2
OWNERS = 128
BLK_DEV = 128
BLOCKS = 16384
PLANTS = 2048
NX = 256
NY = 512
N_GX = 32
N_GY = 4


def draw_source_dev(key, part):
    owner = lax.broadcasted_iota(jnp.int32, (BLOCKS, SEG), 0) // BLK_DEV
    owner_x = owner // N_GY
    owner_y = owner % N_GY
    pick = jax.random.randint(key, (BLOCKS, SEG), 0, 20)
    which = jnp.clip(pick - 12, 0, 7)
    table_x = jnp.array([-1, -1, -1, 0, 0, 1, 1, 1], jnp.int32)
    table_y = jnp.array([-1, 0, 1, -1, 1, -1, 0, 1], jnp.int32)
    near = pick >= 12
    step_x = jnp.where(near, table_x[which], 0)
    step_y = jnp.where(near, table_y[which], 0)
    return ((owner_x + step_x) % N_GX * N_GY + (owner_y + step_y) % N_GY).astype(jnp.int32)


def with_ends(drawn, rng, least, largest):
    dims = drawn.shape
    spot = [jax.random.randint(jax.random.fold_in(rng, axis), (), 0, dims[axis]) for axis in range(len(dims))]
    drawn = drawn.at[tuple(spot)].set(least)
    longest = dims.index(max(dims))
    spot[longest] = (spot[longest] + 1) % dims[longest]
    return drawn.at[tuple(spot)].set(largest)


def levels(stream_key, dims, cuts, low, high):
    level = 1.0
    for dim, shards_of in cuts:
        heights = jax.random.uniform(jax.random.fold_in(jax.random.fold_in(stream_key, 6), dim), (shards_of,), jnp.float32, low / len(cuts), high / len(cuts))
        level = level * jnp.repeat(jnp.exp(heights), dims[dim] // shards_of).reshape((-1,) + (1,) * (len(dims) - 1 - dim))
    return level


def setup_inputs(seed: int = 0) -> dict:
    key_of = jax.random.split(jax.random.key(seed), 15)
    head_start = jnp.clip(-6.0 + 5.5 * jax.random.uniform(key_of[0], (NZ, NX, NY), jnp.float32) ** levels(key_of[0], (NZ, NX, NY), ((1, 32), (2, 4)), -0.2, 0.2), -6.0, -0.5)
    sat_conduct = jnp.clip(jnp.exp(math.log(5.0) - 2.3025851 * jax.random.uniform(key_of[1], (NZ, NX, NY), jnp.float32) ** levels(key_of[1], (NZ, NX, NY), ((1, 32), (2, 4)), -0.2, 0.2)), 0.5, 5.0)
    alpha_dry = jnp.clip(jnp.exp(math.log(3.0) - 1.7917595 * jax.random.uniform(key_of[2], (NZ, NX, NY), jnp.float32) ** levels(key_of[2], (NZ, NX, NY), ((1, 32), (2, 4)), -0.2, 0.2)), 0.5, 3.0)
    wet_flag = with_ends((jax.random.randint(key_of[3], (NZ, NX, NY), 0, 2) < 1).astype(jnp.int32), jax.random.fold_in(key_of[3], 1), 0, 1)
    reversal_head = jnp.clip(-8.0 + 7.0 * jax.random.uniform(key_of[4], (NZ, NX, NY), jnp.float32) ** levels(key_of[4], (NZ, NX, NY), ((1, 32), (2, 4)), -0.2, 0.2), -8.0, -1.0)
    send_row = with_ends(jax.random.randint(key_of[5], (OWNERS, 9, SLOT), 0, NZ * CX), jax.random.fold_in(key_of[5], 1), 0, (NZ * CX) - 1).astype(jnp.int32)
    send_col = with_ends(jax.random.randint(key_of[6], (OWNERS, 9, SLOT), 0, CY), jax.random.fold_in(key_of[6], 1), 0, CY - 1).astype(jnp.int32)
    root_radial = jnp.clip(jnp.exp(math.log(0.2) - 2.3025851 * jax.random.uniform(key_of[7], (BLOCKS, SEG), jnp.float32) ** levels(key_of[7], (BLOCKS, SEG), ((0, 128),), -0.2, 0.2)), 0.02, 0.2)
    root_axial = jnp.clip(jnp.exp(math.log(10.0) - 2.3025851 * jax.random.uniform(key_of[8], (BLOCKS, SEG), jnp.float32) ** levels(key_of[8], (BLOCKS, SEG), ((0, 128),), -0.2, 0.2)), 1.0, 10.0)
    stem_link = jnp.clip(jnp.exp(math.log(10.0) - 2.3025851 * jax.random.uniform(key_of[9], (BLOCKS,), jnp.float32) ** levels(key_of[9], (BLOCKS,), ((0, 128),), -0.2, 0.2)), 1.0, 10.0)
    entry_seg = with_ends(jax.random.randint(key_of[10], (BLOCKS,), 0, SEG), jax.random.fold_in(key_of[10], 1), 0, SEG - 1).astype(jnp.int32)
    source_dev = draw_source_dev(jax.random.fold_in(key_of[14], 71), 0)
    source_slot = with_ends(jax.random.randint(key_of[12], (BLOCKS, SEG), 0, SLOT), jax.random.fold_in(key_of[12], 1), 0, SLOT - 1).astype(jnp.int32)
    demand = jnp.clip(jnp.exp(math.log(128.0) - 2.0794415 * jax.random.uniform(key_of[13], (PLANTS,), jnp.float32) ** levels(key_of[13], (PLANTS,), ((0, 128),), -0.2, 0.2)), 16.0, 128.0)
    return dict(head_start=head_start, sat_conduct=sat_conduct, alpha_dry=alpha_dry, wet_flag=wet_flag, reversal_head=reversal_head, send_row=send_row, send_col=send_col, root_radial=root_radial, root_axial=root_axial, stem_link=stem_link, entry_seg=entry_seg, source_dev=source_dev, source_slot=source_slot, demand=demand)


PORE_INDEX = 1.6
PORE_POWER = 0.375
SPAN_THETA = 0.35
STORAGE = 0.01
TIME_STEP = 1.0
SINK_GAIN = 4.0

def conduct(head_now, sat_conduct, alpha):
    saturation = (1.0 + (alpha * jnp.abs(head_now)) ** PORE_INDEX) ** (-PORE_POWER)
    inner = 1.0 - (1.0 - saturation ** (1.0 / PORE_POWER)) ** PORE_POWER
    return sat_conduct * jnp.sqrt(saturation) * inner * inner

def capacity(head_now, alpha_dry, wetting, reversal_head):
    alpha = alpha_dry * (1.0 + wetting)
    scaled = alpha * jnp.abs(head_now)
    slope = PORE_POWER * PORE_INDEX * alpha * scaled ** (PORE_INDEX - 1.0) * (1.0 + scaled ** PORE_INDEX) ** (-PORE_POWER - 1.0)
    drying_rev = (1.0 + (alpha_dry * jnp.abs(reversal_head)) ** PORE_INDEX) ** (-PORE_POWER)
    wetting_rev = (1.0 + (2.0 * alpha_dry * jnp.abs(reversal_head)) ** PORE_INDEX) ** (-PORE_POWER)
    factor = wetting * drying_rev / wetting_rev + (1.0 - wetting)
    return SPAN_THETA * factor * slope + STORAGE

def shifted(array, offset_x, offset_y):
    return array[:, 1 + offset_x:array.shape[1] - 1 + offset_x, 1 + offset_y:array.shape[2] - 1 + offset_y]

def update(head_pad, cond_pad, capacity_now, head_old, sink_field):
    head_mid = shifted(head_pad, 0, 0)
    cond_mid = shifted(cond_pad, 0, 0)
    numerator = capacity_now * head_old / TIME_STEP
    denominator = capacity_now / TIME_STEP
    for offset in ((1, 0), (-1, 0), (0, 1), (0, -1)):
        face = 0.5 * (cond_mid + shifted(cond_pad, offset[0], offset[1]))
        numerator = numerator + face * shifted(head_pad, offset[0], offset[1])
        denominator = denominator + face
    face_vert = 0.5 * (cond_mid[1:] + cond_mid[:-1])
    no_face = jnp.zeros_like(cond_mid[:1])
    numerator = numerator + jnp.concatenate([no_face, face_vert * (head_mid[:-1] + 1.0)], 0)
    numerator = numerator + jnp.concatenate([face_vert * (head_mid[1:] - 1.0), no_face], 0)
    denominator = denominator + jnp.concatenate([no_face, face_vert], 0) + jnp.concatenate([face_vert, no_face], 0)
    numerator = numerator - jnp.concatenate([jnp.zeros_like(cond_mid[:-1]), cond_mid[-1:]], 0)
    return (numerator - SINK_GAIN * sink_field) / denominator

def moved_down(values, stride, fill):
    return jnp.concatenate([jnp.full_like(values[:, :stride], fill), values[:, :values.shape[1] - stride]], 1)

def moved_up(values, stride, fill):
    return jnp.concatenate([values[:, stride:], jnp.full_like(values[:, :stride], fill)], 1)

def reduce_solve(lower, diagonal, upper, first_rhs, second_rhs):
    length = diagonal.shape[1]
    stride = 1
    while stride < length:
        factor_low = -lower / moved_down(diagonal, stride, 1.0)
        factor_high = -upper / moved_up(diagonal, stride, 1.0)
        new_diagonal = diagonal + factor_low * moved_down(upper, stride, 0.0) + factor_high * moved_up(lower, stride, 0.0)
        first_rhs = first_rhs + factor_low * moved_down(first_rhs, stride, 0.0) + factor_high * moved_up(first_rhs, stride, 0.0)
        second_rhs = second_rhs + factor_low * moved_down(second_rhs, stride, 0.0) + factor_high * moved_up(second_rhs, stride, 0.0)
        lower = factor_low * moved_down(lower, stride, 0.0)
        upper = factor_high * moved_up(upper, stride, 0.0)
        diagonal = new_diagonal
        stride = stride * 2
    return (first_rhs / diagonal, second_rhs / diagonal)

def root_uptake(head_seg, cond_seg, root_radial, root_axial, stem_link, entry_seg, demand, plant_blocks):
    radial = root_radial * cond_seg / (root_radial + cond_seg)
    axial_link = root_axial[:, :-1]
    no_link = jnp.zeros_like(root_axial[:, :1])
    left_link = jnp.concatenate([no_link, axial_link], 1)
    right_link = jnp.concatenate([axial_link, no_link], 1)
    position = lax.broadcasted_iota(jnp.int32, root_radial.shape, 1)
    collar_link = jnp.where(position == entry_seg[:, None], stem_link[:, None], jnp.zeros_like(root_radial))
    diagonal = radial + collar_link + left_link + right_link
    free_part, collar_part = reduce_solve(-left_link, diagonal, -right_link, radial * head_seg, collar_link)
    base_uptake = lax.optimization_barrier(jnp.sum(radial * (head_seg - free_part), 1)).reshape(-1, plant_blocks).sum(1)
    response = lax.optimization_barrier(jnp.sum(radial * collar_part, 1)).reshape(-1, plant_blocks).sum(1)
    collar_head = (base_uptake - demand) / response
    xylem = free_part + jnp.repeat(collar_head, plant_blocks)[:, None] * collar_part
    return (radial * (head_seg - xylem), collar_head)

def reference(head_start, sat_conduct, alpha_dry, wet_flag, reversal_head, send_row, send_col, root_radial, root_axial, stem_link, entry_seg, source_dev, source_slot, demand):
    wetting = wet_flag.astype(head_start.dtype)
    alpha_eff = alpha_dry * (1.0 + wetting)
    plant_blocks = root_radial.shape[0] // demand.shape[0]
    owner = (lax.broadcasted_iota(jnp.int32, root_radial.shape, 0) // BLK_DEV).astype(jnp.int32)
    offset_k = ((owner // N_GY - source_dev // N_GY + 1) % N_GX * 3 + (owner % N_GY - source_dev % N_GY + 1) % N_GY).astype(jnp.int32)
    layer_row = send_row[source_dev, offset_k, source_slot]
    column = send_col[source_dev, offset_k, source_slot]
    layer = layer_row // CX
    row_global = source_dev // N_GY * CX + layer_row % CX
    col_global = source_dev % N_GY * CY + column
    cell_index = ((layer * NX + row_global) * NY + col_global).astype(jnp.int32).reshape(-1)
    head_now = head_start
    collar_head = None
    for iteration in range(PICARD):
        conduct_now = conduct(head_now, sat_conduct, alpha_eff)
        capacity_now = capacity(head_now, alpha_dry, wetting, reversal_head)
        head_seg = head_now.reshape(-1)[cell_index].reshape(root_radial.shape)
        cond_seg = conduct_now.reshape(-1)[cell_index].reshape(root_radial.shape)
        uptake, collar_head = root_uptake(head_seg, cond_seg, root_radial, root_axial, stem_link, entry_seg, demand, plant_blocks)
        sink_field = jnp.zeros((head_now.size,), head_now.dtype).at[cell_index].add(uptake.reshape(-1)).reshape(head_now.shape)
        head_pad = jnp.pad(head_now, ((0, 0), (1, 1), (1, 1)), mode='wrap')
        cond_pad = jnp.pad(conduct_now, ((0, 0), (1, 1), (1, 1)), mode='wrap')
        head_now = update(head_pad, cond_pad, capacity_now, head_start, sink_field)
    return (head_now, collar_head)
```

```python
import jax
import jax.numpy as jnp
from jax import lax
from jax.experimental import pallas as pl
from jax.experimental.pallas import tpu as pltpu
from jax.sharding import PartitionSpec as P

PICARD = 2
PORE_INDEX = 1.6
PORE_POWER = 0.375
SPAN_THETA = 0.35
STORAGE = 0.01
SINK_GAIN = 4.0

F32, BF16, I32 = (jnp.float32, jnp.bfloat16, jnp.int32)
VMEM_LIMIT = 48 * 2**20
LAYERS, CELLS, LANES, SLOTS, BLOCKS, PLANTS = (32, 256, 128, 72, 128, 16)


def split(x):
    hi = x.astype(BF16)
    return (hi, (x - hi.astype(F32)).astype(BF16))


def conduct(head, sat_conduct, alpha):
    power = jnp.exp(PORE_INDEX * jnp.log(alpha * jnp.abs(head)))
    root = jnp.exp((-0.5 * PORE_POWER) * jnp.log(1.0 + power))
    inner = 1.0 - jnp.exp(-PORE_POWER * jnp.log(1.0 + 1.0 / power))
    return sat_conduct * root * inner * inner


def capacity(head, alpha_dry, wetting, reversal_head):
    alpha = alpha_dry * (1.0 + wetting)
    log_scaled = jnp.log(alpha * jnp.abs(head))
    log_term = jnp.log(1.0 + jnp.exp(PORE_INDEX * log_scaled))
    slope = (
        (PORE_POWER * PORE_INDEX)
        * alpha
        * jnp.exp((PORE_INDEX - 1.0) * log_scaled + (-PORE_POWER - 1.0) * log_term)
    )
    turned = jnp.exp(PORE_INDEX * jnp.log(alpha_dry * jnp.abs(reversal_head)))
    ratio = jnp.exp(PORE_POWER * (jnp.log(1.0 + 2.0**PORE_INDEX * turned) - jnp.log(1.0 + turned)))
    factor = wetting * ratio + (1.0 - wetting)
    return SPAN_THETA * factor * slope + STORAGE


def gather_cells(head, cond, row, col, weight, minus, here, plus, edge_minus, edge_plus):
    for field, ref in enumerate((head, cond)):
        for half in range(2):
            turned = ref[half * 128 : half * 128 + 128, :].T
            edge_minus[field * 2 + half : field * 2 + half + 1, :] = turned[0:1]
            edge_plus[field * 2 + half : field * 2 + half + 1, :] = turned[127:128]
            hi, lo = split(turned)
            weight[field * 128 : field * 128 + 128, half * 128 : half * 128 + 128] = hi
            weight[field * 128 : field * 128 + 128, 256 + half * 128 : 384 + half * 128] = lo
        minus[48 + 32 * field : 80 + 32 * field, :] = ref[pl.ds(0, LAYERS, stride=8), :]
        plus[48 + 32 * field : 80 + 32 * field, :] = ref[pl.ds(7, LAYERS, stride=8), :]
    edge_minus[4:8, :] = jnp.zeros((4, LANES), F32)
    edge_plus[4:8, :] = jnp.zeros((4, LANES), F32)
    cells = lax.broadcasted_iota(I32, (CELLS, LANES), 0).astype(F32).astype(BF16)
    columns = lax.broadcasted_iota(I32, (LANES, LANES), 0)
    one, zero = (jnp.ones((), BF16), jnp.zeros((), BF16))
    for j in range(0, SLOTS, 2):
        picks = []
        for i in (j, j + 1):
            wanted = jnp.broadcast_to(row[i : i + 1, :].astype(F32).astype(BF16), (CELLS, LANES))
            picks.append(jnp.where(cells == wanted, one, zero))
        pick = jnp.concatenate(picks, 1)
        got = lax.dot_general(
            weight[...],
            jnp.concatenate([pick, pick], 0),
            (((1,), (0,)), ((), ())),
            preferred_element_type=F32,
        )
        for n, i in enumerate((j, j + 1)):
            k, chunk = divmod(i, 8)
            out = (minus, here, plus)[k // 3]
            mask = columns == col[i : i + 1, :]
            for field in range(2):
                part = got[field * 128 : field * 128 + 128, n * 128 : n * 128 + 128]
                at = k % 3 * 16 + field * 8 + chunk
                out[at : at + 1, :] = jnp.sum(jnp.where(mask, part, 0.0), 0, keepdims=True)


def start_kernel(
    head, sat, alpha_dry, wet, send_row, send_col,
    cond, row, col, minus, here, plus, edge_minus, edge_plus, weight,
):
    for k in range(9):
        for chunk in range(8):
            at = k * 8 + chunk
            row[at : at + 1, :] = send_row[k : k + 1, chunk * 128 : chunk * 128 + 128]
            col[at : at + 1, :] = send_col[k : k + 1, chunk * 128 : chunk * 128 + 128]
    for layer in range(LAYERS):
        at = slice(layer * 8, layer * 8 + 8)
        cond[at, :] = conduct(head[at, :], sat[at, :], alpha_dry[at, :] * (1.0 + wet[at, :].astype(F32)))
    gather_cells(head, cond, row, col, weight, minus, here, plus, edge_minus, edge_plus)


def terms_kernel(
    head, cond, head_old, alpha_dry, wet, reversal, from_minus, from_plus, side_minus, side_plus,
    numerator, denominator, halo,
):
    halo[...] = jnp.zeros_like(halo)
    turned = []
    for i in range(4):
        halo[0:1, :] = side_minus[48 + i : 49 + i, :]
        halo[127:128, :] = side_plus[48 + i : 49 + i, :]
        turned.append(halo[...].T)
    sub = lax.broadcasted_iota(I32, (8, LANES), 0)
    lane = lax.broadcasted_iota(I32, (8, LANES), 1)
    for layer in range(LAYERS):
        at = slice(layer * 8, layer * 8 + 8)
        h, c = (head[at, :], cond[at, :])
        cap = capacity(h, alpha_dry[at, :], wet[at, :].astype(F32), reversal[at, :])
        num, den = (cap * head_old[at, :], cap)
        local = slice(layer % 16 * 8, layer % 16 * 8 + 8)
        halo_h, halo_c = (turned[layer // 16][local], turned[2 + layer // 16][local])

        def add(num, den, near_h, near_c):
            face = 0.5 * (c + near_c)
            return (num + face * near_h, den + face)

        def beside(x, line, spot):
            return jnp.where(sub == spot, jnp.broadcast_to(line, (8, LANES)), x)

        num, den = add(
            num, den,
            beside(pltpu.roll(h, 7, 0), from_plus[48 + layer : 49 + layer, :], 7),
            beside(pltpu.roll(c, 7, 0), from_plus[80 + layer : 81 + layer, :], 7),
        )
        num, den = add(
            num, den,
            beside(pltpu.roll(h, 1, 0), from_minus[48 + layer : 49 + layer, :], 0),
            beside(pltpu.roll(c, 1, 0), from_minus[80 + layer : 81 + layer, :], 0),
        )
        num, den = add(
            num, den,
            jnp.where(lane == 127, halo_h, pltpu.roll(h, 127, 1)),
            jnp.where(lane == 127, halo_c, pltpu.roll(c, 127, 1)),
        )
        num, den = add(
            num, den,
            jnp.where(lane == 0, halo_h, pltpu.roll(h, 1, 1)),
            jnp.where(lane == 0, halo_c, pltpu.roll(c, 1, 1)),
        )
        if layer > 0:
            above = slice(layer * 8 - 8, layer * 8)
            num, den = add(num, den, head[above, :] + 1.0, cond[above, :])
        if layer < LAYERS - 1:
            below = slice(layer * 8 + 8, layer * 8 + 16)
            num, den = add(num, den, head[below, :] - 1.0, cond[below, :])
        else:
            num = num - c
        numerator[at, :] = num
        denominator[at, :] = den


def root_kernel(
    demand, from_minus, here, from_plus, side_minus, side_plus, code, radial_in, axial, stem, entry,
    out_minus, out_here, out_plus, collar_out, weight, table, seg_head, seg_cond, uptake,
):
    for dx in range(3):
        for dy in range(3):
            if dy == 1:
                source, at = ((from_plus, here, from_minus)[dx], 16)
            else:
                source, at = ((side_plus, None, side_minus)[dy], (2 - dx) * 16)
            for field in range(2):
                to = field * 128 + (dx * 3 + dy) * 8
                table[to : to + 8, :] = source[at + field * 8 : at + field * 8 + 8, :]
    for field in range(2):
        table[field * 128 + 72 : field * 128 + 128, :] = jnp.zeros((56, LANES), F32)
        hi, lo = split(table[field * 128 : field * 128 + 128, :].T)
        weight[field * 128 : field * 128 + 128, 0:128] = hi
        weight[field * 128 : field * 128 + 128, 128:256] = lo
    rows = lax.broadcasted_iota(I32, (128, LANES), 0).astype(F32).astype(BF16)
    columns = lax.broadcasted_iota(I32, (LANES, LANES), 0)
    one, zero = (jnp.ones((), BF16), jnp.zeros((), BF16))
    for j in range(0, BLOCKS, 2):
        picks = []
        for i in (j, j + 1):
            wanted = jnp.broadcast_to((code[i : i + 1, :] >> 7).astype(F32).astype(BF16), (128, LANES))
            picks.append(jnp.where(rows == wanted, one, zero))
        pick = jnp.concatenate(picks, 1)
        got = lax.dot_general(
            weight[...],
            jnp.concatenate([pick, pick], 0),
            (((1,), (0,)), ((), ())),
            preferred_element_type=F32,
        )
        for n, i in enumerate((j, j + 1)):
            mask = columns == (code[i : i + 1, :] & 127)
            for field, ref in enumerate((seg_head, seg_cond)):
                part = got[field * 128 : field * 128 + 128, n * 128 : n * 128 + 128]
                ref[i : i + 1, :] = jnp.sum(jnp.where(mask, part, 0.0), 0, keepdims=True)
    group = 32
    lane = lax.broadcasted_iota(I32, (group, LANES), 1)
    plant_row = lax.broadcasted_iota(I32, (group // 8, 1), 0)
    collar_line = jnp.zeros((1, LANES), F32)
    for g in range(BLOCKS // group):
        at = slice(g * group, g * group + group)
        sub = lax.broadcasted_iota(I32, (group, LANES), 0) + g * group
        own = sub == lane
        stem_col = jnp.sum(jnp.where(own, stem[...], 0.0), 1, keepdims=True)
        entry_col = jnp.sum(jnp.where(own, entry[...], 0), 1, keepdims=True)
        hs, ks, rr = (seg_head[at, :], seg_cond[at, :], radial_in[at, :])
        radial = rr * ks / (rr + ks)
        right = jnp.where(lane == 127, 0.0, axial[at, :])
        left = pltpu.roll(right, 1, 1)
        second = jnp.where(lane == entry_col, stem_col, 0.0)
        first = radial * hs
        diagonal = radial + second + left + right
        lower, upper = (-left, -right)
        for step in range(7):
            stride = 2**step
            inverse = 1.0 / diagonal
            low = -lower * pltpu.roll(inverse, stride, 1)
            high = -upper * pltpu.roll(inverse, 128 - stride, 1)
            first, second = (
                x + low * pltpu.roll(x, stride, 1) + high * pltpu.roll(x, 128 - stride, 1)
                for x in (first, second)
            )
            diagonal = diagonal + low * lower + high * upper
            if step < 6:
                lower = low * pltpu.roll(lower, stride, 1)
                upper = high * pltpu.roll(upper, 128 - stride, 1)
        inverse = 1.0 / diagonal
        free, collar = (first * inverse, second * inverse)

        def per_plant(x):
            return jnp.sum(jnp.sum(x.reshape(group // 8, 8, LANES), 1), 1, keepdims=True)

        need = jnp.zeros((group // 8, 1), F32)
        for p in range(group // 8):
            need = jnp.where(plant_row == p, demand[g * (group // 8) + p], need)
        head = (per_plant(radial * (hs - free)) - need) / per_plant(radial * collar)
        spread = jnp.broadcast_to(head[:, None, :], (group // 8, 8, LANES)).reshape(group, LANES)
        uptake[at, :] = radial * (hs - (free + spread * collar))
        mine = lax.broadcasted_iota(I32, (group // 8, LANES), 1) == plant_row + g * (group // 8)
        collar_line = collar_line + jnp.sum(jnp.where(mine, head, 0.0), 0, keepdims=True)
    collar_out[...] = collar_line
    slot_rows = lax.broadcasted_iota(I32, (80, LANES), 0).astype(F32).astype(BF16)
    slot_cols = rows
    total = jnp.zeros((160, LANES), F32)
    for start in range(0, BLOCKS, 8):
        values, places = ([], [])
        for i in range(start, start + 8):
            where = code[i : i + 1, :]
            hi, lo = split(uptake[i : i + 1, :])
            mask = slot_rows == jnp.broadcast_to((where >> 7).astype(F32).astype(BF16), (80, LANES))
            values.append(
                jnp.concatenate(
                    [jnp.where(mask, jnp.broadcast_to(v, (80, LANES)), zero) for v in (hi, lo)], 0
                )
            )
            wanted = jnp.broadcast_to((where & 127).astype(F32).astype(BF16), (128, LANES))
            places.append(jnp.where(slot_cols == wanted, one, zero))
        total = total + lax.dot_general(
            jnp.concatenate(values, 1),
            jnp.concatenate(places, 1),
            (((1,), (1,)), ((), ())),
            preferred_element_type=F32,
        )
    summed = total[0:72] + total[80:152]
    out_minus[...] = summed[0:24]
    out_here[...] = summed[24:48]
    out_plus[...] = summed[48:72]


def sink_of(pieces, row, col):
    low_rows = lax.broadcasted_iota(I32, (128, LANES), 0).astype(F32).astype(BF16)
    places_of = lax.broadcasted_iota(I32, (256, LANES), 0).astype(F32).astype(BF16)
    one, zero = (jnp.ones((), BF16), jnp.zeros((), BF16))
    total = jnp.zeros((256, 256), F32)
    for k in range(9):
        source, base = pieces[k]
        values, places = ([], [])
        for chunk in range(8):
            i = k * 8 + chunk
            r, c = (row[i : i + 1, :], col[i : i + 1, :])
            hi, lo = split(source[base + chunk : base + chunk + 1, :])
            mask = low_rows == jnp.broadcast_to((r & 127).astype(F32).astype(BF16), (128, LANES))
            values.append(
                jnp.concatenate(
                    [jnp.where(mask, jnp.broadcast_to(v, (128, LANES)), zero) for v in (hi, lo)], 0
                )
            )
            wanted = ((r >> 7) * 128 + c).astype(F32).astype(BF16)
            places.append(jnp.where(places_of == jnp.broadcast_to(wanted, (256, LANES)), one, zero))
        total = total + lax.dot_general(
            jnp.concatenate(values, 1),
            jnp.concatenate(places, 1),
            (((1,), (1,)), ((), ())),
            preferred_element_type=F32,
        )
    return total[0:128] + total[128:256]


def new_head(back, row, col, numerator, denominator, head_new):
    from_minus, here, from_plus, side_minus, side_plus = back
    pieces = []
    for dx in range(3):
        for dy in range(3):
            if dy == 1:
                pieces.append(((from_minus, here, from_plus)[dx], 8))
            else:
                pieces.append(((side_minus, None, side_plus)[dy], dx * 8))
    sink = sink_of(pieces, row, col)
    for half in range(2):
        at = slice(half * 128, half * 128 + 128)
        head_new[at, :] = (numerator[at, :] - SINK_GAIN * sink[:, at]) / denominator[at, :]


def next_kernel(
    from_minus, here_in, from_plus, side_minus, side_plus, row, col, numerator, denominator, sat, alpha_dry, wet,
    head, cond, minus, here, plus, edge_minus, edge_plus, weight,
):
    back = (from_minus, here_in, from_plus, side_minus, side_plus)
    new_head(back, row, col, numerator, denominator, head)
    for layer in range(LAYERS):
        at = slice(layer * 8, layer * 8 + 8)
        cond[at, :] = conduct(head[at, :], sat[at, :], alpha_dry[at, :] * (1.0 + wet[at, :].astype(F32)))
    gather_cells(head, cond, row, col, weight, minus, here, plus, edge_minus, edge_plus)


def last_kernel(
    from_minus, here_in, from_plus, side_minus, side_plus, row, col, numerator, denominator, head
):
    back = (from_minus, here_in, from_plus, side_minus, side_plus)
    new_head(back, row, col, numerator, denominator, head)


def call(kernel, outs, scratch=(), specs=None, flops=0, **params):
    shapes = [jax.ShapeDtypeStruct(shape, dtype) for shape, dtype in outs]
    return pl.pallas_call(
        kernel,
        out_shape=shapes,
        scratch_shapes=[pltpu.VMEM(shape, dtype) for shape, dtype in scratch],
        compiler_params=pltpu.CompilerParams(vmem_limit_bytes=VMEM_LIMIT),
        **({} if specs is None else {"in_specs": specs}),
        **params,
    )


MESSAGES = [((112, 128), F32), ((48, 128), F32), ((112, 128), F32), ((8, 128), F32), ((8, 128), F32)]


def up(x, axis):
    size = lax.axis_size(axis)
    return lax.ppermute(x, axis, [(i, (i + 1) % size) for i in range(size)])


def down(x, axis):
    size = lax.axis_size(axis)
    return lax.ppermute(x, axis, [((i + 1) % size, i) for i in range(size)])


def spread(minus, here, plus, edge_minus, edge_plus):
    from_minus = up(plus, "gx")
    from_plus = down(minus, "gx")
    side_minus = up(
        jnp.concatenate([from_minus[32:48], here[32:48], from_plus[32:48], edge_plus], 0), "gy"
    )
    side_plus = down(
        jnp.concatenate([from_minus[0:16], here[0:16], from_plus[0:16], edge_minus], 0), "gy"
    )
    return (from_minus, here, from_plus, side_minus, side_plus)


def give_back(minus, here, plus):
    from_minus = up(minus, "gx")
    from_plus = down(plus, "gx")
    side_plus = down(jnp.concatenate([from_minus[16:24], here[16:24], from_plus[16:24]], 0), "gy")
    side_minus = up(jnp.concatenate([from_minus[0:8], here[0:8], from_plus[0:8]], 0), "gy")
    return (from_minus, here, from_plus, side_minus, side_plus)


def on_device(
    head_start,
    sat_conduct,
    alpha_dry,
    wet_flag,
    reversal_head,
    send_row,
    send_col,
    root_radial,
    root_axial,
    stem_link,
    entry_seg,
    source_dev,
    source_slot,
    demand,
):
    tile = head_start.shape
    head, sat, alpha, wet, reversal = (
        x.reshape(CELLS, LANES) for x in (head_start, sat_conduct, alpha_dry, wet_flag, reversal_head)
    )
    rows_gx = lax.axis_size("gx")
    cols_gy = lax.axis_size("gy")
    offset_k = (lax.axis_index("gx") - source_dev // cols_gy + 1) % rows_gx * 3 + (
        lax.axis_index("gy") - source_dev % cols_gy + 1
    ) % cols_gy
    code = offset_k * send_row.shape[2] + source_slot
    stem, entry = (stem_link.reshape(1, BLOCKS), entry_seg.reshape(1, BLOCKS))
    head_old = head
    cond, row, col, *messages = call(
        start_kernel,
        [((CELLS, LANES), F32), ((SLOTS, LANES), I32), ((SLOTS, LANES), I32)] + MESSAGES,
        [((256, 512), BF16)],
    )(head, sat, alpha, wet, send_row[0], send_col[0])
    smem = [pl.BlockSpec(memory_space=pltpu.SMEM)] + [pl.BlockSpec(memory_space=pltpu.VMEM)] * 10
    for iteration in range(PICARD):
        got = spread(*messages)
        *sums, collar = call(
            root_kernel,
            [((24, 128), F32)] * 3 + [((1, 128), F32)],
            [((256, 256), BF16), ((256, 128), F32)] + [((128, 128), F32)] * 3,
            specs=smem,
        )(demand, *got, code, root_radial, root_axial, stem, entry)
        numerator, denominator = call(
            terms_kernel,
            [((CELLS, LANES), F32)] * 2,
            [((128, 128), F32)],
        )(head, cond, head_old, alpha, wet, reversal, got[0], got[2], got[3], got[4])
        back = give_back(*sums)
        if iteration < PICARD - 1:
            head, cond, *messages = call(
                next_kernel,
                [((CELLS, LANES), F32)] * 2 + MESSAGES,
                [((256, 512), BF16)],
            )(*back, row, col, numerator, denominator, sat, alpha, wet)
        else:
            (head,) = call(last_kernel, [((CELLS, LANES), F32)])(
                *back, row, col, numerator, denominator
            )
    return (head.reshape(tile), collar[0, :PLANTS])


def solution(mesh):
    tile, lists, blocks, line = (
        P(None, "gx", "gy"),
        P(("gx", "gy"), None, None),
        P(("gx", "gy"), None),
        P(("gx", "gy")),
    )
    return jax.shard_map(
        on_device,
        mesh=mesh,
        in_specs=(tile,) * 5 + (lists,) * 2 + (blocks,) * 2 + (line,) * 2 + (blocks,) * 2 + (line,),
        out_specs=(tile, line),
        check_vma=False,
    )
```

```python
import jax
import jax.numpy as jnp
from jax import lax
from jax.experimental import pallas as pl
from jax.experimental.pallas import tpu as pltpu
from jax.sharding import PartitionSpec as P

PICARD = 2
PORE_INDEX = 1.6
PORE_POWER = 0.375
SPAN_THETA = 0.35
STORAGE = 0.01
SINK_GAIN = 4.0

F32, BF16, I32 = (jnp.float32, jnp.bfloat16, jnp.int32)
VMEM_LIMIT = 48 * 2**20
LAYERS, CELLS, LANES, SLOTS, BLOCKS, PLANTS = (32, 256, 128, 72, 128, 16)


def split(x):
    hi = x.astype(BF16)
    return (hi, (x - hi.astype(F32)).astype(BF16))


def conduct(head, sat_conduct, alpha):
    power = jnp.exp(PORE_INDEX * jnp.log(alpha * jnp.abs(head)))
    root = jnp.exp((-0.5 * PORE_POWER) * jnp.log(1.0 + power))
    inner = 1.0 - jnp.exp(-PORE_POWER * jnp.log(1.0 + 1.0 / power))
    return sat_conduct * root * inner * inner


def capacity(head, alpha_dry, wetting, reversal_head):
    alpha = alpha_dry * (1.0 + wetting)
    log_scaled = jnp.log(alpha * jnp.abs(head))
    log_term = jnp.log(1.0 + jnp.exp(PORE_INDEX * log_scaled))
    slope = (
        (PORE_POWER * PORE_INDEX)
        * alpha
        * jnp.exp((PORE_INDEX - 1.0) * log_scaled + (-PORE_POWER - 1.0) * log_term)
    )
    turned = jnp.exp(PORE_INDEX * jnp.log(alpha_dry * jnp.abs(reversal_head)))
    ratio = jnp.exp(PORE_POWER * (jnp.log(1.0 + 2.0**PORE_INDEX * turned) - jnp.log(1.0 + turned)))
    factor = wetting * ratio + (1.0 - wetting)
    return SPAN_THETA * factor * slope + STORAGE


def lay_cells(head, cond, weight, minus, plus, edge_minus, edge_plus):
    for field, ref in enumerate((head, cond)):
        for half in range(2):
            turned = ref[half * 128 : half * 128 + 128, :].T
            edge_minus[field * 2 + half : field * 2 + half + 1, :] = turned[0:1]
            edge_plus[field * 2 + half : field * 2 + half + 1, :] = turned[127:128]
            hi, lo = split(turned)
            weight[field * 128 : field * 128 + 128, half * 128 : half * 128 + 128] = hi
            weight[field * 128 : field * 128 + 128, 256 + half * 128 : 384 + half * 128] = lo
        minus[48 + 32 * field : 80 + 32 * field, :] = ref[pl.ds(0, LAYERS, stride=8), :]
        plus[48 + 32 * field : 80 + 32 * field, :] = ref[pl.ds(7, LAYERS, stride=8), :]
    edge_minus[4:8, :] = jnp.zeros((4, LANES), F32)
    edge_plus[4:8, :] = jnp.zeros((4, LANES), F32)


def gather_cells(row, col, weight, outs):
    cells = lax.broadcasted_iota(I32, (CELLS, LANES), 0).astype(F32).astype(BF16)
    columns = lax.broadcasted_iota(I32, (LANES, LANES), 0)
    one, zero = (jnp.ones((), BF16), jnp.zeros((), BF16))
    for j in range(0, SLOTS, 2):
        out = outs[j // 24]
        if out is None:
            continue
        picks = []
        for i in (j, j + 1):
            wanted = jnp.broadcast_to(row[i : i + 1, :].astype(F32).astype(BF16), (CELLS, LANES))
            picks.append(jnp.where(cells == wanted, one, zero))
        pick = jnp.concatenate(picks, 1)
        got = lax.dot_general(
            weight[...],
            jnp.concatenate([pick, pick], 0),
            (((1,), (0,)), ((), ())),
            preferred_element_type=F32,
        )
        for n, i in enumerate((j, j + 1)):
            k, chunk = divmod(i, 8)
            mask = columns == col[i : i + 1, :]
            for field in range(2):
                part = got[field * 128 : field * 128 + 128, n * 128 : n * 128 + 128]
                at = k % 3 * 16 + field * 8 + chunk
                out[at : at + 1, :] = jnp.sum(jnp.where(mask, part, 0.0), 0, keepdims=True)


def here_kernel(row, col, weight, here):
    gather_cells(row, col, weight, (None, here, None))


def start_kernel(
    head_in, sat_in, alpha_in, wet_in, row_in, col_in,
    cond, row, col, minus, plus, edge_minus, edge_plus, weight,
    head, sat, alpha_dry, wet, send_row, send_col, arrived,
):
    loads = [
        pltpu.make_async_copy(source, target, arrived.at[i])
        for i, (source, target) in enumerate(
            (
                (row_in, send_row), (col_in, send_col), (head_in, head), (alpha_in, alpha_dry), (wet_in, wet),
                (sat_in, sat),
            )
        )
    ]
    for load in loads:
        load.start()
    loads[0].wait()
    loads[1].wait()
    for k in range(9):
        for chunk in range(8):
            at = k * 8 + chunk
            row[at : at + 1, :] = send_row[0, k : k + 1, chunk * 128 : chunk * 128 + 128]
            col[at : at + 1, :] = send_col[0, k : k + 1, chunk * 128 : chunk * 128 + 128]
    for load in loads[2:]:
        load.wait()
    for layer in range(LAYERS):
        at = slice(layer * 8, layer * 8 + 8)
        cond[at, :] = conduct(head[at, :], sat[at, :], alpha_dry[at, :] * (1.0 + wet[at, :].astype(F32)))
    lay_cells(head, cond, weight, minus, plus, edge_minus, edge_plus)
    gather_cells(row, col, weight, (minus, None, plus))


def terms_kernel(
    head, cond, head_old, alpha_dry, wet, reversal, from_minus, from_plus, side_minus, side_plus,
    back_minus, back_here, back_plus, row, col,
    numerator, denominator, halo,
):
    pieces = {3 + dy: (x, 8) for dy, x in enumerate((back_minus, back_here, back_plus))}
    sink = SINK_GAIN * sink_of(pieces, row, col)
    halo[...] = jnp.zeros_like(halo)
    turned = []
    for i in range(4):
        halo[0:1, :] = side_minus[48 + i : 49 + i, :]
        halo[127:128, :] = side_plus[48 + i : 49 + i, :]
        turned.append(halo[...].T)
    sub = lax.broadcasted_iota(I32, (8, LANES), 0)
    lane = lax.broadcasted_iota(I32, (8, LANES), 1)
    for layer in range(LAYERS):
        at = slice(layer * 8, layer * 8 + 8)
        h, c = (head[at, :], cond[at, :])
        cap = capacity(h, alpha_dry[at, :], wet[at, :].astype(F32), reversal[at, :])
        num, den = (cap * head_old[at, :], cap)
        local = slice(layer % 16 * 8, layer % 16 * 8 + 8)
        halo_h, halo_c = (turned[layer // 16][local], turned[2 + layer // 16][local])

        def add(num, den, near_h, near_c):
            face = 0.5 * (c + near_c)
            return (num + face * near_h, den + face)

        def beside(x, line, spot):
            return jnp.where(sub == spot, jnp.broadcast_to(line, (8, LANES)), x)

        num, den = add(
            num, den,
            beside(pltpu.roll(h, 7, 0), from_plus[48 + layer : 49 + layer, :], 7),
            beside(pltpu.roll(c, 7, 0), from_plus[80 + layer : 81 + layer, :], 7),
        )
        num, den = add(
            num, den,
            beside(pltpu.roll(h, 1, 0), from_minus[48 + layer : 49 + layer, :], 0),
            beside(pltpu.roll(c, 1, 0), from_minus[80 + layer : 81 + layer, :], 0),
        )
        num, den = add(
            num, den,
            jnp.where(lane == 127, halo_h, pltpu.roll(h, 127, 1)),
            jnp.where(lane == 127, halo_c, pltpu.roll(c, 127, 1)),
        )
        num, den = add(
            num, den,
            jnp.where(lane == 0, halo_h, pltpu.roll(h, 1, 1)),
            jnp.where(lane == 0, halo_c, pltpu.roll(c, 1, 1)),
        )
        if layer > 0:
            above = slice(layer * 8 - 8, layer * 8)
            num, den = add(num, den, head[above, :] + 1.0, cond[above, :])
        if layer < LAYERS - 1:
            below = slice(layer * 8 + 8, layer * 8 + 16)
            num, den = add(num, den, head[below, :] - 1.0, cond[below, :])
        else:
            num = num - c
        half = layer // 16
        numerator[at, :] = num - sink[local, half * 128 : half * 128 + 128]
        denominator[at, :] = den


def root_kernel(
    demand, from_minus, here, from_plus, side_minus, side_plus, code, radial_in, axial, stem, entry,
    out_minus, out_here, out_plus, collar_out, weight, table, seg_head, seg_cond, uptake,
):
    for dx in range(3):
        for dy in range(3):
            if dy == 1:
                source, at = ((from_plus, here, from_minus)[dx], 16)
            else:
                source, at = ((side_plus, None, side_minus)[dy], (2 - dx) * 16)
            for field in range(2):
                to = field * 72 + (dx * 3 + dy) * 8
                table[to : to + 8, :] = source[at + field * 8 : at + field * 8 + 8, :]
    weight[:, 0:128], weight[:, 128:256] = split(table[...])
    columns = lax.broadcasted_iota(I32, (128, LANES), 0).astype(F32).astype(BF16)
    rows = lax.broadcasted_iota(I32, (SLOTS, LANES), 0)
    one, zero = (jnp.ones((), BF16), jnp.zeros((), BF16))
    for j in range(0, BLOCKS, 2):
        picks = []
        for i in (j, j + 1):
            wanted = jnp.broadcast_to((code[i : i + 1, :] & 127).astype(F32).astype(BF16), (128, LANES))
            picks.append(jnp.where(columns == wanted, one, zero))
        pick = jnp.concatenate(picks, 1)
        got = lax.dot_general(
            weight[...],
            jnp.concatenate([pick, pick], 0),
            (((1,), (0,)), ((), ())),
            preferred_element_type=F32,
        )
        for n, i in enumerate((j, j + 1)):
            mask = rows == (code[i : i + 1, :] >> 7)
            for field, ref in enumerate((seg_head, seg_cond)):
                part = got[field * 72 : field * 72 + 72, n * 128 : n * 128 + 128]
                ref[i : i + 1, :] = jnp.sum(jnp.where(mask, part, 0.0), 0, keepdims=True)
    group = 32
    lane = lax.broadcasted_iota(I32, (group, LANES), 1)
    plant_row = lax.broadcasted_iota(I32, (group // 8, 1), 0)
    collar_line = jnp.zeros((1, LANES), F32)
    for g in range(BLOCKS // group):
        at = slice(g * group, g * group + group)
        sub = lax.broadcasted_iota(I32, (group, LANES), 0) + g * group
        own = sub == lane
        stem_col = jnp.sum(jnp.where(own, stem[...], 0.0), 1, keepdims=True)
        entry_col = jnp.sum(jnp.where(own, entry[...], 0), 1, keepdims=True)
        hs, ks, rr = (seg_head[at, :], seg_cond[at, :], radial_in[at, :])
        radial = rr * ks / (rr + ks)
        right = jnp.where(lane == 127, 0.0, axial[at, :])
        left = pltpu.roll(right, 1, 1)
        second = jnp.where(lane == entry_col, stem_col, 0.0)
        first = radial * hs
        diagonal = radial + second + left + right
        lower, upper = (-left, -right)
        for step in range(7):
            stride = 2**step
            inverse = 1.0 / diagonal
            low = -lower * pltpu.roll(inverse, stride, 1)
            high = -upper * pltpu.roll(inverse, 128 - stride, 1)
            first, second = (
                x + low * pltpu.roll(x, stride, 1) + high * pltpu.roll(x, 128 - stride, 1)
                for x in (first, second)
            )
            diagonal = diagonal + low * lower + high * upper
            if step < 6:
                lower = low * pltpu.roll(lower, stride, 1)
                upper = high * pltpu.roll(upper, 128 - stride, 1)
        inverse = 1.0 / diagonal
        free, collar = (first * inverse, second * inverse)

        def per_plant(x):
            return jnp.sum(jnp.sum(x.reshape(group // 8, 8, LANES), 1), 1, keepdims=True)

        need = jnp.zeros((group // 8, 1), F32)
        for p in range(group // 8):
            need = jnp.where(plant_row == p, demand[g * (group // 8) + p], need)
        head = (per_plant(radial * (hs - free)) - need) / per_plant(radial * collar)
        spread = jnp.broadcast_to(head[:, None, :], (group // 8, 8, LANES)).reshape(group, LANES)
        uptake[at, :] = radial * (hs - (free + spread * collar))
        mine = lax.broadcasted_iota(I32, (group // 8, LANES), 1) == plant_row + g * (group // 8)
        collar_line = collar_line + jnp.sum(jnp.where(mine, head, 0.0), 0, keepdims=True)
    collar_out[...] = collar_line
    slot_rows = lax.broadcasted_iota(I32, (80, LANES), 0).astype(F32).astype(BF16)
    slot_cols = columns
    total = jnp.zeros((160, LANES), F32)
    for start in range(0, BLOCKS, 8):
        values, places = ([], [])
        for i in range(start, start + 8):
            where = code[i : i + 1, :]
            hi, lo = split(uptake[i : i + 1, :])
            mask = slot_rows == jnp.broadcast_to((where >> 7).astype(F32).astype(BF16), (80, LANES))
            values.append(
                jnp.concatenate(
                    [jnp.where(mask, jnp.broadcast_to(v, (80, LANES)), zero) for v in (hi, lo)], 0
                )
            )
            wanted = jnp.broadcast_to((where & 127).astype(F32).astype(BF16), (128, LANES))
            places.append(jnp.where(slot_cols == wanted, one, zero))
        total = total + lax.dot_general(
            jnp.concatenate(values, 1),
            jnp.concatenate(places, 1),
            (((1,), (1,)), ((), ())),
            preferred_element_type=F32,
        )
    summed = total[0:72] + total[80:152]
    for dx in range(3):
        for dy, out in enumerate((out_minus, out_here, out_plus)):
            k = dx * 3 + dy
            out[dx * 8 : dx * 8 + 8, :] = summed[k * 8 : k * 8 + 8]


def sink_of(pieces, row, col):
    low_rows = lax.broadcasted_iota(I32, (128, LANES), 0).astype(F32).astype(BF16)
    places_of = lax.broadcasted_iota(I32, (256, LANES), 0).astype(F32).astype(BF16)
    one, zero = (jnp.ones((), BF16), jnp.zeros((), BF16))
    total = jnp.zeros((256, 256), F32)
    for k, (source, base) in pieces.items():
        values, places = ([], [])
        for chunk in range(8):
            i = k * 8 + chunk
            r, c = (row[i : i + 1, :], col[i : i + 1, :])
            hi, lo = split(source[base + chunk : base + chunk + 1, :])
            mask = low_rows == jnp.broadcast_to((r & 127).astype(F32).astype(BF16), (128, LANES))
            values.append(
                jnp.concatenate(
                    [jnp.where(mask, jnp.broadcast_to(v, (128, LANES)), zero) for v in (hi, lo)], 0
                )
            )
            wanted = ((r >> 7) * 128 + c).astype(F32).astype(BF16)
            places.append(jnp.where(places_of == jnp.broadcast_to(wanted, (256, LANES)), one, zero))
        total = total + lax.dot_general(
            jnp.concatenate(values, 1),
            jnp.concatenate(places, 1),
            (((1,), (1,)), ((), ())),
            preferred_element_type=F32,
        )
    return total[0:128] + total[128:256]


def new_head(from_minus, from_plus, row, col, numerator, denominator, head_new):
    pieces = {}
    for dx, source in ((0, from_minus), (2, from_plus)):
        for dy in range(3):
            pieces[dx * 3 + dy] = (source, dy * 8)
    sink = sink_of(pieces, row, col)
    for half in range(2):
        at = slice(half * 128, half * 128 + 128)
        head_new[at, :] = (numerator[at, :] - SINK_GAIN * sink[:, at]) / denominator[at, :]


def next_kernel(
    from_minus, from_plus, row, col, numerator, denominator, sat, alpha_dry, wet,
    head, cond, minus, plus, edge_minus, edge_plus, weight,
):
    new_head(from_minus, from_plus, row, col, numerator, denominator, head)
    for layer in range(LAYERS):
        at = slice(layer * 8, layer * 8 + 8)
        cond[at, :] = conduct(head[at, :], sat[at, :], alpha_dry[at, :] * (1.0 + wet[at, :].astype(F32)))
    lay_cells(head, cond, weight, minus, plus, edge_minus, edge_plus)
    gather_cells(row, col, weight, (minus, None, plus))


def last_kernel(from_minus, from_plus, row, col, numerator, denominator, head):
    new_head(from_minus, from_plus, row, col, numerator, denominator, head)


def call(kernel, outs, scratch=(), specs=None, micros=1):
    shapes = [jax.ShapeDtypeStruct(shape, dtype) for shape, dtype in outs]
    return pl.pallas_call(
        kernel,
        out_shape=shapes,
        scratch_shapes=[pltpu.VMEM(*x) if isinstance(x, tuple) else x for x in scratch],
        compiler_params=pltpu.CompilerParams(vmem_limit_bytes=VMEM_LIMIT),
        cost_estimate=pl.CostEstimate(
            flops=micros * 10**9, bytes_accessed=micros * 3 * 10**6, transcendentals=0
        ),
        **({} if specs is None else {"in_specs": specs}),
    )


WEIGHT = ((256, 512), BF16)
MESSAGES = [((112, 128), F32), ((112, 128), F32), ((8, 128), F32), ((8, 128), F32), WEIGHT]


def up(x, axis):
    size = lax.axis_size(axis)
    return lax.ppermute(x, axis, [(i, (i + 1) % size) for i in range(size)])


def down(x, axis):
    size = lax.axis_size(axis)
    return lax.ppermute(x, axis, [((i + 1) % size, i) for i in range(size)])


def spread(row, col, minus, plus, edge_minus, edge_plus, weight):
    from_minus = up(plus, "gx")
    from_plus = down(minus, "gx")
    (here,) = call(here_kernel, [((48, 128), F32)])(row, col, weight)
    side_minus = up(
        jnp.concatenate([from_minus[32:48], here[32:48], from_plus[32:48], edge_plus], 0), "gy"
    )
    side_plus = down(
        jnp.concatenate([from_minus[0:16], here[0:16], from_plus[0:16], edge_minus], 0), "gy"
    )
    return (from_minus, here, from_plus, side_minus, side_plus)


def give_back(minus, here, plus):
    back_minus = up(minus, "gy")
    back_plus = down(plus, "gy")
    from_minus = up(jnp.concatenate([x[0:8] for x in (back_minus, here, back_plus)], 0), "gx")
    from_plus = down(jnp.concatenate([x[16:24] for x in (back_minus, here, back_plus)], 0), "gx")
    return ((back_minus, here, back_plus), (from_minus, from_plus))


def on_device(
    head_start,
    sat_conduct,
    alpha_dry,
    wet_flag,
    reversal_head,
    send_row,
    send_col,
    root_radial,
    root_axial,
    stem_link,
    entry_seg,
    source_dev,
    source_slot,
    demand,
):
    tile = head_start.shape
    head, sat, alpha, wet, reversal = (
        x.reshape(CELLS, LANES) for x in (head_start, sat_conduct, alpha_dry, wet_flag, reversal_head)
    )
    rows_gx = lax.axis_size("gx")
    cols_gy = lax.axis_size("gy")
    offset_k = (lax.axis_index("gx") - source_dev // cols_gy + 1) % rows_gx * 3 + (
        lax.axis_index("gy") - source_dev % cols_gy + 1
    ) % cols_gy
    code = offset_k * send_row.shape[2] + source_slot
    stem, entry = (stem_link.reshape(1, BLOCKS), entry_seg.reshape(1, BLOCKS))
    head_old = head
    far = pl.BlockSpec(memory_space=pltpu.HBM)
    tile_scratch = [((CELLS, LANES), F32)] * 3 + [((CELLS, LANES), I32)] + [(send_row.shape, I32)] * 2
    cond, row, col, *messages = call(
        start_kernel,
        [((CELLS, LANES), F32), ((SLOTS, LANES), I32), ((SLOTS, LANES), I32)] + MESSAGES,
        tile_scratch + [pltpu.SemaphoreType.DMA((6,))],
        specs=[far] * 6,
        micros=4,
    )(head, sat, alpha, wet, send_row, send_col)
    smem = [pl.BlockSpec(memory_space=pltpu.SMEM)] + [pl.BlockSpec(memory_space=pltpu.VMEM)] * 10
    for iteration in range(PICARD):
        got = spread(row, col, *messages)
        *sums, collar = call(
            root_kernel,
            [((24, 128), F32)] * 3 + [((1, 128), F32)],
            [((144, 256), BF16), ((144, 128), F32)] + [((128, 128), F32)] * 3,
            specs=smem,
            micros=6,
        )(demand, *got, code, root_radial, root_axial, stem, entry)
        near, far_back = give_back(*sums)
        numerator, denominator = call(
            terms_kernel,
            [((CELLS, LANES), F32)] * 2,
            [((128, 128), F32)],
        )(head, cond, head_old, alpha, wet, reversal, got[0], got[2], got[3], got[4], *near, row, col)
        if iteration < PICARD - 1:
            head, cond, *messages = call(
                next_kernel, [((CELLS, LANES), F32)] * 2 + MESSAGES, micros=5
            )(*far_back, row, col, numerator, denominator, sat, alpha, wet)
        else:
            (head,) = call(last_kernel, [((CELLS, LANES), F32)])(
                *far_back, row, col, numerator, denominator
            )
    return (head.reshape(tile), collar[0, :PLANTS])


def solution(mesh):
    tile, lists, blocks, line = (
        P(None, "gx", "gy"),
        P(("gx", "gy"), None, None),
        P(("gx", "gy"), None),
        P(("gx", "gy")),
    )
    return jax.shard_map(
        on_device,
        mesh=mesh,
        in_specs=(tile,) * 5 + (lists,) * 2 + (blocks,) * 2 + (line,) * 2 + (blocks,) * 2 + (line,),
        out_specs=(tile, line),
        check_vma=False,
    )
```

```python
import jax
import jax.numpy as jnp
from jax import lax
from jax.experimental import pallas as pl
from jax.experimental.pallas import tpu as pltpu
from jax.sharding import PartitionSpec as P

PICARD = 2
PORE_INDEX = 1.6
PORE_POWER = 0.375
SPAN_THETA = 0.35
STORAGE = 0.01
SINK_GAIN = 4.0

F32, BF16, I32 = (jnp.float32, jnp.bfloat16, jnp.int32)
VMEM_LIMIT = 48 * 2**20
LAYERS, CELLS, LANES, SLOTS, BLOCKS, PLANTS = (32, 256, 128, 72, 128, 16)


def split(x):
    hi = x.astype(BF16)
    return (hi, (x - hi.astype(F32)).astype(BF16))


def conduct(head, sat_conduct, alpha):
    power = jnp.exp(PORE_INDEX * jnp.log(alpha * jnp.abs(head)))
    root = jnp.exp((-0.5 * PORE_POWER) * jnp.log(1.0 + power))
    inner = 1.0 - jnp.exp(-PORE_POWER * jnp.log(1.0 + 1.0 / power))
    return sat_conduct * root * inner * inner


def capacity(head, alpha_dry, wetting, reversal_head):
    alpha = alpha_dry * (1.0 + wetting)
    log_scaled = jnp.log(alpha * jnp.abs(head))
    log_term = jnp.log(1.0 + jnp.exp(PORE_INDEX * log_scaled))
    slope = (
        (PORE_POWER * PORE_INDEX)
        * alpha
        * jnp.exp((PORE_INDEX - 1.0) * log_scaled + (-PORE_POWER - 1.0) * log_term)
    )
    turned = jnp.exp(PORE_INDEX * jnp.log(alpha_dry * jnp.abs(reversal_head)))
    ratio = jnp.exp(PORE_POWER * (jnp.log(1.0 + 2.0**PORE_INDEX * turned) - jnp.log(1.0 + turned)))
    factor = wetting * ratio + (1.0 - wetting)
    return SPAN_THETA * factor * slope + STORAGE


def x_places():
    odd = lax.rem(lax.axis_index("gx"), 2)
    return (2 - 2 * odd, 2 * odd)


def lay_cells(head, cond, weight, chip, cross, edge_minus, edge_plus):
    even = x_places()[0] == 2
    for field, ref in enumerate((head, cond)):
        for half in range(2):
            turned = ref[half * 128 : half * 128 + 128, :].T
            edge_minus[field * 2 + half : field * 2 + half + 1, :] = turned[0:1]
            edge_plus[field * 2 + half : field * 2 + half + 1, :] = turned[127:128]
            hi, lo = split(turned)
            weight[field * 128 : field * 128 + 128, half * 128 : half * 128 + 128] = hi
            weight[field * 128 : field * 128 + 128, 256 + half * 128 : 384 + half * 128] = lo
        first = ref[pl.ds(0, LAYERS, stride=8), :]
        last = ref[pl.ds(7, LAYERS, stride=8), :]
        chip[48 + 32 * field : 80 + 32 * field, :] = jnp.where(even, last, first)
        cross[48 + 32 * field : 80 + 32 * field, :] = jnp.where(even, first, last)
    edge_minus[4:8, :] = jnp.zeros((4, LANES), F32)
    edge_plus[4:8, :] = jnp.zeros((4, LANES), F32)


def eight(ref, at):
    return ref[pl.ds(pl.multiple_of(at, 8), 8), :]


def gather_cells(row, col, weight, outs):
    cells = lax.broadcasted_iota(I32, (CELLS, LANES), 0).astype(F32).astype(BF16)
    columns = lax.broadcasted_iota(I32, (LANES, LANES), 0)
    one, zero = (jnp.ones((), BF16), jnp.zeros((), BF16))
    for out, place in outs:
        for dy in range(3):
            rows8, cols8 = (eight(x, (place * 3 + dy) * 8) for x in (row, col))
            for chunk in range(0, 8, 2):
                picks = []
                for i in (chunk, chunk + 1):
                    wanted = rows8[i : i + 1].astype(F32).astype(BF16)
                    wanted = jnp.broadcast_to(wanted, (CELLS, LANES))
                    picks.append(jnp.where(cells == wanted, one, zero))
                pick = jnp.concatenate(picks, 1)
                got = lax.dot_general(
                    weight[...],
                    jnp.concatenate([pick, pick], 0),
                    (((1,), (0,)), ((), ())),
                    preferred_element_type=F32,
                )
                for n, i in enumerate((chunk, chunk + 1)):
                    mask = columns == cols8[i : i + 1]
                    for field in range(2):
                        part = got[field * 128 : field * 128 + 128, n * 128 : n * 128 + 128]
                        at = dy * 16 + field * 8 + i
                        out[at : at + 1, :] = jnp.sum(jnp.where(mask, part, 0.0), 0, keepdims=True)


def here_kernel(row, col, weight, _, here):
    gather_cells(row, col, weight, ((here, 1),))


def gather_far(head, cond, row, col, weight, chip, cross, edge_minus, edge_plus):
    lay_cells(head, cond, weight, chip, cross, edge_minus, edge_plus)
    chip_place, cross_place = x_places()
    gather_cells(row, col, weight, ((chip, chip_place), (cross, cross_place)))


def start_kernel(head, cond, row, col, chip, cross, edge_minus, edge_plus, weight):
    gather_far(head, cond, row, col, weight, chip, cross, edge_minus, edge_plus)


def terms_kernel(
    head, cond, head_old, alpha_dry, wet, reversal, chip, cross, side_minus, side_plus,
    back_minus, back_here, back_plus, row, col,
    numerator, denominator, halo,
):
    pieces = [(x, 8, 3 + dy) for dy, x in enumerate((back_minus, back_here, back_plus))]
    sink = SINK_GAIN * sink_of(pieces, row, col)
    even = x_places()[0] == 2
    from_plus = jnp.where(even, chip[48:112, :], cross[48:112, :])
    from_minus = jnp.where(even, cross[48:112, :], chip[48:112, :])
    halo[...] = jnp.zeros_like(halo)
    turned = []
    for i in range(4):
        halo[0:1, :] = side_minus[48 + i : 49 + i, :]
        halo[127:128, :] = side_plus[48 + i : 49 + i, :]
        turned.append(halo[...].T)
    sub = lax.broadcasted_iota(I32, (8, LANES), 0)
    lane = lax.broadcasted_iota(I32, (8, LANES), 1)
    for layer in range(LAYERS):
        at = slice(layer * 8, layer * 8 + 8)
        h, c = (head[at, :], cond[at, :])
        cap = capacity(h, alpha_dry[at, :], wet[at, :].astype(F32), reversal[at, :])
        num, den = (cap * head_old[at, :], cap)
        local = slice(layer % 16 * 8, layer % 16 * 8 + 8)
        halo_h, halo_c = (turned[layer // 16][local], turned[2 + layer // 16][local])

        def add(num, den, near_h, near_c):
            face = 0.5 * (c + near_c)
            return (num + face * near_h, den + face)

        def beside(x, line, spot):
            return jnp.where(sub == spot, jnp.broadcast_to(line, (8, LANES)), x)

        num, den = add(
            num, den,
            beside(pltpu.roll(h, 7, 0), from_plus[layer : layer + 1], 7),
            beside(pltpu.roll(c, 7, 0), from_plus[32 + layer : 33 + layer], 7),
        )
        num, den = add(
            num, den,
            beside(pltpu.roll(h, 1, 0), from_minus[layer : layer + 1], 0),
            beside(pltpu.roll(c, 1, 0), from_minus[32 + layer : 33 + layer], 0),
        )
        num, den = add(
            num, den,
            jnp.where(lane == 127, halo_h, pltpu.roll(h, 127, 1)),
            jnp.where(lane == 127, halo_c, pltpu.roll(c, 127, 1)),
        )
        num, den = add(
            num, den,
            jnp.where(lane == 0, halo_h, pltpu.roll(h, 1, 1)),
            jnp.where(lane == 0, halo_c, pltpu.roll(c, 1, 1)),
        )
        if layer > 0:
            above = slice(layer * 8 - 8, layer * 8)
            num, den = add(num, den, head[above, :] + 1.0, cond[above, :])
        if layer < LAYERS - 1:
            below = slice(layer * 8 + 8, layer * 8 + 16)
            num, den = add(num, den, head[below, :] - 1.0, cond[below, :])
        else:
            num = num - c
        half = layer // 16
        numerator[at, :] = num - sink[local, half * 128 : half * 128 + 128]
        denominator[at, :] = den


def root_kernel(
    chip, here, cross, side_minus, side_plus, code, radial_in, axial, lines,
    out_minus, out_here, out_plus, collar_out, weight, table, seg_head, seg_cond, uptake, summed,
):
    cross_place, chip_place = x_places()
    places = (chip_place, 1, cross_place)
    for n, place in enumerate(places):
        for dy in range(3):
            if dy == 1:
                source, at = ((chip, here, cross)[n], 16)
            else:
                source, at = ((side_plus, None, side_minus)[dy], n * 16)
            for field in range(2):
                to = pl.multiple_of(field * 72 + (place * 3 + dy) * 8, 8)
                table[pl.ds(to, 8), :] = source[at + field * 8 : at + field * 8 + 8, :]
    weight[:, 0:128], weight[:, 128:256] = split(table[...])
    columns = lax.broadcasted_iota(I32, (128, LANES), 0).astype(F32).astype(BF16)
    rows = lax.broadcasted_iota(I32, (SLOTS, LANES), 0)
    one, zero = (jnp.ones((), BF16), jnp.zeros((), BF16))
    for j in range(0, BLOCKS, 2):
        picks = []
        for i in (j, j + 1):
            wanted = jnp.broadcast_to((code[i : i + 1, :] & 127).astype(F32).astype(BF16), (128, LANES))
            picks.append(jnp.where(columns == wanted, one, zero))
        pick = jnp.concatenate(picks, 1)
        got = lax.dot_general(
            weight[...],
            jnp.concatenate([pick, pick], 0),
            (((1,), (0,)), ((), ())),
            preferred_element_type=F32,
        )
        for n, i in enumerate((j, j + 1)):
            mask = rows == (code[i : i + 1, :] >> 7)
            for field, ref in enumerate((seg_head, seg_cond)):
                part = got[field * 72 : field * 72 + 72, n * 128 : n * 128 + 128]
                ref[i : i + 1, :] = jnp.sum(jnp.where(mask, part, 0.0), 0, keepdims=True)
    group = 32
    lane = lax.broadcasted_iota(I32, (group, LANES), 1)
    plant_row = lax.broadcasted_iota(I32, (group // 8, 1), 0)
    collar_line = jnp.zeros((1, LANES), F32)
    for g in range(BLOCKS // group):
        at = slice(g * group, g * group + group)
        sub = lax.broadcasted_iota(I32, (group, LANES), 0) + g * group
        own = sub == lane
        stem_col = jnp.sum(jnp.where(own, lines[0:1, :], 0.0), 1, keepdims=True)
        entry_col = jnp.sum(jnp.where(own, lines[1:2, :], 0.0), 1, keepdims=True)
        hs, ks, rr = (seg_head[at, :], seg_cond[at, :], radial_in[at, :])
        radial = rr * ks / (rr + ks)
        right = jnp.where(lane == 127, 0.0, axial[at, :])
        left = pltpu.roll(right, 1, 1)
        second = jnp.where(lane.astype(F32) == entry_col, stem_col, 0.0)
        first = radial * hs
        diagonal = radial + second + left + right
        lower, upper = (-left, -right)
        for step in range(7):
            stride = 2**step
            inverse = 1.0 / diagonal
            low = -lower * pltpu.roll(inverse, stride, 1)
            high = -upper * pltpu.roll(inverse, 128 - stride, 1)
            first, second = (
                x + low * pltpu.roll(x, stride, 1) + high * pltpu.roll(x, 128 - stride, 1)
                for x in (first, second)
            )
            diagonal = diagonal + low * lower + high * upper
            if step < 6:
                lower = low * pltpu.roll(lower, stride, 1)
                upper = high * pltpu.roll(upper, 128 - stride, 1)
        inverse = 1.0 / diagonal
        free, collar = (first * inverse, second * inverse)

        def per_plant(x):
            return jnp.sum(jnp.sum(x.reshape(group // 8, 8, LANES), 1), 1, keepdims=True)

        mine = lax.broadcasted_iota(I32, (group // 8, LANES), 1) == plant_row + g * (group // 8)
        need = jnp.sum(jnp.where(mine, lines[2:3, :], 0.0), 1, keepdims=True)
        head = (per_plant(radial * (hs - free)) - need) / per_plant(radial * collar)
        spread = jnp.broadcast_to(head[:, None, :], (group // 8, 8, LANES)).reshape(group, LANES)
        uptake[at, :] = radial * (hs - (free + spread * collar))
        collar_line = collar_line + jnp.sum(jnp.where(mine, head, 0.0), 0, keepdims=True)
    collar_out[...] = collar_line[:, 0:PLANTS]
    slot_rows = lax.broadcasted_iota(I32, (80, LANES), 0).astype(F32).astype(BF16)
    slot_cols = columns
    total = jnp.zeros((160, LANES), F32)
    for start in range(0, BLOCKS, 8):
        values, spots = ([], [])
        for i in range(start, start + 8):
            where = code[i : i + 1, :]
            hi, lo = split(uptake[i : i + 1, :])
            mask = slot_rows == jnp.broadcast_to((where >> 7).astype(F32).astype(BF16), (80, LANES))
            values.append(
                jnp.concatenate(
                    [jnp.where(mask, jnp.broadcast_to(v, (80, LANES)), zero) for v in (hi, lo)], 0
                )
            )
            wanted = jnp.broadcast_to((where & 127).astype(F32).astype(BF16), (128, LANES))
            spots.append(jnp.where(slot_cols == wanted, one, zero))
        total = total + lax.dot_general(
            jnp.concatenate(values, 1),
            jnp.concatenate(spots, 1),
            (((1,), (1,)), ((), ())),
            preferred_element_type=F32,
        )
    summed[...] = total[0:72] + total[80:152]
    for n, place in enumerate(places):
        for dy, out in enumerate((out_minus, out_here, out_plus)):
            out[n * 8 : n * 8 + 8, :] = eight(summed, (place * 3 + dy) * 8)


def sink_of(pieces, row, col):
    low_rows = lax.broadcasted_iota(I32, (128, LANES), 0).astype(F32).astype(BF16)
    places_of = lax.broadcasted_iota(I32, (256, LANES), 0).astype(F32).astype(BF16)
    one, zero = (jnp.ones((), BF16), jnp.zeros((), BF16))
    total = jnp.zeros((256, 256), F32)
    for source, base, k in pieces:
        values, places = ([], [])
        rows8, cols8 = (eight(x, k * 8) for x in (row, col))
        for chunk in range(8):
            r, c = (rows8[chunk : chunk + 1], cols8[chunk : chunk + 1])
            hi, lo = split(source[base + chunk : base + chunk + 1, :])
            mask = low_rows == jnp.broadcast_to((r & 127).astype(F32).astype(BF16), (128, LANES))
            values.append(
                jnp.concatenate(
                    [jnp.where(mask, jnp.broadcast_to(v, (128, LANES)), zero) for v in (hi, lo)], 0
                )
            )
            wanted = ((r >> 7) * 128 + c).astype(F32).astype(BF16)
            places.append(jnp.where(places_of == jnp.broadcast_to(wanted, (256, LANES)), one, zero))
        total = total + lax.dot_general(
            jnp.concatenate(values, 1),
            jnp.concatenate(places, 1),
            (((1,), (1,)), ((), ())),
            preferred_element_type=F32,
        )
    return total[0:128] + total[128:256]


def new_head(chip, cross, row, col, numerator, denominator, head_new):
    places = x_places()
    pieces = [
        (source, dy * 8, places[n] * 3 + dy)
        for n, source in enumerate((chip, cross))
        for dy in range(3)
    ]
    sink = sink_of(pieces, row, col)
    for half in range(2):
        at = slice(half * 128, half * 128 + 128)
        head_new[at, :] = (numerator[at, :] - SINK_GAIN * sink[:, at]) / denominator[at, :]


def next_kernel(
    chip_in, cross_in, row, col, numerator, denominator, sat, alpha_dry, wet,
    head, cond, chip, cross, edge_minus, edge_plus, weight,
):
    new_head(chip_in, cross_in, row, col, numerator, denominator, head)
    for layer in range(LAYERS):
        at = slice(layer * 8, layer * 8 + 8)
        cond[at, :] = conduct(head[at, :], sat[at, :], alpha_dry[at, :] * (1.0 + wet[at, :].astype(F32)))
    gather_far(head, cond, row, col, weight, chip, cross, edge_minus, edge_plus)


def last_kernel(chip, cross, row, col, numerator, denominator, head):
    new_head(chip, cross, row, col, numerator, denominator, head)


def call(kernel, outs, scratch=(), specs=None, micros=1):
    shapes = [jax.ShapeDtypeStruct(shape, dtype) for shape, dtype in outs]
    return pl.pallas_call(
        kernel,
        out_shape=shapes,
        scratch_shapes=[pltpu.VMEM(*x) if isinstance(x, tuple) else x for x in scratch],
        compiler_params=pltpu.CompilerParams(vmem_limit_bytes=VMEM_LIMIT),
        cost_estimate=pl.CostEstimate(
            flops=micros * 10**9, bytes_accessed=micros * 3 * 10**6, transcendentals=0
        ),
        **({} if specs is None else {"in_specs": specs}),
    )


WEIGHT = ((256, 512), BF16)
MESSAGES = [((112, 128), F32), ((112, 128), F32), ((8, 128), F32), ((8, 128), F32), WEIGHT]


def up(x, axis):
    size = lax.axis_size(axis)
    return lax.ppermute(x, axis, [(i, (i + 1) % size) for i in range(size)])


def down(x, axis):
    size = lax.axis_size(axis)
    return lax.ppermute(x, axis, [((i + 1) % size, i) for i in range(size)])


def swap(x, axis, first):
    size = lax.axis_size(axis)
    pairs = [((first + i) % size, (first + i + 1) % size) for i in range(0, size, 2)]
    return lax.ppermute(x, axis, [p for i, j in pairs for p in ((i, j), (j, i))])


def spread(row, col, chip, cross, edge_minus, edge_plus, weight):
    from_cross = swap(cross, "gx", 1)
    from_chip = swap(chip, "gx", 0)
    (here,) = call(here_kernel, [((48, 128), F32)])(row, col, weight, from_chip)
    parts = (from_chip, here, from_cross)
    side_minus = up(jnp.concatenate([x[32:48] for x in parts] + [edge_plus], 0), "gy")
    side_plus = down(jnp.concatenate([x[0:16] for x in parts] + [edge_minus], 0), "gy")
    return (*parts, side_minus, side_plus)


def give_back(minus, here, plus):
    back = (up(minus, "gy"), here, down(plus, "gy"))
    from_cross = swap(jnp.concatenate([x[16:24] for x in back], 0), "gx", 1)
    from_chip = swap(jnp.concatenate([x[0:8] for x in back], 0), "gx", 0)
    return (back, (from_chip, from_cross))


def on_device(
    head_start,
    sat_conduct,
    alpha_dry,
    wet_flag,
    reversal_head,
    send_row,
    send_col,
    root_radial,
    root_axial,
    stem_link,
    entry_seg,
    source_dev,
    source_slot,
    demand,
):
    tile = head_start.shape
    head, sat, alpha, wet, reversal = (
        x.reshape(CELLS, LANES) for x in (head_start, sat_conduct, alpha_dry, wet_flag, reversal_head)
    )
    rows_gx = lax.axis_size("gx")
    cols_gy = lax.axis_size("gy")
    offset_k = (lax.axis_index("gx") - source_dev // cols_gy + 1) % rows_gx * 3 + (
        lax.axis_index("gy") - source_dev % cols_gy + 1
    ) % cols_gy
    code = offset_k * send_row.shape[2] + source_slot
    lines = jnp.stack(
        (stem_link, entry_seg.astype(F32), jnp.pad(demand, (0, BLOCKS - demand.shape[0])))
    )
    row, col = (x.reshape(SLOTS, LANES) for x in (send_row, send_col))
    head_old = head
    cond = conduct(head, sat, alpha * (1.0 + wet.astype(F32)))
    messages = call(start_kernel, MESSAGES, micros=3)(head, cond, row, col)
    for iteration in range(PICARD):
        got = spread(row, col, *messages)
        *sums, collar = call(
            root_kernel,
            [((24, 128), F32)] * 3 + [((1, PLANTS), F32)],
            [((144, 256), BF16), ((144, 128), F32)] + [((128, 128), F32)] * 3 + [((72, 128), F32)],
            micros=6,
        )(*got, code, root_radial, root_axial, lines)
        near, far_back = give_back(*sums)
        numerator, denominator = call(
            terms_kernel,
            [((CELLS, LANES), F32)] * 2,
            [((128, 128), F32)],
        )(head, cond, head_old, alpha, wet, reversal, got[0], got[2], got[3], got[4], *near, row, col)
        if iteration < PICARD - 1:
            head, cond, *messages = call(
                next_kernel, [((CELLS, LANES), F32)] * 2 + MESSAGES, micros=5
            )(*far_back, row, col, numerator, denominator, sat, alpha, wet)
        else:
            (head,) = call(last_kernel, [((CELLS, LANES), F32)])(
                *far_back, row, col, numerator, denominator
            )
    return (head.reshape(tile), collar.reshape(-1))


def solution(mesh):
    tile, lists, blocks, line = (
        P(None, "gx", "gy"),
        P(("gx", "gy"), None, None),
        P(("gx", "gy"), None),
        P(("gx", "gy")),
    )
    return jax.shard_map(
        on_device,
        mesh=mesh,
        in_specs=(tile,) * 5 + (lists,) * 2 + (blocks,) * 2 + (line,) * 2 + (blocks,) * 2 + (line,),
        out_specs=(tile, line),
        check_vma=False,
    )
```

```python
import jax
import jax.numpy as jnp
from jax import lax
from jax.experimental import pallas as pl
from jax.experimental.pallas import tpu as pltpu
from jax.sharding import PartitionSpec as P

PICARD = 2
PORE_INDEX = 1.6
PORE_POWER = 0.375
SPAN_THETA = 0.35
STORAGE = 0.01
SINK_GAIN = 4.0

F32, BF16, I32 = (jnp.float32, jnp.bfloat16, jnp.int32)
VMEM_LIMIT = 48 * 2**20
LAYERS, CELLS, LANES, SLOTS, BLOCKS, PLANTS = (32, 256, 128, 72, 128, 16)


def split(x):
    hi = x.astype(BF16)
    return (hi, (x - hi.astype(F32)).astype(BF16))


def conduct(head, sat_conduct, alpha):
    power = jnp.exp(PORE_INDEX * jnp.log(alpha * jnp.abs(head)))
    root = jnp.exp((-0.5 * PORE_POWER) * jnp.log(1.0 + power))
    inner = 1.0 - jnp.exp(-PORE_POWER * jnp.log(1.0 + 1.0 / power))
    return sat_conduct * root * inner * inner


def capacity(head, alpha_dry, wetting, reversal_head):
    alpha = alpha_dry * (1.0 + wetting)
    log_scaled = jnp.log(alpha * jnp.abs(head))
    log_term = jnp.log(1.0 + jnp.exp(PORE_INDEX * log_scaled))
    slope = (
        (PORE_POWER * PORE_INDEX)
        * alpha
        * jnp.exp((PORE_INDEX - 1.0) * log_scaled + (-PORE_POWER - 1.0) * log_term)
    )
    turned = jnp.exp(PORE_INDEX * jnp.log(alpha_dry * jnp.abs(reversal_head)))
    ratio = jnp.exp(PORE_POWER * (jnp.log(1.0 + 2.0**PORE_INDEX * turned) - jnp.log(1.0 + turned)))
    factor = wetting * ratio + (1.0 - wetting)
    return SPAN_THETA * factor * slope + STORAGE


def x_places():
    odd = lax.rem(lax.axis_index("gx"), 2)
    return (2 - 2 * odd, 2 * odd)


def lay_cells(head, cond, weight, chip, cross, edge_minus, edge_plus):
    even = x_places()[0] == 2
    for field, ref in enumerate((head, cond)):
        for half in range(2):
            turned = ref[half * 128 : half * 128 + 128, :].T
            edge_minus[field * 2 + half : field * 2 + half + 1, :] = turned[0:1]
            edge_plus[field * 2 + half : field * 2 + half + 1, :] = turned[127:128]
            hi, lo = split(turned)
            weight[field * 128 : field * 128 + 128, half * 128 : half * 128 + 128] = hi
            weight[field * 128 : field * 128 + 128, 256 + half * 128 : 384 + half * 128] = lo
        first = ref[pl.ds(0, LAYERS, stride=8), :]
        last = ref[pl.ds(7, LAYERS, stride=8), :]
        at = chip.shape[0] - 64 + 32 * field
        chip[at : at + 32, :] = jnp.where(even, last, first)
        cross[at : at + 32, :] = jnp.where(even, first, last)
    edge_minus[4:8, :] = jnp.zeros((4, LANES), F32)
    edge_plus[4:8, :] = jnp.zeros((4, LANES), F32)


def eight(ref, at):
    return ref[pl.ds(pl.multiple_of(at, 8), 8), :]


def gather_cells(row, col, weight, outs):
    cells = lax.broadcasted_iota(I32, (CELLS, LANES), 0).astype(F32).astype(BF16)
    columns = lax.broadcasted_iota(I32, (LANES, LANES), 0)
    one, zero = (jnp.ones((), BF16), jnp.zeros((), BF16))
    for out, place in outs:
        for dy in range(3):
            rows8, cols8 = (eight(x, (place * 3 + dy) * 8) for x in (row, col))
            for chunk in range(0, 8, 2):
                picks = []
                for i in (chunk, chunk + 1):
                    wanted = rows8[i : i + 1].astype(F32).astype(BF16)
                    wanted = jnp.broadcast_to(wanted, (CELLS, LANES))
                    picks.append(jnp.where(cells == wanted, one, zero))
                pick = jnp.concatenate(picks, 1)
                got = lax.dot_general(
                    weight[...],
                    jnp.concatenate([pick, pick], 0),
                    (((1,), (0,)), ((), ())),
                    preferred_element_type=F32,
                )
                for n, i in enumerate((chunk, chunk + 1)):
                    mask = columns == cols8[i : i + 1]
                    for field in range(2):
                        part = got[field * 128 : field * 128 + 128, n * 128 : n * 128 + 128]
                        at = dy * 16 + field * 8 + i
                        out[at : at + 1, :] = jnp.sum(jnp.where(mask, part, 0.0), 0, keepdims=True)


def gather_far(row, col, weight, chip, cross):
    chip_place, cross_place = x_places()
    gather_cells(row, col, weight, ((cross, cross_place), (chip, chip_place)))


def start_kernel(head, cond, row, col, chip, cross, edge_minus, edge_plus, weight):
    lay_cells(head, cond, weight, chip, cross, edge_minus, edge_plus)
    gather_far(row, col, weight, chip, cross)


def far_kernel(row, col, weight, chip_edge, cross_edge, chip, cross):
    gather_far(row, col, weight, chip, cross)
    chip[48:112, :] = chip_edge[...]
    cross[48:112, :] = cross_edge[...]


def here_kernel(row, col, weight, _, here):
    gather_cells(row, col, weight, ((here, 1),))


def collar_kernel(lines, second):
    sub = lax.broadcasted_iota(I32, (BLOCKS, LANES), 0)
    lane = lax.broadcasted_iota(I32, (BLOCKS, LANES), 1)
    own = sub == lane
    stem = jnp.sum(jnp.where(own, lines[0:1, :], 0.0), 1, keepdims=True)
    entry = jnp.sum(jnp.where(own, lines[1:2, :], 0.0), 1, keepdims=True)
    second[...] = jnp.where(lane.astype(F32) == entry, stem, 0.0)


def terms_kernel(
    head, cond, head_old, alpha_dry, wet, reversal, chip, cross, side_minus, side_plus,
    back_minus, back_here, back_plus, back_chip, row, col,
    numerator, denominator, halo,
):
    pieces = [(x, 8, 3 + dy) for dy, x in enumerate((back_minus, back_here, back_plus))]
    pieces += [(back_chip, dy * 8, x_places()[0] * 3 + dy) for dy in range(3)]
    sink = SINK_GAIN * sink_of(pieces, row, col)
    even = x_places()[0] == 2
    from_plus = jnp.where(even, chip[48:112, :], cross[48:112, :])
    from_minus = jnp.where(even, cross[48:112, :], chip[48:112, :])
    halo[...] = jnp.zeros_like(halo)
    turned = []
    for i in range(4):
        halo[0:1, :] = side_minus[48 + i : 49 + i, :]
        halo[127:128, :] = side_plus[48 + i : 49 + i, :]
        turned.append(halo[...].T)
    sub = lax.broadcasted_iota(I32, (8, LANES), 0)
    lane = lax.broadcasted_iota(I32, (8, LANES), 1)
    for layer in range(LAYERS):
        at = slice(layer * 8, layer * 8 + 8)
        h, c = (head[at, :], cond[at, :])
        cap = capacity(h, alpha_dry[at, :], wet[at, :].astype(F32), reversal[at, :])
        num, den = (cap * head_old[at, :], cap)
        local = slice(layer % 16 * 8, layer % 16 * 8 + 8)
        halo_h, halo_c = (turned[layer // 16][local], turned[2 + layer // 16][local])

        def add(num, den, near_h, near_c):
            face = 0.5 * (c + near_c)
            return (num + face * near_h, den + face)

        def beside(x, line, spot):
            return jnp.where(sub == spot, jnp.broadcast_to(line, (8, LANES)), x)

        num, den = add(
            num, den,
            beside(pltpu.roll(h, 7, 0), from_plus[layer : layer + 1], 7),
            beside(pltpu.roll(c, 7, 0), from_plus[32 + layer : 33 + layer], 7),
        )
        num, den = add(
            num, den,
            beside(pltpu.roll(h, 1, 0), from_minus[layer : layer + 1], 0),
            beside(pltpu.roll(c, 1, 0), from_minus[32 + layer : 33 + layer], 0),
        )
        num, den = add(
            num, den,
            jnp.where(lane == 127, halo_h, pltpu.roll(h, 127, 1)),
            jnp.where(lane == 127, halo_c, pltpu.roll(c, 127, 1)),
        )
        num, den = add(
            num, den,
            jnp.where(lane == 0, halo_h, pltpu.roll(h, 1, 1)),
            jnp.where(lane == 0, halo_c, pltpu.roll(c, 1, 1)),
        )
        if layer > 0:
            above = slice(layer * 8 - 8, layer * 8)
            num, den = add(num, den, head[above, :] + 1.0, cond[above, :])
        if layer < LAYERS - 1:
            below = slice(layer * 8 + 8, layer * 8 + 16)
            num, den = add(num, den, head[below, :] - 1.0, cond[below, :])
        else:
            num = num - c
        half = layer // 16
        numerator[at, :] = num - sink[local, half * 128 : half * 128 + 128]
        denominator[at, :] = den


def root_kernel(
    chip, here, cross, side_minus, side_plus, code, radial_in, axial, lines, collar_link,
    out_minus, out_here, out_plus, collar_out, weight, table, seg_head, seg_cond, uptake, summed,
):
    cross_place, chip_place = x_places()
    places = (chip_place, 1, cross_place)
    for n, place in enumerate(places):
        for dy in range(3):
            if dy == 1:
                source, at = ((chip, here, cross)[n], 16)
            else:
                source, at = ((side_plus, None, side_minus)[dy], n * 16)
            for field in range(2):
                to = pl.multiple_of(field * 72 + (place * 3 + dy) * 8, 8)
                table[pl.ds(to, 8), :] = source[at + field * 8 : at + field * 8 + 8, :]
    weight[:, 0:128], weight[:, 128:256] = split(table[...])
    columns = lax.broadcasted_iota(I32, (128, LANES), 0).astype(F32).astype(BF16)
    rows = lax.broadcasted_iota(I32, (SLOTS, LANES), 0)
    one, zero = (jnp.ones((), BF16), jnp.zeros((), BF16))
    for j in range(0, BLOCKS, 8):
        picks = []
        for i in range(j, j + 8):
            wanted = jnp.broadcast_to((code[i : i + 1, :] & 127).astype(F32).astype(BF16), (128, LANES))
            picks.append(jnp.where(columns == wanted, one, zero))
        pick = jnp.concatenate(picks, 1)
        got = lax.dot_general(
            weight[...],
            jnp.concatenate([pick, pick], 0),
            (((1,), (0,)), ((), ())),
            preferred_element_type=F32,
        )
        for n, i in enumerate(range(j, j + 8)):
            mask = rows == (code[i : i + 1, :] >> 7)
            for field, ref in enumerate((seg_head, seg_cond)):
                part = got[field * 72 : field * 72 + 72, n * 128 : n * 128 + 128]
                ref[i : i + 1, :] = jnp.sum(jnp.where(mask, part, 0.0), 0, keepdims=True)
    group = 32
    lane = lax.broadcasted_iota(I32, (group, LANES), 1)
    plant_row = lax.broadcasted_iota(I32, (group // 8, 1), 0)
    collar_line = jnp.zeros((1, LANES), F32)
    for g in range(BLOCKS // group):
        at = slice(g * group, g * group + group)
        hs, ks, rr = (seg_head[at, :], seg_cond[at, :], radial_in[at, :])
        radial = rr * ks / (rr + ks)
        right = jnp.where(lane == 127, 0.0, axial[at, :])
        left = pltpu.roll(right, 1, 1)
        second = collar_link[at, :]
        first = radial * hs
        diagonal = radial + second + left + right
        lower, upper = (-left, -right)
        for step in range(7):
            stride = 2**step
            inverse = 1.0 / diagonal
            low = -lower * pltpu.roll(inverse, stride, 1)
            high = -upper * pltpu.roll(inverse, 128 - stride, 1)
            first, second = (
                x + low * pltpu.roll(x, stride, 1) + high * pltpu.roll(x, 128 - stride, 1)
                for x in (first, second)
            )
            diagonal = diagonal + low * lower + high * upper
            if step < 6:
                lower = low * pltpu.roll(lower, stride, 1)
                upper = high * pltpu.roll(upper, 128 - stride, 1)
        inverse = 1.0 / diagonal
        free, collar = (first * inverse, second * inverse)

        def per_plant(x):
            return jnp.sum(jnp.sum(x.reshape(group // 8, 8, LANES), 1), 1, keepdims=True)

        mine = lax.broadcasted_iota(I32, (group // 8, LANES), 1) == plant_row + g * (group // 8)
        need = jnp.sum(jnp.where(mine, lines[2:3, :], 0.0), 1, keepdims=True)
        head = (per_plant(radial * (hs - free)) - need) / per_plant(radial * collar)
        spread = jnp.broadcast_to(head[:, None, :], (group // 8, 8, LANES)).reshape(group, LANES)
        uptake[at, :] = radial * (hs - (free + spread * collar))
        collar_line = collar_line + jnp.sum(jnp.where(mine, head, 0.0), 0, keepdims=True)
    collar_out[...] = collar_line[:, 0:PLANTS]
    slot_rows = lax.broadcasted_iota(I32, (80, LANES), 0).astype(F32).astype(BF16)
    slot_cols = columns
    total = jnp.zeros((160, LANES), F32)
    for start in range(0, BLOCKS, 8):
        values, spots = ([], [])
        for i in range(start, start + 8):
            where = code[i : i + 1, :]
            hi, lo = split(uptake[i : i + 1, :])
            mask = slot_rows == jnp.broadcast_to((where >> 7).astype(F32).astype(BF16), (80, LANES))
            values.append(
                jnp.concatenate(
                    [jnp.where(mask, jnp.broadcast_to(v, (80, LANES)), zero) for v in (hi, lo)], 0
                )
            )
            wanted = jnp.broadcast_to((where & 127).astype(F32).astype(BF16), (128, LANES))
            spots.append(jnp.where(slot_cols == wanted, one, zero))
        total = total + lax.dot_general(
            jnp.concatenate(values, 1),
            jnp.concatenate(spots, 1),
            (((1,), (1,)), ((), ())),
            preferred_element_type=F32,
        )
    summed[...] = total[0:72] + total[80:152]
    for n, place in enumerate(places):
        for dy, out in enumerate((out_minus, out_here, out_plus)):
            out[n * 8 : n * 8 + 8, :] = eight(summed, (place * 3 + dy) * 8)


def sink_of(pieces, row, col):
    low_rows = lax.broadcasted_iota(I32, (128, LANES), 0).astype(F32).astype(BF16)
    places_of = lax.broadcasted_iota(I32, (256, LANES), 0).astype(F32).astype(BF16)
    one, zero = (jnp.ones((), BF16), jnp.zeros((), BF16))
    total = jnp.zeros((256, 256), F32)
    for source, base, k in pieces:
        values, places = ([], [])
        rows8, cols8 = (eight(x, k * 8) for x in (row, col))
        for chunk in range(8):
            r, c = (rows8[chunk : chunk + 1], cols8[chunk : chunk + 1])
            hi, lo = split(source[base + chunk : base + chunk + 1, :])
            mask = low_rows == jnp.broadcast_to((r & 127).astype(F32).astype(BF16), (128, LANES))
            values.append(
                jnp.concatenate(
                    [jnp.where(mask, jnp.broadcast_to(v, (128, LANES)), zero) for v in (hi, lo)], 0
                )
            )
            wanted = ((r >> 7) * 128 + c).astype(F32).astype(BF16)
            places.append(jnp.where(places_of == jnp.broadcast_to(wanted, (256, LANES)), one, zero))
        total = total + lax.dot_general(
            jnp.concatenate(values, 1),
            jnp.concatenate(places, 1),
            (((1,), (1,)), ((), ())),
            preferred_element_type=F32,
        )
    return total[0:128] + total[128:256]


def new_head(cross, row, col, numerator, denominator, head_new):
    place = x_places()[1]
    sink = sink_of([(cross, dy * 8, place * 3 + dy) for dy in range(3)], row, col)
    for half in range(2):
        at = slice(half * 128, half * 128 + 128)
        head_new[at, :] = (numerator[at, :] - SINK_GAIN * sink[:, at]) / denominator[at, :]


def next_kernel(
    cross, row, col, numerator, denominator, sat, alpha_dry, wet,
    head, cond, chip_edge, cross_edge, edge_minus, edge_plus, weight,
):
    new_head(cross, row, col, numerator, denominator, head)
    for layer in range(LAYERS):
        at = slice(layer * 8, layer * 8 + 8)
        cond[at, :] = conduct(head[at, :], sat[at, :], alpha_dry[at, :] * (1.0 + wet[at, :].astype(F32)))
    lay_cells(head, cond, weight, chip_edge, cross_edge, edge_minus, edge_plus)


def last_kernel(cross, row, col, numerator, denominator, head):
    new_head(cross, row, col, numerator, denominator, head)


def call(kernel, outs, scratch=(), specs=None, micros=1):
    shapes = [jax.ShapeDtypeStruct(shape, dtype) for shape, dtype in outs]
    return pl.pallas_call(
        kernel,
        out_shape=shapes,
        scratch_shapes=[pltpu.VMEM(*x) if isinstance(x, tuple) else x for x in scratch],
        compiler_params=pltpu.CompilerParams(vmem_limit_bytes=VMEM_LIMIT),
        cost_estimate=pl.CostEstimate(
            flops=micros * 10**9, bytes_accessed=micros * 3 * 10**6, transcendentals=0
        ),
        **({} if specs is None else {"in_specs": specs}),
    )


MESSAGE = ((112, 128), F32)
EDGE = ((64, 128), F32)
SIDES = [((8, 128), F32)] * 2 + [((256, 512), BF16)]


def up(x, axis):
    size = lax.axis_size(axis)
    return lax.ppermute(x, axis, [(i, (i + 1) % size) for i in range(size)])


def down(x, axis):
    size = lax.axis_size(axis)
    return lax.ppermute(x, axis, [((i + 1) % size, i) for i in range(size)])


def swap(x, axis, first):
    size = lax.axis_size(axis)
    pairs = [((first + i) % size, (first + i + 1) % size) for i in range(0, size, 2)]
    return lax.ppermute(x, axis, [p for i, j in pairs for p in ((i, j), (j, i))])


def spread(row, col, chip, cross, edge_minus, edge_plus, weight):
    from_cross = swap(cross, "gx", 1)
    from_chip = swap(chip, "gx", 0)
    (here,) = call(here_kernel, [((48, 128), F32)])(row, col, weight, from_chip)
    parts = (from_chip, here, from_cross)
    side_minus = up(jnp.concatenate([x[32:48] for x in parts] + [edge_plus], 0), "gy")
    side_plus = down(jnp.concatenate([x[0:16] for x in parts] + [edge_minus], 0), "gy")
    return (*parts, side_minus, side_plus)


def give_back(minus, here, plus):
    back = (up(minus, "gy"), here, down(plus, "gy"))
    from_cross = swap(jnp.concatenate([x[16:24] for x in back], 0), "gx", 1)
    from_chip = swap(jnp.concatenate([x[0:8] for x in back], 0), "gx", 0)
    return (back, (from_chip, from_cross))


def on_device(
    head_start,
    sat_conduct,
    alpha_dry,
    wet_flag,
    reversal_head,
    send_row,
    send_col,
    root_radial,
    root_axial,
    stem_link,
    entry_seg,
    source_dev,
    source_slot,
    demand,
):
    tile = head_start.shape
    head, sat, alpha, wet, reversal = (
        x.reshape(CELLS, LANES) for x in (head_start, sat_conduct, alpha_dry, wet_flag, reversal_head)
    )
    rows_gx = lax.axis_size("gx")
    cols_gy = lax.axis_size("gy")
    offset_k = (lax.axis_index("gx") - source_dev // cols_gy + 1) % rows_gx * 3 + (
        lax.axis_index("gy") - source_dev % cols_gy + 1
    ) % cols_gy
    code = offset_k * send_row.shape[2] + source_slot
    lines = jnp.stack(
        (stem_link, entry_seg.astype(F32), jnp.pad(demand, (0, BLOCKS - demand.shape[0])))
    )
    row, col = (x.reshape(SLOTS, LANES) for x in (send_row, send_col))
    head_old = head
    cond = conduct(head, sat, alpha * (1.0 + wet.astype(F32)))
    messages = call(start_kernel, [MESSAGE] * 2 + SIDES, micros=2)(head, cond, row, col)
    (collar_link,) = call(collar_kernel, [((BLOCKS, LANES), F32)])(lines)
    for iteration in range(PICARD):
        got = spread(row, col, *messages)
        *sums, collar = call(
            root_kernel,
            [((24, 128), F32)] * 3 + [((1, PLANTS), F32)],
            [((144, 256), BF16), ((144, 128), F32)] + [((128, 128), F32)] * 3 + [((72, 128), F32)],
            micros=6,
        )(*got, code, root_radial, root_axial, lines, collar_link)
        near, (from_chip, from_cross) = give_back(*sums)
        numerator, denominator = call(
            terms_kernel,
            [((CELLS, LANES), F32)] * 2,
            [((128, 128), F32)],
        )(
            head, cond, head_old, alpha, wet, reversal, got[0], got[2], got[3], got[4],
            *near, from_chip, row, col,
        )
        if iteration < PICARD - 1:
            head, cond, *edges, side_minus, side_plus, weight = call(
                next_kernel, [((CELLS, LANES), F32)] * 2 + [EDGE] * 2 + SIDES, micros=2
            )(from_cross, row, col, numerator, denominator, sat, alpha, wet)
            far = call(far_kernel, [MESSAGE] * 2, micros=2)(row, col, weight, *edges)
            messages = (*far, side_minus, side_plus, weight)
        else:
            (head,) = call(last_kernel, [((CELLS, LANES), F32)])(
                from_cross, row, col, numerator, denominator
            )
    return (head.reshape(tile), collar.reshape(-1))


def solution(mesh):
    tile, lists, blocks, line = (
        P(None, "gx", "gy"),
        P(("gx", "gy"), None, None),
        P(("gx", "gy"), None),
        P(("gx", "gy")),
    )
    return jax.shard_map(
        on_device,
        mesh=mesh,
        in_specs=(tile,) * 5 + (lists,) * 2 + (blocks,) * 2 + (line,) * 2 + (blocks,) * 2 + (line,),
        out_specs=(tile, line),
        check_vma=False,
    )
```

```python
import jax
import jax.numpy as jnp
from jax import lax
from jax.experimental import pallas as pl
from jax.experimental.pallas import tpu as pltpu
from jax.sharding import PartitionSpec as P

PICARD = 2
PORE_INDEX = 1.6
PORE_POWER = 0.375
SPAN_THETA = 0.35
STORAGE = 0.01
SINK_GAIN = 4.0

F32, BF16, I32 = (jnp.float32, jnp.bfloat16, jnp.int32)
VMEM_LIMIT = 48 * 2**20
LAYERS, CELLS, LANES, SLOTS, BLOCKS, PLANTS = (32, 256, 128, 72, 128, 16)


def split(x):
    hi = x.astype(BF16)
    return (hi, (x - hi.astype(F32)).astype(BF16))


def conduct(head, sat_conduct, alpha):
    power = jnp.exp(PORE_INDEX * jnp.log(alpha * jnp.abs(head)))
    root = jnp.exp((-0.5 * PORE_POWER) * jnp.log(1.0 + power))
    inner = 1.0 - jnp.exp(-PORE_POWER * jnp.log(1.0 + 1.0 / power))
    return sat_conduct * root * inner * inner


def capacity(head, alpha_dry, wetting, reversal_head):
    alpha = alpha_dry * (1.0 + wetting)
    log_scaled = jnp.log(alpha * jnp.abs(head))
    log_term = jnp.log(1.0 + jnp.exp(PORE_INDEX * log_scaled))
    slope = (
        (PORE_POWER * PORE_INDEX)
        * alpha
        * jnp.exp((PORE_INDEX - 1.0) * log_scaled + (-PORE_POWER - 1.0) * log_term)
    )
    turned = jnp.exp(PORE_INDEX * jnp.log(alpha_dry * jnp.abs(reversal_head)))
    ratio = jnp.exp(PORE_POWER * (jnp.log(1.0 + 2.0**PORE_INDEX * turned) - jnp.log(1.0 + turned)))
    factor = wetting * ratio + (1.0 - wetting)
    return SPAN_THETA * factor * slope + STORAGE


def x_places():
    odd = lax.rem(lax.axis_index("gx"), 2)
    return (2 - 2 * odd, 2 * odd)


def lay_cells(head, cond, weight, chip_edge, cross, edge_minus, edge_plus):
    even = x_places()[0] == 2
    for field, ref in enumerate((head, cond)):
        for half in range(2):
            turned = ref[half * 128 : half * 128 + 128, :].T
            edge_minus[field * 2 + half : field * 2 + half + 1, :] = turned[0:1]
            edge_plus[field * 2 + half : field * 2 + half + 1, :] = turned[127:128]
            hi, lo = split(turned)
            weight[field * 128 : field * 128 + 128, half * 128 : half * 128 + 128] = hi
            weight[field * 128 : field * 128 + 128, 256 + half * 128 : 384 + half * 128] = lo
        first = ref[pl.ds(0, LAYERS, stride=8), :]
        last = ref[pl.ds(7, LAYERS, stride=8), :]
        chip_edge[32 * field : 32 * field + 32, :] = jnp.where(even, last, first)
        at = cross.shape[0] - 64 + 32 * field
        cross[at : at + 32, :] = jnp.where(even, first, last)
    edge_minus[4:8, :] = jnp.zeros((4, LANES), F32)
    edge_plus[4:8, :] = jnp.zeros((4, LANES), F32)


def eight(ref, at):
    return ref[pl.ds(pl.multiple_of(at, 8), 8), :]


def gather_cells(row, col, weight, outs):
    cells = lax.broadcasted_iota(I32, (CELLS, LANES), 0).astype(F32).astype(BF16)
    columns = lax.broadcasted_iota(I32, (LANES, LANES), 0)
    one, zero = (jnp.ones((), BF16), jnp.zeros((), BF16))
    for out, place in outs:
        for dy in range(3):
            rows8, cols8 = (eight(x, (place * 3 + dy) * 8) for x in (row, col))
            for chunk in range(0, 8, 2):
                picks = []
                for i in (chunk, chunk + 1):
                    wanted = rows8[i : i + 1].astype(F32).astype(BF16)
                    wanted = jnp.broadcast_to(wanted, (CELLS, LANES))
                    picks.append(jnp.where(cells == wanted, one, zero))
                pick = jnp.concatenate(picks, 1)
                got = lax.dot_general(
                    weight[...],
                    jnp.concatenate([pick, pick], 0),
                    (((1,), (0,)), ((), ())),
                    preferred_element_type=F32,
                )
                for n, i in enumerate((chunk, chunk + 1)):
                    mask = columns == cols8[i : i + 1]
                    for field in range(2):
                        part = got[field * 128 : field * 128 + 128, n * 128 : n * 128 + 128]
                        at = dy * 16 + field * 8 + i
                        out[at : at + 1, :] = jnp.sum(jnp.where(mask, part, 0.0), 0, keepdims=True)


def start_kernel(head, cond, row, col, chip_edge, cross, edge_minus, edge_plus, weight):
    lay_cells(head, cond, weight, chip_edge, cross, edge_minus, edge_plus)
    gather_cells(row, col, weight, ((cross, x_places()[1]),))


def cross_kernel(row, col, weight, cross_edge, cross):
    gather_cells(row, col, weight, ((cross, x_places()[1]),))
    cross[48:112, :] = cross_edge[...]


def rest_kernel(row, col, weight, _, chip, here):
    gather_cells(row, col, weight, ((chip, x_places()[0]), (here, 1)))


def collar_kernel(stem, entry, demand, second, need):
    sub = lax.broadcasted_iota(I32, (BLOCKS, LANES), 0)
    lane = lax.broadcasted_iota(I32, (BLOCKS, LANES), 1)
    own = sub == lane
    stem_col = jnp.sum(jnp.where(own, stem[...], 0.0), 1, keepdims=True)
    entry_col = jnp.sum(jnp.where(own, entry[...].astype(F32), 0.0), 1, keepdims=True)
    second[...] = jnp.where(lane.astype(F32) == entry_col, stem_col, 0.0)
    need[...] = jnp.zeros((1, LANES), F32)
    need[:, 0:PLANTS] = demand[...]


def terms_kernel(
    head, cond, head_old, alpha_dry, wet, reversal, chip_edges, cross, side_minus, side_plus,
    back_minus, back_here, back_plus, back_chip, row, col,
    numerator, denominator, halo,
):
    pieces = [(x, 8, 3 + dy) for dy, x in enumerate((back_minus, back_here, back_plus))]
    pieces += [(back_chip, dy * 8, x_places()[0] * 3 + dy) for dy in range(3)]
    sink = SINK_GAIN * sink_of(pieces, row, col)
    even = x_places()[0] == 2
    from_plus = jnp.where(even, chip_edges[...], cross[48:112, :])
    from_minus = jnp.where(even, cross[48:112, :], chip_edges[...])
    halo[...] = jnp.zeros_like(halo)
    turned = []
    for i in range(4):
        halo[0:1, :] = side_minus[48 + i : 49 + i, :]
        halo[127:128, :] = side_plus[48 + i : 49 + i, :]
        turned.append(halo[...].T)
    sub = lax.broadcasted_iota(I32, (8, LANES), 0)
    lane = lax.broadcasted_iota(I32, (8, LANES), 1)
    for layer in range(LAYERS):
        at = slice(layer * 8, layer * 8 + 8)
        h, c = (head[at, :], cond[at, :])
        cap = capacity(h, alpha_dry[at, :], wet[at, :].astype(F32), reversal[at, :])
        num, den = (cap * head_old[at, :], cap)
        local = slice(layer % 16 * 8, layer % 16 * 8 + 8)
        halo_h, halo_c = (turned[layer // 16][local], turned[2 + layer // 16][local])

        def add(num, den, near_h, near_c):
            face = 0.5 * (c + near_c)
            return (num + face * near_h, den + face)

        def beside(x, line, spot):
            return jnp.where(sub == spot, jnp.broadcast_to(line, (8, LANES)), x)

        num, den = add(
            num, den,
            beside(pltpu.roll(h, 7, 0), from_plus[layer : layer + 1], 7),
            beside(pltpu.roll(c, 7, 0), from_plus[32 + layer : 33 + layer], 7),
        )
        num, den = add(
            num, den,
            beside(pltpu.roll(h, 1, 0), from_minus[layer : layer + 1], 0),
            beside(pltpu.roll(c, 1, 0), from_minus[32 + layer : 33 + layer], 0),
        )
        num, den = add(
            num, den,
            jnp.where(lane == 127, halo_h, pltpu.roll(h, 127, 1)),
            jnp.where(lane == 127, halo_c, pltpu.roll(c, 127, 1)),
        )
        num, den = add(
            num, den,
            jnp.where(lane == 0, halo_h, pltpu.roll(h, 1, 1)),
            jnp.where(lane == 0, halo_c, pltpu.roll(c, 1, 1)),
        )
        if layer > 0:
            above = slice(layer * 8 - 8, layer * 8)
            num, den = add(num, den, head[above, :] + 1.0, cond[above, :])
        if layer < LAYERS - 1:
            below = slice(layer * 8 + 8, layer * 8 + 16)
            num, den = add(num, den, head[below, :] - 1.0, cond[below, :])
        else:
            num = num - c
        half = layer // 16
        numerator[at, :] = num - sink[local, half * 128 : half * 128 + 128]
        denominator[at, :] = den


def root_kernel(
    chip, here, cross, side_minus, side_plus, code, radial_in, axial, collar_link, demand,
    out_minus, out_here, out_plus, collar_out, weight, table, seg_head, seg_cond, uptake, summed,
):
    cross_place, chip_place = x_places()
    places = (chip_place, 1, cross_place)
    for n, place in enumerate(places):
        for dy in range(3):
            if dy == 1:
                source, at = ((chip, here, cross)[n], 16)
            else:
                source, at = ((side_plus, None, side_minus)[dy], n * 16)
            for field in range(2):
                to = pl.multiple_of(field * 72 + (place * 3 + dy) * 8, 8)
                table[pl.ds(to, 8), :] = source[at + field * 8 : at + field * 8 + 8, :]
    weight[:, 0:128], weight[:, 128:256] = split(table[...])
    columns = lax.broadcasted_iota(I32, (128, LANES), 0).astype(F32).astype(BF16)
    rows = lax.broadcasted_iota(I32, (SLOTS, LANES), 0)
    one, zero = (jnp.ones((), BF16), jnp.zeros((), BF16))
    for j in range(0, BLOCKS, 8):
        picks = []
        for i in range(j, j + 8):
            wanted = jnp.broadcast_to((code[i : i + 1, :] & 127).astype(F32).astype(BF16), (128, LANES))
            picks.append(jnp.where(columns == wanted, one, zero))
        pick = jnp.concatenate(picks, 1)
        got = lax.dot_general(
            weight[...],
            jnp.concatenate([pick, pick], 0),
            (((1,), (0,)), ((), ())),
            preferred_element_type=F32,
        )
        for n, i in enumerate(range(j, j + 8)):
            mask = rows == (code[i : i + 1, :] >> 7)
            for field, ref in enumerate((seg_head, seg_cond)):
                part = got[field * 72 : field * 72 + 72, n * 128 : n * 128 + 128]
                ref[i : i + 1, :] = jnp.sum(jnp.where(mask, part, 0.0), 0, keepdims=True)
    group = 32
    lane = lax.broadcasted_iota(I32, (group, LANES), 1)
    plant_row = lax.broadcasted_iota(I32, (group // 8, 1), 0)
    collar_line = jnp.zeros((1, LANES), F32)
    for g in range(BLOCKS // group):
        at = slice(g * group, g * group + group)
        hs, ks, rr = (seg_head[at, :], seg_cond[at, :], radial_in[at, :])
        radial = rr * ks / (rr + ks)
        right = jnp.where(lane == 127, 0.0, axial[at, :])
        left = pltpu.roll(right, 1, 1)
        second = collar_link[at, :]
        first = radial * hs
        diagonal = radial + second + left + right
        lower, upper = (-left, -right)
        for step in range(7):
            stride = 2**step
            inverse = 1.0 / diagonal
            low = -lower * pltpu.roll(inverse, stride, 1)
            high = -upper * pltpu.roll(inverse, 128 - stride, 1)
            first, second = (
                x + low * pltpu.roll(x, stride, 1) + high * pltpu.roll(x, 128 - stride, 1)
                for x in (first, second)
            )
            diagonal = diagonal + low * lower + high * upper
            if step < 6:
                lower = low * pltpu.roll(lower, stride, 1)
                upper = high * pltpu.roll(upper, 128 - stride, 1)
        inverse = 1.0 / diagonal
        free, collar = (first * inverse, second * inverse)

        def per_plant(x):
            return jnp.sum(jnp.sum(x.reshape(group // 8, 8, LANES), 1), 1, keepdims=True)

        mine = lax.broadcasted_iota(I32, (group // 8, LANES), 1) == plant_row + g * (group // 8)
        need = jnp.sum(jnp.where(mine, demand[...], 0.0), 1, keepdims=True)
        head = (per_plant(radial * (hs - free)) - need) / per_plant(radial * collar)
        spread = jnp.broadcast_to(head[:, None, :], (group // 8, 8, LANES)).reshape(group, LANES)
        uptake[at, :] = radial * (hs - (free + spread * collar))
        collar_line = collar_line + jnp.sum(jnp.where(mine, head, 0.0), 0, keepdims=True)
    collar_out[...] = collar_line[:, 0:PLANTS]
    slot_rows = lax.broadcasted_iota(I32, (80, LANES), 0).astype(F32).astype(BF16)
    slot_cols = columns
    total = jnp.zeros((160, LANES), F32)
    for start in range(0, BLOCKS, 8):
        values, spots = ([], [])
        for i in range(start, start + 8):
            where = code[i : i + 1, :]
            hi, lo = split(uptake[i : i + 1, :])
            mask = slot_rows == jnp.broadcast_to((where >> 7).astype(F32).astype(BF16), (80, LANES))
            values.append(
                jnp.concatenate(
                    [jnp.where(mask, jnp.broadcast_to(v, (80, LANES)), zero) for v in (hi, lo)], 0
                )
            )
            wanted = jnp.broadcast_to((where & 127).astype(F32).astype(BF16), (128, LANES))
            spots.append(jnp.where(slot_cols == wanted, one, zero))
        total = total + lax.dot_general(
            jnp.concatenate(values, 1),
            jnp.concatenate(spots, 1),
            (((1,), (1,)), ((), ())),
            preferred_element_type=F32,
        )
    summed[...] = total[0:72] + total[80:152]
    for n, place in enumerate(places):
        for dy, out in enumerate((out_minus, out_here, out_plus)):
            out[n * 8 : n * 8 + 8, :] = eight(summed, (place * 3 + dy) * 8)


def sink_of(pieces, row, col):
    low_rows = lax.broadcasted_iota(I32, (128, LANES), 0).astype(F32).astype(BF16)
    places_of = lax.broadcasted_iota(I32, (256, LANES), 0).astype(F32).astype(BF16)
    one, zero = (jnp.ones((), BF16), jnp.zeros((), BF16))
    total = jnp.zeros((256, 256), F32)
    for source, base, k in pieces:
        values, places = ([], [])
        rows8, cols8 = (eight(x, k * 8) for x in (row, col))
        for chunk in range(8):
            r, c = (rows8[chunk : chunk + 1], cols8[chunk : chunk + 1])
            hi, lo = split(source[base + chunk : base + chunk + 1, :])
            mask = low_rows == jnp.broadcast_to((r & 127).astype(F32).astype(BF16), (128, LANES))
            values.append(
                jnp.concatenate(
                    [jnp.where(mask, jnp.broadcast_to(v, (128, LANES)), zero) for v in (hi, lo)], 0
                )
            )
            wanted = ((r >> 7) * 128 + c).astype(F32).astype(BF16)
            places.append(jnp.where(places_of == jnp.broadcast_to(wanted, (256, LANES)), one, zero))
        total = total + lax.dot_general(
            jnp.concatenate(values, 1),
            jnp.concatenate(places, 1),
            (((1,), (1,)), ((), ())),
            preferred_element_type=F32,
        )
    return total[0:128] + total[128:256]


def new_head(cross, row, col, numerator, denominator, head_new):
    place = x_places()[1]
    sink = sink_of([(cross, dy * 8, place * 3 + dy) for dy in range(3)], row, col)
    for half in range(2):
        at = slice(half * 128, half * 128 + 128)
        head_new[at, :] = (numerator[at, :] - SINK_GAIN * sink[:, at]) / denominator[at, :]


def next_kernel(
    cross, row, col, numerator, denominator, sat, alpha_dry, wet,
    head, cond, chip_edge, cross_edge, edge_minus, edge_plus, weight,
):
    new_head(cross, row, col, numerator, denominator, head)
    for layer in range(LAYERS):
        at = slice(layer * 8, layer * 8 + 8)
        cond[at, :] = conduct(head[at, :], sat[at, :], alpha_dry[at, :] * (1.0 + wet[at, :].astype(F32)))
    lay_cells(head, cond, weight, chip_edge, cross_edge, edge_minus, edge_plus)


def last_kernel(cross, row, col, numerator, denominator, head):
    new_head(cross, row, col, numerator, denominator, head)


def call(kernel, outs, scratch=(), specs=None, micros=1):
    shapes = [jax.ShapeDtypeStruct(shape, dtype) for shape, dtype in outs]
    return pl.pallas_call(
        kernel,
        out_shape=shapes,
        scratch_shapes=[pltpu.VMEM(*x) if isinstance(x, tuple) else x for x in scratch],
        compiler_params=pltpu.CompilerParams(vmem_limit_bytes=VMEM_LIMIT),
        cost_estimate=pl.CostEstimate(
            flops=micros * 10**9, bytes_accessed=micros * 3 * 10**6, transcendentals=0
        ),
        **({} if specs is None else {"in_specs": specs}),
    )


MESSAGE = ((112, 128), F32)
EDGE = ((64, 128), F32)
SLOT = ((48, 128), F32)
SIDES = [((8, 128), F32)] * 2 + [((256, 512), BF16)]


def up(x, axis):
    size = lax.axis_size(axis)
    return lax.ppermute(x, axis, [(i, (i + 1) % size) for i in range(size)])


def down(x, axis):
    size = lax.axis_size(axis)
    return lax.ppermute(x, axis, [((i + 1) % size, i) for i in range(size)])


def swap(x, axis, first):
    size = lax.axis_size(axis)
    pairs = [((first + i) % size, (first + i + 1) % size) for i in range(0, size, 2)]
    return lax.ppermute(x, axis, [p for i, j in pairs for p in ((i, j), (j, i))])


def spread(row, col, chip_edge, cross, edge_minus, edge_plus, weight):
    from_cross = swap(cross, "gx", 1)
    chip_edges = swap(chip_edge, "gx", 0)
    chip, here = call(rest_kernel, [SLOT] * 2, micros=2)(row, col, weight, chip_edges)
    from_chip = swap(chip, "gx", 0)
    parts = (from_chip, here, from_cross)
    side_minus = up(jnp.concatenate([x[32:48] for x in parts] + [edge_plus], 0), "gy")
    side_plus = down(jnp.concatenate([x[0:16] for x in parts] + [edge_minus], 0), "gy")
    return (*parts, side_minus, side_plus), chip_edges


def give_back(minus, here, plus):
    back = (up(minus, "gy"), here, down(plus, "gy"))
    from_cross = swap(jnp.concatenate([x[16:24] for x in back], 0), "gx", 1)
    from_chip = swap(jnp.concatenate([x[0:8] for x in back], 0), "gx", 0)
    return (back, (from_chip, from_cross))


def on_device(
    head_start,
    sat_conduct,
    alpha_dry,
    wet_flag,
    reversal_head,
    send_row,
    send_col,
    root_radial,
    root_axial,
    stem_link,
    entry_seg,
    source_dev,
    source_slot,
    demand,
):
    tile = head_start.shape
    head, sat, alpha, wet, reversal = (
        x.reshape(CELLS, LANES) for x in (head_start, sat_conduct, alpha_dry, wet_flag, reversal_head)
    )
    rows_gx = lax.axis_size("gx")
    cols_gy = lax.axis_size("gy")
    offset_k = (lax.axis_index("gx") - source_dev // cols_gy + 1) % rows_gx * 3 + (
        lax.axis_index("gy") - source_dev % cols_gy + 1
    ) % cols_gy
    code = offset_k * send_row.shape[2] + source_slot
    row, col = (x.reshape(SLOTS, LANES) for x in (send_row, send_col))
    head_old = head
    cond = conduct(head, sat, alpha * (1.0 + wet.astype(F32)))
    messages = call(start_kernel, [EDGE, MESSAGE] + SIDES, micros=2)(head, cond, row, col)
    collar_link, need = call(collar_kernel, [((BLOCKS, LANES), F32), ((1, LANES), F32)])(
        stem_link.reshape(1, BLOCKS), entry_seg.reshape(1, BLOCKS), demand.reshape(1, PLANTS)
    )
    for iteration in range(PICARD):
        got, chip_edges = spread(row, col, *messages)
        *sums, collar = call(
            root_kernel,
            [((24, 128), F32)] * 3 + [((1, PLANTS), F32)],
            [((144, 256), BF16), ((144, 128), F32)] + [((128, 128), F32)] * 3 + [((72, 128), F32)],
            micros=6,
        )(*got, code, root_radial, root_axial, collar_link, need)
        near, (from_chip, from_cross) = give_back(*sums)
        numerator, denominator = call(
            terms_kernel,
            [((CELLS, LANES), F32)] * 2,
            [((128, 128), F32)],
        )(
            head, cond, head_old, alpha, wet, reversal, chip_edges, got[2], got[3], got[4],
            *near, from_chip, row, col,
        )
        if iteration < PICARD - 1:
            head, cond, chip_edge, cross_edge, *sides, weight = call(
                next_kernel, [((CELLS, LANES), F32)] * 2 + [EDGE] * 2 + SIDES, micros=2
            )(from_cross, row, col, numerator, denominator, sat, alpha, wet)
            (cross,) = call(cross_kernel, [MESSAGE])(row, col, weight, cross_edge)
            messages = (chip_edge, cross, *sides, weight)
        else:
            (head,) = call(last_kernel, [((CELLS, LANES), F32)])(
                from_cross, row, col, numerator, denominator
            )
    return (head.reshape(tile), collar.reshape(-1))


def solution(mesh):
    tile, lists, blocks, line = (
        P(None, "gx", "gy"),
        P(("gx", "gy"), None, None),
        P(("gx", "gy"), None),
        P(("gx", "gy")),
    )
    return jax.shard_map(
        on_device,
        mesh=mesh,
        in_specs=(tile,) * 5 + (lists,) * 2 + (blocks,) * 2 + (line,) * 2 + (blocks,) * 2 + (line,),
        out_specs=(tile, line),
        check_vma=False,
    )
```

```python
import jax
import jax.numpy as jnp
from jax import lax
from jax.experimental import pallas as pl
from jax.experimental.pallas import tpu as pltpu
from jax.sharding import PartitionSpec as P

PICARD = 2
PORE_INDEX = 1.6
PORE_POWER = 0.375
SPAN_THETA = 0.35
STORAGE = 0.01
SINK_GAIN = 4.0

F32, BF16, I32 = (jnp.float32, jnp.bfloat16, jnp.int32)
VMEM_LIMIT = 48 * 2**20
LAYERS, CELLS, LANES, SLOTS, BLOCKS, PLANTS = (32, 256, 128, 72, 128, 16)


def split(x):
    hi = x.astype(BF16)
    return (hi, (x - hi.astype(F32)).astype(BF16))


def conduct(head, sat_conduct, alpha):
    power = jnp.exp(PORE_INDEX * jnp.log(alpha * jnp.abs(head)))
    root = jnp.exp((-0.5 * PORE_POWER) * jnp.log(1.0 + power))
    inner = 1.0 - jnp.exp(-PORE_POWER * jnp.log(1.0 + 1.0 / power))
    return sat_conduct * root * inner * inner


def capacity(head, alpha_dry, wetting, reversal_head):
    alpha = alpha_dry * (1.0 + wetting)
    log_scaled = jnp.log(alpha * jnp.abs(head))
    log_term = jnp.log(1.0 + jnp.exp(PORE_INDEX * log_scaled))
    slope = (
        (PORE_POWER * PORE_INDEX)
        * alpha
        * jnp.exp((PORE_INDEX - 1.0) * log_scaled + (-PORE_POWER - 1.0) * log_term)
    )
    turned = jnp.exp(PORE_INDEX * jnp.log(alpha_dry * jnp.abs(reversal_head)))
    ratio = jnp.exp(PORE_POWER * (jnp.log(1.0 + 2.0**PORE_INDEX * turned) - jnp.log(1.0 + turned)))
    factor = wetting * ratio + (1.0 - wetting)
    return SPAN_THETA * factor * slope + STORAGE


def x_places():
    odd = lax.rem(lax.axis_index("gx"), 2)
    return (2 - 2 * odd, 2 * odd)


def lay_cells(head, cond, weight, chip_edge, cross, edge_minus, edge_plus):
    even = x_places()[0] == 2
    for field, ref in enumerate((head, cond)):
        for half in range(2):
            turned = ref[half * 128 : half * 128 + 128, :].T
            edge_minus[field * 2 + half : field * 2 + half + 1, :] = turned[0:1]
            edge_plus[field * 2 + half : field * 2 + half + 1, :] = turned[127:128]
            hi, lo = split(turned)
            weight[field * 128 : field * 128 + 128, half * 128 : half * 128 + 128] = hi
            weight[field * 128 : field * 128 + 128, 256 + half * 128 : 384 + half * 128] = lo
        first = ref[pl.ds(0, LAYERS, stride=8), :]
        last = ref[pl.ds(7, LAYERS, stride=8), :]
        chip_edge[32 * field : 32 * field + 32, :] = jnp.where(even, last, first)
        at = cross.shape[0] - 64 + 32 * field
        cross[at : at + 32, :] = jnp.where(even, first, last)
    edge_minus[4:8, :] = jnp.zeros((4, LANES), F32)
    edge_plus[4:8, :] = jnp.zeros((4, LANES), F32)


def eight(ref, at):
    return ref[pl.ds(pl.multiple_of(at, 8), 8), :]


def gather_cells(row, col, weight, outs):
    cells = lax.broadcasted_iota(I32, (CELLS, LANES), 0).astype(F32).astype(BF16)
    columns = lax.broadcasted_iota(I32, (LANES, LANES), 0)
    one, zero = (jnp.ones((), BF16), jnp.zeros((), BF16))
    for out, place in outs:
        for dy in range(3):
            rows8, cols8 = (eight(x, (place * 3 + dy) * 8) for x in (row, col))
            for chunk in range(0, 8, 2):
                picks = []
                for i in (chunk, chunk + 1):
                    wanted = rows8[i : i + 1].astype(F32).astype(BF16)
                    wanted = jnp.broadcast_to(wanted, (CELLS, LANES))
                    picks.append(jnp.where(cells == wanted, one, zero))
                pick = jnp.concatenate(picks, 1)
                got = lax.dot_general(
                    weight[...],
                    jnp.concatenate([pick, pick], 0),
                    (((1,), (0,)), ((), ())),
                    preferred_element_type=F32,
                )
                for n, i in enumerate((chunk, chunk + 1)):
                    mask = columns == cols8[i : i + 1]
                    for field in range(2):
                        part = got[field * 128 : field * 128 + 128, n * 128 : n * 128 + 128]
                        at = dy * 16 + field * 8 + i
                        out[at : at + 1, :] = jnp.sum(jnp.where(mask, part, 0.0), 0, keepdims=True)


def leads():
    return lax.axis_index("gx") == 0


def start_kernel(
    head, cond, row, col, chip_edge, cross, edge_minus, edge_plus, weight, chip, here
):
    lay_cells(head, cond, weight, chip_edge, cross, edge_minus, edge_plus)
    gather_cells(row, col, weight, ((cross, x_places()[1]),))

    @pl.when(leads())
    def _():
        gather_cells(row, col, weight, ((chip, x_places()[0]), (here, 1)))


def first_rest_kernel(row, col, weight, _, chip_in, here_in, chip, here):
    @pl.when(leads())
    def _():
        chip[...] = chip_in[...]
        here[...] = here_in[...]

    @pl.when(jnp.logical_not(leads()))
    def _():
        gather_cells(row, col, weight, ((chip, x_places()[0]), (here, 1)))


def cross_kernel(row, col, weight, cross_edge, cross):
    gather_cells(row, col, weight, ((cross, x_places()[1]),))
    cross[48:112, :] = cross_edge[...]


def rest_kernel(row, col, weight, _, chip, here):
    gather_cells(row, col, weight, ((chip, x_places()[0]), (here, 1)))


def collar_kernel(stem, entry, demand, second, need):
    sub = lax.broadcasted_iota(I32, (BLOCKS, LANES), 0)
    lane = lax.broadcasted_iota(I32, (BLOCKS, LANES), 1)
    own = sub == lane
    stem_col = jnp.sum(jnp.where(own, stem[...], 0.0), 1, keepdims=True)
    entry_col = jnp.sum(jnp.where(own, entry[...].astype(F32), 0.0), 1, keepdims=True)
    second[...] = jnp.where(lane.astype(F32) == entry_col, stem_col, 0.0)
    need[...] = jnp.zeros((1, LANES), F32)
    need[:, 0:PLANTS] = demand[...]


def terms_kernel(
    head, cond, head_old, alpha_dry, wet, reversal, chip_edges, cross, side_minus, side_plus,
    back_minus, back_here, back_plus, back_chip, row, col,
    numerator, denominator, halo,
):
    pieces = [(x, 8, 3 + dy) for dy, x in enumerate((back_minus, back_here, back_plus))]
    pieces += [(back_chip, dy * 8, x_places()[0] * 3 + dy) for dy in range(3)]
    sink = SINK_GAIN * sink_of(pieces, row, col)
    even = x_places()[0] == 2
    from_plus = jnp.where(even, chip_edges[...], cross[48:112, :])
    from_minus = jnp.where(even, cross[48:112, :], chip_edges[...])
    halo[...] = jnp.zeros_like(halo)
    turned = []
    for i in range(4):
        halo[0:1, :] = side_minus[48 + i : 49 + i, :]
        halo[127:128, :] = side_plus[48 + i : 49 + i, :]
        turned.append(halo[...].T)
    sub = lax.broadcasted_iota(I32, (8, LANES), 0)
    lane = lax.broadcasted_iota(I32, (8, LANES), 1)
    for layer in range(LAYERS):
        at = slice(layer * 8, layer * 8 + 8)
        h, c = (head[at, :], cond[at, :])
        cap = capacity(h, alpha_dry[at, :], wet[at, :].astype(F32), reversal[at, :])
        num, den = (cap * head_old[at, :], cap)
        local = slice(layer % 16 * 8, layer % 16 * 8 + 8)
        halo_h, halo_c = (turned[layer // 16][local], turned[2 + layer // 16][local])

        def add(num, den, near_h, near_c):
            face = 0.5 * (c + near_c)
            return (num + face * near_h, den + face)

        def beside(x, line, spot):
            return jnp.where(sub == spot, jnp.broadcast_to(line, (8, LANES)), x)

        num, den = add(
            num, den,
            beside(pltpu.roll(h, 7, 0), from_plus[layer : layer + 1], 7),
            beside(pltpu.roll(c, 7, 0), from_plus[32 + layer : 33 + layer], 7),
        )
        num, den = add(
            num, den,
            beside(pltpu.roll(h, 1, 0), from_minus[layer : layer + 1], 0),
            beside(pltpu.roll(c, 1, 0), from_minus[32 + layer : 33 + layer], 0),
        )
        num, den = add(
            num, den,
            jnp.where(lane == 127, halo_h, pltpu.roll(h, 127, 1)),
            jnp.where(lane == 127, halo_c, pltpu.roll(c, 127, 1)),
        )
        num, den = add(
            num, den,
            jnp.where(lane == 0, halo_h, pltpu.roll(h, 1, 1)),
            jnp.where(lane == 0, halo_c, pltpu.roll(c, 1, 1)),
        )
        if layer > 0:
            above = slice(layer * 8 - 8, layer * 8)
            num, den = add(num, den, head[above, :] + 1.0, cond[above, :])
        if layer < LAYERS - 1:
            below = slice(layer * 8 + 8, layer * 8 + 16)
            num, den = add(num, den, head[below, :] - 1.0, cond[below, :])
        else:
            num = num - c
        half = layer // 16
        numerator[at, :] = num - sink[local, half * 128 : half * 128 + 128]
        denominator[at, :] = den


def root_kernel(
    chip, here, cross, side_minus, side_plus, code, radial_in, axial, collar_link, demand,
    out_minus, out_here, out_plus, collar_out, weight, table, seg_head, seg_cond, uptake, summed,
):
    cross_place, chip_place = x_places()
    places = (chip_place, 1, cross_place)
    for n, place in enumerate(places):
        for dy in range(3):
            if dy == 1:
                source, at = ((chip, here, cross)[n], 16)
            else:
                source, at = ((side_plus, None, side_minus)[dy], n * 16)
            for field in range(2):
                to = pl.multiple_of(field * 72 + (place * 3 + dy) * 8, 8)
                table[pl.ds(to, 8), :] = source[at + field * 8 : at + field * 8 + 8, :]
    weight[:, 0:128], weight[:, 128:256] = split(table[...])
    columns = lax.broadcasted_iota(I32, (128, LANES), 0).astype(F32).astype(BF16)
    rows = lax.broadcasted_iota(I32, (SLOTS, LANES), 0)
    one, zero = (jnp.ones((), BF16), jnp.zeros((), BF16))
    for j in range(0, BLOCKS, 8):
        picks = []
        for i in range(j, j + 8):
            wanted = jnp.broadcast_to((code[i : i + 1, :] & 127).astype(F32).astype(BF16), (128, LANES))
            picks.append(jnp.where(columns == wanted, one, zero))
        pick = jnp.concatenate(picks, 1)
        got = lax.dot_general(
            weight[...],
            jnp.concatenate([pick, pick], 0),
            (((1,), (0,)), ((), ())),
            preferred_element_type=F32,
        )
        for n, i in enumerate(range(j, j + 8)):
            mask = rows == (code[i : i + 1, :] >> 7)
            for field, ref in enumerate((seg_head, seg_cond)):
                part = got[field * 72 : field * 72 + 72, n * 128 : n * 128 + 128]
                ref[i : i + 1, :] = jnp.sum(jnp.where(mask, part, 0.0), 0, keepdims=True)
    group = 32
    lane = lax.broadcasted_iota(I32, (group, LANES), 1)
    plant_row = lax.broadcasted_iota(I32, (group // 8, 1), 0)
    collar_line = jnp.zeros((1, LANES), F32)
    for g in range(BLOCKS // group):
        at = slice(g * group, g * group + group)
        hs, ks, rr = (seg_head[at, :], seg_cond[at, :], radial_in[at, :])
        radial = rr * ks / (rr + ks)
        right = jnp.where(lane == 127, 0.0, axial[at, :])
        left = pltpu.roll(right, 1, 1)
        second = collar_link[at, :]
        first = radial * hs
        diagonal = radial + second + left + right
        lower, upper = (-left, -right)
        for step in range(7):
            stride = 2**step
            inverse = 1.0 / diagonal
            low = -lower * pltpu.roll(inverse, stride, 1)
            high = -upper * pltpu.roll(inverse, 128 - stride, 1)
            first, second = (
                x + low * pltpu.roll(x, stride, 1) + high * pltpu.roll(x, 128 - stride, 1)
                for x in (first, second)
            )
            diagonal = diagonal + low * lower + high * upper
            if step < 6:
                lower = low * pltpu.roll(lower, stride, 1)
                upper = high * pltpu.roll(upper, 128 - stride, 1)
        inverse = 1.0 / diagonal
        free, collar = (first * inverse, second * inverse)

        def per_plant(x):
            return jnp.sum(jnp.sum(x.reshape(group // 8, 8, LANES), 1), 1, keepdims=True)

        mine = lax.broadcasted_iota(I32, (group // 8, LANES), 1) == plant_row + g * (group // 8)
        need = jnp.sum(jnp.where(mine, demand[...], 0.0), 1, keepdims=True)
        head = (per_plant(radial * (hs - free)) - need) / per_plant(radial * collar)
        spread = jnp.broadcast_to(head[:, None, :], (group // 8, 8, LANES)).reshape(group, LANES)
        uptake[at, :] = radial * (hs - (free + spread * collar))
        collar_line = collar_line + jnp.sum(jnp.where(mine, head, 0.0), 0, keepdims=True)
    collar_out[...] = collar_line[:, 0:PLANTS]
    slot_rows = lax.broadcasted_iota(I32, (80, LANES), 0).astype(F32).astype(BF16)
    slot_cols = columns
    total = jnp.zeros((160, LANES), F32)
    for start in range(0, BLOCKS, 8):
        values, spots = ([], [])
        for i in range(start, start + 8):
            where = code[i : i + 1, :]
            hi, lo = split(uptake[i : i + 1, :])
            mask = slot_rows == jnp.broadcast_to((where >> 7).astype(F32).astype(BF16), (80, LANES))
            values.append(
                jnp.concatenate(
                    [jnp.where(mask, jnp.broadcast_to(v, (80, LANES)), zero) for v in (hi, lo)], 0
                )
            )
            wanted = jnp.broadcast_to((where & 127).astype(F32).astype(BF16), (128, LANES))
            spots.append(jnp.where(slot_cols == wanted, one, zero))
        total = total + lax.dot_general(
            jnp.concatenate(values, 1),
            jnp.concatenate(spots, 1),
            (((1,), (1,)), ((), ())),
            preferred_element_type=F32,
        )
    summed[...] = total[0:72] + total[80:152]
    for n, place in enumerate(places):
        for dy, out in enumerate((out_minus, out_here, out_plus)):
            out[n * 8 : n * 8 + 8, :] = eight(summed, (place * 3 + dy) * 8)


def sink_of(pieces, row, col):
    low_rows = lax.broadcasted_iota(I32, (128, LANES), 0).astype(F32).astype(BF16)
    places_of = lax.broadcasted_iota(I32, (256, LANES), 0).astype(F32).astype(BF16)
    one, zero = (jnp.ones((), BF16), jnp.zeros((), BF16))
    total = jnp.zeros((256, 256), F32)
    for source, base, k in pieces:
        values, places = ([], [])
        rows8, cols8 = (eight(x, k * 8) for x in (row, col))
        for chunk in range(8):
            r, c = (rows8[chunk : chunk + 1], cols8[chunk : chunk + 1])
            hi, lo = split(source[base + chunk : base + chunk + 1, :])
            mask = low_rows == jnp.broadcast_to((r & 127).astype(F32).astype(BF16), (128, LANES))
            values.append(
                jnp.concatenate(
                    [jnp.where(mask, jnp.broadcast_to(v, (128, LANES)), zero) for v in (hi, lo)], 0
                )
            )
            wanted = ((r >> 7) * 128 + c).astype(F32).astype(BF16)
            places.append(jnp.where(places_of == jnp.broadcast_to(wanted, (256, LANES)), one, zero))
        total = total + lax.dot_general(
            jnp.concatenate(values, 1),
            jnp.concatenate(places, 1),
            (((1,), (1,)), ((), ())),
            preferred_element_type=F32,
        )
    return total[0:128] + total[128:256]


def new_head(cross, row, col, numerator, denominator, head_new):
    place = x_places()[1]
    sink = sink_of([(cross, dy * 8, place * 3 + dy) for dy in range(3)], row, col)
    for half in range(2):
        at = slice(half * 128, half * 128 + 128)
        head_new[at, :] = (numerator[at, :] - SINK_GAIN * sink[:, at]) / denominator[at, :]


def next_kernel(
    cross, row, col, numerator, denominator, sat, alpha_dry, wet,
    head, cond, chip_edge, cross_edge, edge_minus, edge_plus, weight,
):
    new_head(cross, row, col, numerator, denominator, head)
    for layer in range(LAYERS):
        at = slice(layer * 8, layer * 8 + 8)
        cond[at, :] = conduct(head[at, :], sat[at, :], alpha_dry[at, :] * (1.0 + wet[at, :].astype(F32)))
    lay_cells(head, cond, weight, chip_edge, cross_edge, edge_minus, edge_plus)


def last_kernel(cross, row, col, numerator, denominator, head):
    new_head(cross, row, col, numerator, denominator, head)


def call(kernel, outs, scratch=(), specs=None, micros=1):
    shapes = [jax.ShapeDtypeStruct(shape, dtype) for shape, dtype in outs]
    return pl.pallas_call(
        kernel,
        out_shape=shapes,
        scratch_shapes=[pltpu.VMEM(*x) if isinstance(x, tuple) else x for x in scratch],
        compiler_params=pltpu.CompilerParams(vmem_limit_bytes=VMEM_LIMIT),
        cost_estimate=pl.CostEstimate(
            flops=micros * 10**9, bytes_accessed=micros * 3 * 10**6, transcendentals=0
        ),
        **({} if specs is None else {"in_specs": specs}),
    )


MESSAGE = ((112, 128), F32)
EDGE = ((64, 128), F32)
SLOT = ((48, 128), F32)
SIDES = [((8, 128), F32)] * 2 + [((256, 512), BF16)]


def up(x, axis):
    size = lax.axis_size(axis)
    return lax.ppermute(x, axis, [(i, (i + 1) % size) for i in range(size)])


def down(x, axis):
    size = lax.axis_size(axis)
    return lax.ppermute(x, axis, [((i + 1) % size, i) for i in range(size)])


def swap(x, axis, first):
    size = lax.axis_size(axis)
    pairs = [((first + i) % size, (first + i + 1) % size) for i in range(0, size, 2)]
    return lax.ppermute(x, axis, [p for i, j in pairs for p in ((i, j), (j, i))])


def spread(row, col, chip_edge, cross, edge_minus, edge_plus, weight, *early):
    from_cross = swap(cross, "gx", 1)
    chip_edges = swap(chip_edge, "gx", 0)
    chip, here = call(first_rest_kernel if early else rest_kernel, [SLOT] * 2, micros=2)(
        row, col, weight, chip_edges, *early
    )
    from_chip = swap(chip, "gx", 0)
    parts = (from_chip, here, from_cross)
    side_minus = up(jnp.concatenate([x[32:48] for x in parts] + [edge_plus], 0), "gy")
    side_plus = down(jnp.concatenate([x[0:16] for x in parts] + [edge_minus], 0), "gy")
    return (*parts, side_minus, side_plus), chip_edges


def give_back(minus, here, plus):
    back = (up(minus, "gy"), here, down(plus, "gy"))
    from_cross = swap(jnp.concatenate([x[16:24] for x in back], 0), "gx", 1)
    from_chip = swap(jnp.concatenate([x[0:8] for x in back], 0), "gx", 0)
    return (back, (from_chip, from_cross))


def on_device(
    head_start,
    sat_conduct,
    alpha_dry,
    wet_flag,
    reversal_head,
    send_row,
    send_col,
    root_radial,
    root_axial,
    stem_link,
    entry_seg,
    source_dev,
    source_slot,
    demand,
):
    tile = head_start.shape
    head, sat, alpha, wet, reversal = (
        x.reshape(CELLS, LANES) for x in (head_start, sat_conduct, alpha_dry, wet_flag, reversal_head)
    )
    rows_gx = lax.axis_size("gx")
    cols_gy = lax.axis_size("gy")
    offset_k = (lax.axis_index("gx") - source_dev // cols_gy + 1) % rows_gx * 3 + (
        lax.axis_index("gy") - source_dev % cols_gy + 1
    ) % cols_gy
    code = offset_k * send_row.shape[2] + source_slot
    row, col = (x.reshape(SLOTS, LANES) for x in (send_row, send_col))
    head_old = head
    cond = conduct(head, sat, alpha * (1.0 + wet.astype(F32)))
    messages = call(start_kernel, [EDGE, MESSAGE] + SIDES + [SLOT] * 2, micros=2)(head, cond, row, col)
    collar_link, need = call(collar_kernel, [((BLOCKS, LANES), F32), ((1, LANES), F32)])(
        stem_link.reshape(1, BLOCKS), entry_seg.reshape(1, BLOCKS), demand.reshape(1, PLANTS)
    )
    for iteration in range(PICARD):
        got, chip_edges = spread(row, col, *messages)
        *sums, collar = call(
            root_kernel,
            [((24, 128), F32)] * 3 + [((1, PLANTS), F32)],
            [((144, 256), BF16), ((144, 128), F32)] + [((128, 128), F32)] * 3 + [((72, 128), F32)],
            micros=6,
        )(*got, code, root_radial, root_axial, collar_link, need)
        near, (from_chip, from_cross) = give_back(*sums)
        numerator, denominator = call(
            terms_kernel,
            [((CELLS, LANES), F32)] * 2,
            [((128, 128), F32)],
        )(
            head, cond, head_old, alpha, wet, reversal, chip_edges, got[2], got[3], got[4],
            *near, from_chip, row, col,
        )
        if iteration < PICARD - 1:
            head, cond, chip_edge, cross_edge, *sides, weight = call(
                next_kernel, [((CELLS, LANES), F32)] * 2 + [EDGE] * 2 + SIDES, micros=2
            )(from_cross, row, col, numerator, denominator, sat, alpha, wet)
            (cross,) = call(cross_kernel, [MESSAGE])(row, col, weight, cross_edge)
            messages = (chip_edge, cross, *sides, weight)
        else:
            (head,) = call(last_kernel, [((CELLS, LANES), F32)])(
                from_cross, row, col, numerator, denominator
            )
    return (head.reshape(tile), collar.reshape(-1))


def solution(mesh):
    tile, lists, blocks, line = (
        P(None, "gx", "gy"),
        P(("gx", "gy"), None, None),
        P(("gx", "gy"), None),
        P(("gx", "gy")),
    )
    return jax.shard_map(
        on_device,
        mesh=mesh,
        in_specs=(tile,) * 5 + (lists,) * 2 + (blocks,) * 2 + (line,) * 2 + (blocks,) * 2 + (line,),
        out_specs=(tile, line),
        check_vma=False,
    )
```

```python
import jax
import jax.numpy as jnp
from jax import lax
from jax.experimental import pallas as pl
from jax.experimental.pallas import tpu as pltpu
from jax.sharding import PartitionSpec as P

PICARD = 2
PORE_INDEX = 1.6
PORE_POWER = 0.375
SPAN_THETA = 0.35
STORAGE = 0.01
SINK_GAIN = 4.0

F32, BF16, I32 = (jnp.float32, jnp.bfloat16, jnp.int32)
VMEM_LIMIT = 48 * 2**20
LAYERS, CELLS, LANES, SLOTS, BLOCKS, PLANTS = (32, 256, 128, 72, 128, 16)


def split(x):
    hi = x.astype(BF16)
    return (hi, (x - hi.astype(F32)).astype(BF16))


def conduct(head, sat_conduct, alpha):
    power = jnp.exp(PORE_INDEX * jnp.log(alpha * jnp.abs(head)))
    root = jnp.exp((-0.5 * PORE_POWER) * jnp.log(1.0 + power))
    inner = 1.0 - jnp.exp(-PORE_POWER * jnp.log(1.0 + 1.0 / power))
    return sat_conduct * root * inner * inner


def capacity(head, alpha_dry, wetting, reversal_head):
    alpha = alpha_dry * (1.0 + wetting)
    log_scaled = jnp.log(alpha * jnp.abs(head))
    log_term = jnp.log(1.0 + jnp.exp(PORE_INDEX * log_scaled))
    slope = (
        (PORE_POWER * PORE_INDEX)
        * alpha
        * jnp.exp((PORE_INDEX - 1.0) * log_scaled + (-PORE_POWER - 1.0) * log_term)
    )
    turned = jnp.exp(PORE_INDEX * jnp.log(alpha_dry * jnp.abs(reversal_head)))
    ratio = jnp.exp(PORE_POWER * (jnp.log(1.0 + 2.0**PORE_INDEX * turned) - jnp.log(1.0 + turned)))
    factor = wetting * ratio + (1.0 - wetting)
    return SPAN_THETA * factor * slope + STORAGE


def x_places():
    odd = lax.rem(lax.axis_index("gx"), 2)
    return (2 - 2 * odd, 2 * odd)


def lay_cells(head, cond, weight, chip_edge, cross, edge_minus, edge_plus):
    even = x_places()[0] == 2
    for field, ref in enumerate((head, cond)):
        for half in range(2):
            turned = ref[half * 128 : half * 128 + 128, :].T
            edge_minus[field * 2 + half : field * 2 + half + 1, :] = turned[0:1]
            edge_plus[field * 2 + half : field * 2 + half + 1, :] = turned[127:128]
            hi, lo = split(turned)
            weight[field * 128 : field * 128 + 128, half * 128 : half * 128 + 128] = hi
            weight[field * 128 : field * 128 + 128, 256 + half * 128 : 384 + half * 128] = lo
        first = ref[pl.ds(0, LAYERS, stride=8), :]
        last = ref[pl.ds(7, LAYERS, stride=8), :]
        chip_edge[32 * field : 32 * field + 32, :] = jnp.where(even, last, first)
        at = cross.shape[0] - 64 + 32 * field
        cross[at : at + 32, :] = jnp.where(even, first, last)
    edge_minus[4:8, :] = jnp.zeros((4, LANES), F32)
    edge_plus[4:8, :] = jnp.zeros((4, LANES), F32)


def eight(ref, at):
    return ref[pl.ds(pl.multiple_of(at, 8), 8), :]


def gather_cells(row, col, weight, outs):
    cells = lax.broadcasted_iota(I32, (CELLS, LANES), 0).astype(F32).astype(BF16)
    columns = lax.broadcasted_iota(I32, (LANES, LANES), 0)
    one, zero = (jnp.ones((), BF16), jnp.zeros((), BF16))
    for out, place in outs:
        for dy in range(3):
            rows8, cols8 = (eight(x, (place * 3 + dy) * 8) for x in (row, col))
            for chunk in range(0, 8, 2):
                picks = []
                for i in (chunk, chunk + 1):
                    wanted = rows8[i : i + 1].astype(F32).astype(BF16)
                    wanted = jnp.broadcast_to(wanted, (CELLS, LANES))
                    picks.append(jnp.where(cells == wanted, one, zero))
                pick = jnp.concatenate(picks, 1)
                got = lax.dot_general(
                    weight[...],
                    jnp.concatenate([pick, pick], 0),
                    (((1,), (0,)), ((), ())),
                    preferred_element_type=F32,
                )
                for n, i in enumerate((chunk, chunk + 1)):
                    mask = columns == cols8[i : i + 1]
                    for field in range(2):
                        part = got[field * 128 : field * 128 + 128, n * 128 : n * 128 + 128]
                        at = dy * 16 + field * 8 + i
                        out[at : at + 1, :] = jnp.sum(jnp.where(mask, part, 0.0), 0, keepdims=True)


def start_kernel(head, cond, row, col, chip_edge, cross, edge_minus, edge_plus, weight):
    lay_cells(head, cond, weight, chip_edge, cross, edge_minus, edge_plus)
    gather_cells(row, col, weight, ((cross, x_places()[1]),))


def cross_kernel(row, col, weight, cross_edge, cross):
    gather_cells(row, col, weight, ((cross, x_places()[1]),))
    cross[48:112, :] = cross_edge[...]


def rest_kernel(row, col, weight, chip_edge, _, chip, here):
    gather_cells(row, col, weight, ((chip, x_places()[0]), (here, 1)))
    chip[48:112, :] = chip_edge[...]


def collar_kernel(stem, entry, demand, second, need):
    sub = lax.broadcasted_iota(I32, (BLOCKS, LANES), 0)
    lane = lax.broadcasted_iota(I32, (BLOCKS, LANES), 1)
    own = sub == lane
    stem_col = jnp.sum(jnp.where(own, stem[...], 0.0), 1, keepdims=True)
    entry_col = jnp.sum(jnp.where(own, entry[...].astype(F32), 0.0), 1, keepdims=True)
    second[...] = jnp.where(lane.astype(F32) == entry_col, stem_col, 0.0)
    need[...] = jnp.zeros((1, LANES), F32)
    need[:, 0:PLANTS] = demand[...]


def terms_kernel(
    head, cond, head_old, alpha_dry, wet, reversal, chip, cross, side_minus, side_plus,
    back_minus, back_here, back_plus, back_chip, row, col,
    numerator, denominator, halo,
):
    pieces = [(x, 8, 3 + dy) for dy, x in enumerate((back_minus, back_here, back_plus))]
    pieces += [(back_chip, dy * 8, x_places()[0] * 3 + dy) for dy in range(3)]
    sink = SINK_GAIN * sink_of(pieces, row, col)
    even = x_places()[0] == 2
    from_plus = jnp.where(even, chip[48:112, :], cross[48:112, :])
    from_minus = jnp.where(even, cross[48:112, :], chip[48:112, :])
    halo[...] = jnp.zeros_like(halo)
    turned = []
    for i in range(4):
        halo[0:1, :] = side_minus[48 + i : 49 + i, :]
        halo[127:128, :] = side_plus[48 + i : 49 + i, :]
        turned.append(halo[...].T)
    sub = lax.broadcasted_iota(I32, (8, LANES), 0)
    lane = lax.broadcasted_iota(I32, (8, LANES), 1)
    for layer in range(LAYERS):
        at = slice(layer * 8, layer * 8 + 8)
        h, c = (head[at, :], cond[at, :])
        cap = capacity(h, alpha_dry[at, :], wet[at, :].astype(F32), reversal[at, :])
        num, den = (cap * head_old[at, :], cap)
        local = slice(layer % 16 * 8, layer % 16 * 8 + 8)
        halo_h, halo_c = (turned[layer // 16][local], turned[2 + layer // 16][local])

        def add(num, den, near_h, near_c):
            face = 0.5 * (c + near_c)
            return (num + face * near_h, den + face)

        def beside(x, line, spot):
            return jnp.where(sub == spot, jnp.broadcast_to(line, (8, LANES)), x)

        num, den = add(
            num, den,
            beside(pltpu.roll(h, 7, 0), from_plus[layer : layer + 1], 7),
            beside(pltpu.roll(c, 7, 0), from_plus[32 + layer : 33 + layer], 7),
        )
        num, den = add(
            num, den,
            beside(pltpu.roll(h, 1, 0), from_minus[layer : layer + 1], 0),
            beside(pltpu.roll(c, 1, 0), from_minus[32 + layer : 33 + layer], 0),
        )
        num, den = add(
            num, den,
            jnp.where(lane == 127, halo_h, pltpu.roll(h, 127, 1)),
            jnp.where(lane == 127, halo_c, pltpu.roll(c, 127, 1)),
        )
        num, den = add(
            num, den,
            jnp.where(lane == 0, halo_h, pltpu.roll(h, 1, 1)),
            jnp.where(lane == 0, halo_c, pltpu.roll(c, 1, 1)),
        )
        if layer > 0:
            above = slice(layer * 8 - 8, layer * 8)
            num, den = add(num, den, head[above, :] + 1.0, cond[above, :])
        if layer < LAYERS - 1:
            below = slice(layer * 8 + 8, layer * 8 + 16)
            num, den = add(num, den, head[below, :] - 1.0, cond[below, :])
        else:
            num = num - c
        half = layer // 16
        numerator[at, :] = num - sink[local, half * 128 : half * 128 + 128]
        denominator[at, :] = den


def root_kernel(
    chip, here, cross, side_minus, side_plus, code, radial_in, axial, collar_link, demand,
    out_minus, out_here, out_plus, collar_out, weight, table, seg_head, seg_cond, uptake, summed,
):
    cross_place, chip_place = x_places()
    places = (chip_place, 1, cross_place)
    for n, place in enumerate(places):
        for dy in range(3):
            if dy == 1:
                source, at = ((chip, here, cross)[n], 16)
            else:
                source, at = ((side_plus, None, side_minus)[dy], n * 16)
            for field in range(2):
                to = pl.multiple_of(field * 72 + (place * 3 + dy) * 8, 8)
                table[pl.ds(to, 8), :] = source[at + field * 8 : at + field * 8 + 8, :]
    weight[:, 0:128], weight[:, 128:256] = split(table[...])
    columns = lax.broadcasted_iota(I32, (128, LANES), 0).astype(F32).astype(BF16)
    rows = lax.broadcasted_iota(I32, (SLOTS, LANES), 0)
    one, zero = (jnp.ones((), BF16), jnp.zeros((), BF16))
    for j in range(0, BLOCKS, 8):
        picks = []
        for i in range(j, j + 8):
            wanted = jnp.broadcast_to((code[i : i + 1, :] & 127).astype(F32).astype(BF16), (128, LANES))
            picks.append(jnp.where(columns == wanted, one, zero))
        pick = jnp.concatenate(picks, 1)
        got = lax.dot_general(
            weight[...],
            jnp.concatenate([pick, pick], 0),
            (((1,), (0,)), ((), ())),
            preferred_element_type=F32,
        )
        for n, i in enumerate(range(j, j + 8)):
            mask = rows == (code[i : i + 1, :] >> 7)
            for field, ref in enumerate((seg_head, seg_cond)):
                part = got[field * 72 : field * 72 + 72, n * 128 : n * 128 + 128]
                ref[i : i + 1, :] = jnp.sum(jnp.where(mask, part, 0.0), 0, keepdims=True)
    group = 32
    lane = lax.broadcasted_iota(I32, (group, LANES), 1)
    plant_row = lax.broadcasted_iota(I32, (group // 8, 1), 0)
    collar_line = jnp.zeros((1, LANES), F32)
    for g in range(BLOCKS // group):
        at = slice(g * group, g * group + group)
        hs, ks, rr = (seg_head[at, :], seg_cond[at, :], radial_in[at, :])
        radial = rr * ks / (rr + ks)
        right = jnp.where(lane == 127, 0.0, axial[at, :])
        left = pltpu.roll(right, 1, 1)
        second = collar_link[at, :]
        first = radial * hs
        diagonal = radial + second + left + right
        lower, upper = (-left, -right)
        for step in range(7):
            stride = 2**step
            inverse = 1.0 / diagonal
            low = -lower * pltpu.roll(inverse, stride, 1)
            high = -upper * pltpu.roll(inverse, 128 - stride, 1)
            first, second = (
                x + low * pltpu.roll(x, stride, 1) + high * pltpu.roll(x, 128 - stride, 1)
                for x in (first, second)
            )
            diagonal = diagonal + low * lower + high * upper
            if step < 6:
                lower = low * pltpu.roll(lower, stride, 1)
                upper = high * pltpu.roll(upper, 128 - stride, 1)
        inverse = 1.0 / diagonal
        free, collar = (first * inverse, second * inverse)

        def per_plant(x):
            return jnp.sum(jnp.sum(x.reshape(group // 8, 8, LANES), 1), 1, keepdims=True)

        mine = lax.broadcasted_iota(I32, (group // 8, LANES), 1) == plant_row + g * (group // 8)
        need = jnp.sum(jnp.where(mine, demand[...], 0.0), 1, keepdims=True)
        head = (per_plant(radial * (hs - free)) - need) / per_plant(radial * collar)
        spread = jnp.broadcast_to(head[:, None, :], (group // 8, 8, LANES)).reshape(group, LANES)
        uptake[at, :] = radial * (hs - (free + spread * collar))
        collar_line = collar_line + jnp.sum(jnp.where(mine, head, 0.0), 0, keepdims=True)
    collar_out[...] = collar_line[:, 0:PLANTS]
    slot_rows = lax.broadcasted_iota(I32, (80, LANES), 0).astype(F32).astype(BF16)
    slot_cols = columns
    total = jnp.zeros((160, LANES), F32)
    for start in range(0, BLOCKS, 8):
        values, spots = ([], [])
        for i in range(start, start + 8):
            where = code[i : i + 1, :]
            hi, lo = split(uptake[i : i + 1, :])
            mask = slot_rows == jnp.broadcast_to((where >> 7).astype(F32).astype(BF16), (80, LANES))
            values.append(
                jnp.concatenate(
                    [jnp.where(mask, jnp.broadcast_to(v, (80, LANES)), zero) for v in (hi, lo)], 0
                )
            )
            wanted = jnp.broadcast_to((where & 127).astype(F32).astype(BF16), (128, LANES))
            spots.append(jnp.where(slot_cols == wanted, one, zero))
        total = total + lax.dot_general(
            jnp.concatenate(values, 1),
            jnp.concatenate(spots, 1),
            (((1,), (1,)), ((), ())),
            preferred_element_type=F32,
        )
    summed[...] = total[0:72] + total[80:152]
    for n, place in enumerate(places):
        for dy, out in enumerate((out_minus, out_here, out_plus)):
            out[n * 8 : n * 8 + 8, :] = eight(summed, (place * 3 + dy) * 8)


def sink_of(pieces, row, col):
    low_rows = lax.broadcasted_iota(I32, (128, LANES), 0).astype(F32).astype(BF16)
    places_of = lax.broadcasted_iota(I32, (256, LANES), 0).astype(F32).astype(BF16)
    one, zero = (jnp.ones((), BF16), jnp.zeros((), BF16))
    total = jnp.zeros((256, 256), F32)
    for source, base, k in pieces:
        values, places = ([], [])
        rows8, cols8 = (eight(x, k * 8) for x in (row, col))
        for chunk in range(8):
            r, c = (rows8[chunk : chunk + 1], cols8[chunk : chunk + 1])
            hi, lo = split(source[base + chunk : base + chunk + 1, :])
            mask = low_rows == jnp.broadcast_to((r & 127).astype(F32).astype(BF16), (128, LANES))
            values.append(
                jnp.concatenate(
                    [jnp.where(mask, jnp.broadcast_to(v, (128, LANES)), zero) for v in (hi, lo)], 0
                )
            )
            wanted = ((r >> 7) * 128 + c).astype(F32).astype(BF16)
            places.append(jnp.where(places_of == jnp.broadcast_to(wanted, (256, LANES)), one, zero))
        total = total + lax.dot_general(
            jnp.concatenate(values, 1),
            jnp.concatenate(places, 1),
            (((1,), (1,)), ((), ())),
            preferred_element_type=F32,
        )
    return total[0:128] + total[128:256]


def new_head(cross, row, col, numerator, denominator, head_new):
    place = x_places()[1]
    sink = sink_of([(cross, dy * 8, place * 3 + dy) for dy in range(3)], row, col)
    for half in range(2):
        at = slice(half * 128, half * 128 + 128)
        head_new[at, :] = (numerator[at, :] - SINK_GAIN * sink[:, at]) / denominator[at, :]


def next_kernel(
    cross, row, col, numerator, denominator, sat, alpha_dry, wet,
    head, cond, chip_edge, cross_edge, edge_minus, edge_plus, weight,
):
    new_head(cross, row, col, numerator, denominator, head)
    for layer in range(LAYERS):
        at = slice(layer * 8, layer * 8 + 8)
        cond[at, :] = conduct(head[at, :], sat[at, :], alpha_dry[at, :] * (1.0 + wet[at, :].astype(F32)))
    lay_cells(head, cond, weight, chip_edge, cross_edge, edge_minus, edge_plus)


def last_kernel(cross, row, col, numerator, denominator, head):
    new_head(cross, row, col, numerator, denominator, head)


def call(kernel, outs, scratch=(), specs=None, micros=1):
    shapes = [jax.ShapeDtypeStruct(shape, dtype) for shape, dtype in outs]
    return pl.pallas_call(
        kernel,
        out_shape=shapes,
        scratch_shapes=[pltpu.VMEM(*x) if isinstance(x, tuple) else x for x in scratch],
        compiler_params=pltpu.CompilerParams(vmem_limit_bytes=VMEM_LIMIT),
        cost_estimate=pl.CostEstimate(
            flops=micros * 10**9, bytes_accessed=micros * 3 * 10**6, transcendentals=0
        ),
        **({} if specs is None else {"in_specs": specs}),
    )


MESSAGE = ((112, 128), F32)
EDGE = ((64, 128), F32)
SLOT = ((48, 128), F32)
SIDES = [((8, 128), F32)] * 2 + [((256, 512), BF16)]


def up(x, axis):
    size = lax.axis_size(axis)
    return lax.ppermute(x, axis, [(i, (i + 1) % size) for i in range(size)])


def down(x, axis):
    size = lax.axis_size(axis)
    return lax.ppermute(x, axis, [((i + 1) % size, i) for i in range(size)])


def swap(x, axis, first):
    size = lax.axis_size(axis)
    pairs = [((first + i) % size, (first + i + 1) % size) for i in range(0, size, 2)]
    return lax.ppermute(x, axis, [p for i, j in pairs for p in ((i, j), (j, i))])


def spread(row, col, chip_edge, cross, edge_minus, edge_plus, weight):
    from_cross = swap(cross, "gx", 1)
    gate = lax.ppermute(edge_minus, "gx", [(2, 3), (3, 2)])
    chip, here = call(rest_kernel, [MESSAGE, SLOT], micros=2)(row, col, weight, chip_edge, gate)
    from_chip = swap(chip, "gx", 0)
    parts = (from_chip, here, from_cross)
    side_minus = up(jnp.concatenate([x[32:48] for x in parts] + [edge_plus], 0), "gy")
    side_plus = down(jnp.concatenate([x[0:16] for x in parts] + [edge_minus], 0), "gy")
    return (*parts, side_minus, side_plus)


def give_back(minus, here, plus):
    back = (up(minus, "gy"), here, down(plus, "gy"))
    from_cross = swap(jnp.concatenate([x[16:24] for x in back], 0), "gx", 1)
    from_chip = swap(jnp.concatenate([x[0:8] for x in back], 0), "gx", 0)
    return (back, (from_chip, from_cross))


def on_device(
    head_start,
    sat_conduct,
    alpha_dry,
    wet_flag,
    reversal_head,
    send_row,
    send_col,
    root_radial,
    root_axial,
    stem_link,
    entry_seg,
    source_dev,
    source_slot,
    demand,
):
    tile = head_start.shape
    head, sat, alpha, wet, reversal = (
        x.reshape(CELLS, LANES) for x in (head_start, sat_conduct, alpha_dry, wet_flag, reversal_head)
    )
    rows_gx = lax.axis_size("gx")
    cols_gy = lax.axis_size("gy")
    offset_k = (lax.axis_index("gx") - source_dev // cols_gy + 1) % rows_gx * 3 + (
        lax.axis_index("gy") - source_dev % cols_gy + 1
    ) % cols_gy
    code = offset_k * send_row.shape[2] + source_slot
    row, col = (x.reshape(SLOTS, LANES) for x in (send_row, send_col))
    head_old = head
    cond = conduct(head, sat, alpha * (1.0 + wet.astype(F32)))
    messages = call(start_kernel, [EDGE, MESSAGE] + SIDES, micros=2)(head, cond, row, col)
    collar_link, need = call(collar_kernel, [((BLOCKS, LANES), F32), ((1, LANES), F32)])(
        stem_link.reshape(1, BLOCKS), entry_seg.reshape(1, BLOCKS), demand.reshape(1, PLANTS)
    )
    for iteration in range(PICARD):
        got = spread(row, col, *messages)
        *sums, collar = call(
            root_kernel,
            [((24, 128), F32)] * 3 + [((1, PLANTS), F32)],
            [((144, 256), BF16), ((144, 128), F32)] + [((128, 128), F32)] * 3 + [((72, 128), F32)],
            micros=6,
        )(*got, code, root_radial, root_axial, collar_link, need)
        near, (from_chip, from_cross) = give_back(*sums)
        numerator, denominator = call(
            terms_kernel,
            [((CELLS, LANES), F32)] * 2,
            [((128, 128), F32)],
        )(
            head, cond, head_old, alpha, wet, reversal, got[0], got[2], got[3], got[4],
            *near, from_chip, row, col,
        )
        if iteration < PICARD - 1:
            head, cond, chip_edge, cross_edge, *sides, weight = call(
                next_kernel, [((CELLS, LANES), F32)] * 2 + [EDGE] * 2 + SIDES, micros=2
            )(from_cross, row, col, numerator, denominator, sat, alpha, wet)
            (cross,) = call(cross_kernel, [MESSAGE])(row, col, weight, cross_edge)
            messages = (chip_edge, cross, *sides, weight)
        else:
            (head,) = call(last_kernel, [((CELLS, LANES), F32)])(
                from_cross, row, col, numerator, denominator
            )
    return (head.reshape(tile), collar.reshape(-1))


def solution(mesh):
    tile, lists, blocks, line = (
        P(None, "gx", "gy"),
        P(("gx", "gy"), None, None),
        P(("gx", "gy"), None),
        P(("gx", "gy")),
    )
    return jax.shard_map(
        on_device,
        mesh=mesh,
        in_specs=(tile,) * 5 + (lists,) * 2 + (blocks,) * 2 + (line,) * 2 + (blocks,) * 2 + (line,),
        out_specs=(tile, line),
        check_vma=False,
    )
```

```python
import jax
import jax.numpy as jnp
from jax import lax
from jax.experimental import pallas as pl
from jax.experimental.pallas import tpu as pltpu
from jax.sharding import PartitionSpec as P

PICARD = 2
PORE_INDEX = 1.6
PORE_POWER = 0.375
SPAN_THETA = 0.35
STORAGE = 0.01
SINK_GAIN = 4.0

F32, BF16, I32 = (jnp.float32, jnp.bfloat16, jnp.int32)
VMEM_LIMIT = 48 * 2**20
LAYERS, CELLS, LANES, SLOTS, BLOCKS, PLANTS = (32, 256, 128, 72, 128, 16)


def split(x):
    hi = x.astype(BF16)
    return (hi, (x - hi.astype(F32)).astype(BF16))


def conduct(head, sat_conduct, alpha):
    power = jnp.exp(PORE_INDEX * jnp.log(alpha * jnp.abs(head)))
    root = jnp.exp((-0.5 * PORE_POWER) * jnp.log(1.0 + power))
    inner = 1.0 - jnp.exp(-PORE_POWER * jnp.log(1.0 + 1.0 / power))
    return sat_conduct * root * inner * inner


def capacity(head, alpha_dry, wetting, reversal_head):
    alpha = alpha_dry * (1.0 + wetting)
    log_scaled = jnp.log(alpha * jnp.abs(head))
    log_term = jnp.log(1.0 + jnp.exp(PORE_INDEX * log_scaled))
    slope = (
        (PORE_POWER * PORE_INDEX)
        * alpha
        * jnp.exp((PORE_INDEX - 1.0) * log_scaled + (-PORE_POWER - 1.0) * log_term)
    )
    turned = jnp.exp(PORE_INDEX * jnp.log(alpha_dry * jnp.abs(reversal_head)))
    ratio = jnp.exp(PORE_POWER * (jnp.log(1.0 + 2.0**PORE_INDEX * turned) - jnp.log(1.0 + turned)))
    factor = wetting * ratio + (1.0 - wetting)
    return SPAN_THETA * factor * slope + STORAGE


def x_places():
    odd = lax.rem(lax.axis_index("gx"), 2)
    return (2 - 2 * odd, 2 * odd)


def lay_cells(head, cond, weight, chip_edge, cross, edge_minus, edge_plus):
    even = x_places()[0] == 2
    for field, ref in enumerate((head, cond)):
        for half in range(2):
            turned = ref[half * 128 : half * 128 + 128, :].T
            edge_minus[field * 2 + half : field * 2 + half + 1, :] = turned[0:1]
            edge_plus[field * 2 + half : field * 2 + half + 1, :] = turned[127:128]
            hi, lo = split(turned)
            weight[field * 128 : field * 128 + 128, half * 128 : half * 128 + 128] = hi
            weight[field * 128 : field * 128 + 128, 256 + half * 128 : 384 + half * 128] = lo
        first = ref[pl.ds(0, LAYERS, stride=8), :]
        last = ref[pl.ds(7, LAYERS, stride=8), :]
        chip_edge[32 * field : 32 * field + 32, :] = jnp.where(even, last, first)
        at = cross.shape[0] - 64 + 32 * field
        cross[at : at + 32, :] = jnp.where(even, first, last)
    edge_minus[4:8, :] = jnp.zeros((4, LANES), F32)
    edge_plus[4:8, :] = jnp.zeros((4, LANES), F32)


def eight(ref, at):
    return ref[pl.ds(pl.multiple_of(at, 8), 8), :]


def gather_cells(row, col, weight, outs):
    cells = lax.broadcasted_iota(I32, (CELLS, LANES), 0).astype(F32).astype(BF16)
    columns = lax.broadcasted_iota(I32, (LANES, LANES), 0)
    one, zero = (jnp.ones((), BF16), jnp.zeros((), BF16))
    for out, place in outs:
        for dy in range(3):
            rows8, cols8 = (eight(x, (place * 3 + dy) * 8) for x in (row, col))
            for chunk in range(0, 8, 2):
                picks = []
                for i in (chunk, chunk + 1):
                    wanted = rows8[i : i + 1].astype(F32).astype(BF16)
                    wanted = jnp.broadcast_to(wanted, (CELLS, LANES))
                    picks.append(jnp.where(cells == wanted, one, zero))
                pick = jnp.concatenate(picks, 1)
                got = lax.dot_general(
                    weight[...],
                    jnp.concatenate([pick, pick], 0),
                    (((1,), (0,)), ((), ())),
                    preferred_element_type=F32,
                )
                for n, i in enumerate((chunk, chunk + 1)):
                    mask = columns == cols8[i : i + 1]
                    for field in range(2):
                        part = got[field * 128 : field * 128 + 128, n * 128 : n * 128 + 128]
                        at = dy * 16 + field * 8 + i
                        out[at : at + 1, :] = jnp.sum(jnp.where(mask, part, 0.0), 0, keepdims=True)


def leads():
    return lax.axis_index("gx") == 0


def start_kernel(
    head, cond, row, col, chip_edge, cross, edge_minus, edge_plus, weight, chip
):
    lay_cells(head, cond, weight, chip_edge, cross, edge_minus, edge_plus)
    gather_cells(row, col, weight, ((cross, x_places()[1]),))

    @pl.when(leads())
    def _():
        gather_cells(row, col, weight, ((chip, x_places()[0]),))


def first_rest_kernel(row, col, weight, _, chip_in, chip, here):
    @pl.when(leads())
    def _():
        chip[...] = chip_in[...]
        gather_cells(row, col, weight, ((here, 1),))

    @pl.when(jnp.logical_not(leads()))
    def _():
        gather_cells(row, col, weight, ((chip, x_places()[0]), (here, 1)))


def cross_kernel(row, col, weight, cross_edge, cross):
    gather_cells(row, col, weight, ((cross, x_places()[1]),))
    cross[48:112, :] = cross_edge[...]


def rest_kernel(row, col, weight, _, chip, here):
    gather_cells(row, col, weight, ((chip, x_places()[0]), (here, 1)))


def collar_kernel(stem, entry, demand, second, need):
    sub = lax.broadcasted_iota(I32, (BLOCKS, LANES), 0)
    lane = lax.broadcasted_iota(I32, (BLOCKS, LANES), 1)
    own = sub == lane
    stem_col = jnp.sum(jnp.where(own, stem[...], 0.0), 1, keepdims=True)
    entry_col = jnp.sum(jnp.where(own, entry[...].astype(F32), 0.0), 1, keepdims=True)
    second[...] = jnp.where(lane.astype(F32) == entry_col, stem_col, 0.0)
    need[...] = jnp.zeros((1, LANES), F32)
    need[:, 0:PLANTS] = demand[...]


def terms_kernel(
    head, cond, head_old, alpha_dry, wet, reversal, chip_edges, cross, side_minus, side_plus,
    back_minus, back_here, back_plus, back_chip, row, col,
    numerator, denominator, halo,
):
    pieces = [(x, 8, 3 + dy) for dy, x in enumerate((back_minus, back_here, back_plus))]
    pieces += [(back_chip, dy * 8, x_places()[0] * 3 + dy) for dy in range(3)]
    sink = SINK_GAIN * sink_of(pieces, row, col)
    even = x_places()[0] == 2
    from_plus = jnp.where(even, chip_edges[...], cross[48:112, :])
    from_minus = jnp.where(even, cross[48:112, :], chip_edges[...])
    halo[...] = jnp.zeros_like(halo)
    turned = []
    for i in range(4):
        halo[0:1, :] = side_minus[48 + i : 49 + i, :]
        halo[127:128, :] = side_plus[48 + i : 49 + i, :]
        turned.append(halo[...].T)
    sub = lax.broadcasted_iota(I32, (8, LANES), 0)
    lane = lax.broadcasted_iota(I32, (8, LANES), 1)
    for layer in range(LAYERS):
        at = slice(layer * 8, layer * 8 + 8)
        h, c = (head[at, :], cond[at, :])
        cap = capacity(h, alpha_dry[at, :], wet[at, :].astype(F32), reversal[at, :])
        num, den = (cap * head_old[at, :], cap)
        local = slice(layer % 16 * 8, layer % 16 * 8 + 8)
        halo_h, halo_c = (turned[layer // 16][local], turned[2 + layer // 16][local])

        def add(num, den, near_h, near_c):
            face = 0.5 * (c + near_c)
            return (num + face * near_h, den + face)

        def beside(x, line, spot):
            return jnp.where(sub == spot, jnp.broadcast_to(line, (8, LANES)), x)

        num, den = add(
            num, den,
            beside(pltpu.roll(h, 7, 0), from_plus[layer : layer + 1], 7),
            beside(pltpu.roll(c, 7, 0), from_plus[32 + layer : 33 + layer], 7),
        )
        num, den = add(
            num, den,
            beside(pltpu.roll(h, 1, 0), from_minus[layer : layer + 1], 0),
            beside(pltpu.roll(c, 1, 0), from_minus[32 + layer : 33 + layer], 0),
        )
        num, den = add(
            num, den,
            jnp.where(lane == 127, halo_h, pltpu.roll(h, 127, 1)),
            jnp.where(lane == 127, halo_c, pltpu.roll(c, 127, 1)),
        )
        num, den = add(
            num, den,
            jnp.where(lane == 0, halo_h, pltpu.roll(h, 1, 1)),
            jnp.where(lane == 0, halo_c, pltpu.roll(c, 1, 1)),
        )
        if layer > 0:
            above = slice(layer * 8 - 8, layer * 8)
            num, den = add(num, den, head[above, :] + 1.0, cond[above, :])
        if layer < LAYERS - 1:
            below = slice(layer * 8 + 8, layer * 8 + 16)
            num, den = add(num, den, head[below, :] - 1.0, cond[below, :])
        else:
            num = num - c
        half = layer // 16
        numerator[at, :] = num - sink[local, half * 128 : half * 128 + 128]
        denominator[at, :] = den


def root_kernel(
    chip, here, cross, side_minus, side_plus, code, radial_in, axial, collar_link, demand,
    out_minus, out_here, out_plus, collar_out, weight, table, seg_head, seg_cond, uptake, summed,
):
    cross_place, chip_place = x_places()
    places = (chip_place, 1, cross_place)
    for n, place in enumerate(places):
        for dy in range(3):
            if dy == 1:
                source, at = ((chip, here, cross)[n], 16)
            else:
                source, at = ((side_plus, None, side_minus)[dy], n * 16)
            for field in range(2):
                to = pl.multiple_of(field * 72 + (place * 3 + dy) * 8, 8)
                table[pl.ds(to, 8), :] = source[at + field * 8 : at + field * 8 + 8, :]
    weight[:, 0:128], weight[:, 128:256] = split(table[...])
    columns = lax.broadcasted_iota(I32, (128, LANES), 0).astype(F32).astype(BF16)
    rows = lax.broadcasted_iota(I32, (SLOTS, LANES), 0)
    one, zero = (jnp.ones((), BF16), jnp.zeros((), BF16))
    for j in range(0, BLOCKS, 8):
        picks = []
        for i in range(j, j + 8):
            wanted = jnp.broadcast_to((code[i : i + 1, :] & 127).astype(F32).astype(BF16), (128, LANES))
            picks.append(jnp.where(columns == wanted, one, zero))
        pick = jnp.concatenate(picks, 1)
        got = lax.dot_general(
            weight[...],
            jnp.concatenate([pick, pick], 0),
            (((1,), (0,)), ((), ())),
            preferred_element_type=F32,
        )
        for n, i in enumerate(range(j, j + 8)):
            mask = rows == (code[i : i + 1, :] >> 7)
            for field, ref in enumerate((seg_head, seg_cond)):
                part = got[field * 72 : field * 72 + 72, n * 128 : n * 128 + 128]
                ref[i : i + 1, :] = jnp.sum(jnp.where(mask, part, 0.0), 0, keepdims=True)
    group = 32
    lane = lax.broadcasted_iota(I32, (group, LANES), 1)
    plant_row = lax.broadcasted_iota(I32, (group // 8, 1), 0)
    collar_line = jnp.zeros((1, LANES), F32)
    for g in range(BLOCKS // group):
        at = slice(g * group, g * group + group)
        hs, ks, rr = (seg_head[at, :], seg_cond[at, :], radial_in[at, :])
        radial = rr * ks / (rr + ks)
        right = jnp.where(lane == 127, 0.0, axial[at, :])
        left = pltpu.roll(right, 1, 1)
        second = collar_link[at, :]
        first = radial * hs
        diagonal = radial + second + left + right
        lower, upper = (-left, -right)
        for step in range(7):
            stride = 2**step
            inverse = 1.0 / diagonal
            low = -lower * pltpu.roll(inverse, stride, 1)
            high = -upper * pltpu.roll(inverse, 128 - stride, 1)
            first, second = (
                x + low * pltpu.roll(x, stride, 1) + high * pltpu.roll(x, 128 - stride, 1)
                for x in (first, second)
            )
            diagonal = diagonal + low * lower + high * upper
            if step < 6:
                lower = low * pltpu.roll(lower, stride, 1)
                upper = high * pltpu.roll(upper, 128 - stride, 1)
        inverse = 1.0 / diagonal
        free, collar = (first * inverse, second * inverse)

        def per_plant(x):
            return jnp.sum(jnp.sum(x.reshape(group // 8, 8, LANES), 1), 1, keepdims=True)

        mine = lax.broadcasted_iota(I32, (group // 8, LANES), 1) == plant_row + g * (group // 8)
        need = jnp.sum(jnp.where(mine, demand[...], 0.0), 1, keepdims=True)
        head = (per_plant(radial * (hs - free)) - need) / per_plant(radial * collar)
        spread = jnp.broadcast_to(head[:, None, :], (group // 8, 8, LANES)).reshape(group, LANES)
        uptake[at, :] = radial * (hs - (free + spread * collar))
        collar_line = collar_line + jnp.sum(jnp.where(mine, head, 0.0), 0, keepdims=True)
    collar_out[...] = collar_line[:, 0:PLANTS]
    slot_rows = lax.broadcasted_iota(I32, (80, LANES), 0).astype(F32).astype(BF16)
    slot_cols = columns
    total = jnp.zeros((160, LANES), F32)
    for start in range(0, BLOCKS, 8):
        values, spots = ([], [])
        for i in range(start, start + 8):
            where = code[i : i + 1, :]
            hi, lo = split(uptake[i : i + 1, :])
            mask = slot_rows == jnp.broadcast_to((where >> 7).astype(F32).astype(BF16), (80, LANES))
            values.append(
                jnp.concatenate(
                    [jnp.where(mask, jnp.broadcast_to(v, (80, LANES)), zero) for v in (hi, lo)], 0
                )
            )
            wanted = jnp.broadcast_to((where & 127).astype(F32).astype(BF16), (128, LANES))
            spots.append(jnp.where(slot_cols == wanted, one, zero))
        total = total + lax.dot_general(
            jnp.concatenate(values, 1),
            jnp.concatenate(spots, 1),
            (((1,), (1,)), ((), ())),
            preferred_element_type=F32,
        )
    summed[...] = total[0:72] + total[80:152]
    for n, place in enumerate(places):
        for dy, out in enumerate((out_minus, out_here, out_plus)):
            out[n * 8 : n * 8 + 8, :] = eight(summed, (place * 3 + dy) * 8)


def sink_of(pieces, row, col):
    low_rows = lax.broadcasted_iota(I32, (128, LANES), 0).astype(F32).astype(BF16)
    places_of = lax.broadcasted_iota(I32, (256, LANES), 0).astype(F32).astype(BF16)
    one, zero = (jnp.ones((), BF16), jnp.zeros((), BF16))
    total = jnp.zeros((256, 256), F32)
    for source, base, k in pieces:
        values, places = ([], [])
        rows8, cols8 = (eight(x, k * 8) for x in (row, col))
        for chunk in range(8):
            r, c = (rows8[chunk : chunk + 1], cols8[chunk : chunk + 1])
            hi, lo = split(source[base + chunk : base + chunk + 1, :])
            mask = low_rows == jnp.broadcast_to((r & 127).astype(F32).astype(BF16), (128, LANES))
            values.append(
                jnp.concatenate(
                    [jnp.where(mask, jnp.broadcast_to(v, (128, LANES)), zero) for v in (hi, lo)], 0
                )
            )
            wanted = ((r >> 7) * 128 + c).astype(F32).astype(BF16)
            places.append(jnp.where(places_of == jnp.broadcast_to(wanted, (256, LANES)), one, zero))
        total = total + lax.dot_general(
            jnp.concatenate(values, 1),
            jnp.concatenate(places, 1),
            (((1,), (1,)), ((), ())),
            preferred_element_type=F32,
        )
    return total[0:128] + total[128:256]


def new_head(cross, row, col, numerator, denominator, head_new):
    place = x_places()[1]
    sink = sink_of([(cross, dy * 8, place * 3 + dy) for dy in range(3)], row, col)
    for half in range(2):
        at = slice(half * 128, half * 128 + 128)
        head_new[at, :] = (numerator[at, :] - SINK_GAIN * sink[:, at]) / denominator[at, :]


def next_kernel(
    cross, row, col, numerator, denominator, sat, alpha_dry, wet,
    head, cond, chip_edge, cross_edge, edge_minus, edge_plus, weight,
):
    new_head(cross, row, col, numerator, denominator, head)
    for layer in range(LAYERS):
        at = slice(layer * 8, layer * 8 + 8)
        cond[at, :] = conduct(head[at, :], sat[at, :], alpha_dry[at, :] * (1.0 + wet[at, :].astype(F32)))
    lay_cells(head, cond, weight, chip_edge, cross_edge, edge_minus, edge_plus)


def last_kernel(cross, row, col, numerator, denominator, head):
    new_head(cross, row, col, numerator, denominator, head)


def call(kernel, outs, scratch=(), specs=None, micros=1):
    shapes = [jax.ShapeDtypeStruct(shape, dtype) for shape, dtype in outs]
    return pl.pallas_call(
        kernel,
        out_shape=shapes,
        scratch_shapes=[pltpu.VMEM(*x) if isinstance(x, tuple) else x for x in scratch],
        compiler_params=pltpu.CompilerParams(vmem_limit_bytes=VMEM_LIMIT),
        cost_estimate=pl.CostEstimate(
            flops=micros * 10**9, bytes_accessed=micros * 3 * 10**6, transcendentals=0
        ),
        **({} if specs is None else {"in_specs": specs}),
    )


MESSAGE = ((112, 128), F32)
EDGE = ((64, 128), F32)
SLOT = ((48, 128), F32)
SIDES = [((8, 128), F32)] * 2 + [((256, 512), BF16)]


def up(x, axis):
    size = lax.axis_size(axis)
    return lax.ppermute(x, axis, [(i, (i + 1) % size) for i in range(size)])


def down(x, axis):
    size = lax.axis_size(axis)
    return lax.ppermute(x, axis, [((i + 1) % size, i) for i in range(size)])


def swap(x, axis, first):
    size = lax.axis_size(axis)
    pairs = [((first + i) % size, (first + i + 1) % size) for i in range(0, size, 2)]
    return lax.ppermute(x, axis, [p for i, j in pairs for p in ((i, j), (j, i))])


def spread(row, col, chip_edge, cross, edge_minus, edge_plus, weight, *early):
    from_cross = swap(cross, "gx", 1)
    chip_edges = swap(chip_edge, "gx", 0)
    chip, here = call(first_rest_kernel if early else rest_kernel, [SLOT] * 2, micros=2)(
        row, col, weight, chip_edges, *early
    )
    from_chip = swap(chip, "gx", 0)
    parts = (from_chip, here, from_cross)
    side_minus = up(jnp.concatenate([x[32:48] for x in parts] + [edge_plus], 0), "gy")
    side_plus = down(jnp.concatenate([x[0:16] for x in parts] + [edge_minus], 0), "gy")
    return (*parts, side_minus, side_plus), chip_edges


def give_back(minus, here, plus):
    back = (up(minus, "gy"), here, down(plus, "gy"))
    from_cross = swap(jnp.concatenate([x[16:24] for x in back], 0), "gx", 1)
    from_chip = swap(jnp.concatenate([x[0:8] for x in back], 0), "gx", 0)
    return (back, (from_chip, from_cross))


def on_device(
    head_start,
    sat_conduct,
    alpha_dry,
    wet_flag,
    reversal_head,
    send_row,
    send_col,
    root_radial,
    root_axial,
    stem_link,
    entry_seg,
    source_dev,
    source_slot,
    demand,
):
    tile = head_start.shape
    head, sat, alpha, wet, reversal = (
        x.reshape(CELLS, LANES) for x in (head_start, sat_conduct, alpha_dry, wet_flag, reversal_head)
    )
    rows_gx = lax.axis_size("gx")
    cols_gy = lax.axis_size("gy")
    offset_k = (lax.axis_index("gx") - source_dev // cols_gy + 1) % rows_gx * 3 + (
        lax.axis_index("gy") - source_dev % cols_gy + 1
    ) % cols_gy
    code = offset_k * send_row.shape[2] + source_slot
    row, col = (x.reshape(SLOTS, LANES) for x in (send_row, send_col))
    head_old = head
    cond = conduct(head, sat, alpha * (1.0 + wet.astype(F32)))
    messages = call(start_kernel, [EDGE, MESSAGE] + SIDES + [SLOT], micros=2)(head, cond, row, col)
    collar_link, need = call(collar_kernel, [((BLOCKS, LANES), F32), ((1, LANES), F32)])(
        stem_link.reshape(1, BLOCKS), entry_seg.reshape(1, BLOCKS), demand.reshape(1, PLANTS)
    )
    for iteration in range(PICARD):
        got, chip_edges = spread(row, col, *messages)
        *sums, collar = call(
            root_kernel,
            [((24, 128), F32)] * 3 + [((1, PLANTS), F32)],
            [((144, 256), BF16), ((144, 128), F32)] + [((128, 128), F32)] * 3 + [((72, 128), F32)],
            micros=6,
        )(*got, code, root_radial, root_axial, collar_link, need)
        near, (from_chip, from_cross) = give_back(*sums)
        numerator, denominator = call(
            terms_kernel,
            [((CELLS, LANES), F32)] * 2,
            [((128, 128), F32)],
        )(
            head, cond, head_old, alpha, wet, reversal, chip_edges, got[2], got[3], got[4],
            *near, from_chip, row, col,
        )
        if iteration < PICARD - 1:
            head, cond, chip_edge, cross_edge, *sides, weight = call(
                next_kernel, [((CELLS, LANES), F32)] * 2 + [EDGE] * 2 + SIDES, micros=2
            )(from_cross, row, col, numerator, denominator, sat, alpha, wet)
            (cross,) = call(cross_kernel, [MESSAGE])(row, col, weight, cross_edge)
            messages = (chip_edge, cross, *sides, weight)
        else:
            (head,) = call(last_kernel, [((CELLS, LANES), F32)])(
                from_cross, row, col, numerator, denominator
            )
    return (head.reshape(tile), collar.reshape(-1))


def solution(mesh):
    tile, lists, blocks, line = (
        P(None, "gx", "gy"),
        P(("gx", "gy"), None, None),
        P(("gx", "gy"), None),
        P(("gx", "gy")),
    )
    return jax.shard_map(
        on_device,
        mesh=mesh,
        in_specs=(tile,) * 5 + (lists,) * 2 + (blocks,) * 2 + (line,) * 2 + (blocks,) * 2 + (line,),
        out_specs=(tile, line),
        check_vma=False,
    )
```

```python
import jax
import jax.numpy as jnp
from jax import lax
from jax.experimental import pallas as pl
from jax.experimental.pallas import tpu as pltpu
from jax.sharding import PartitionSpec as P

PICARD = 2
PORE_INDEX = 1.6
PORE_POWER = 0.375
SPAN_THETA = 0.35
STORAGE = 0.01
SINK_GAIN = 4.0

F32, BF16, I32 = (jnp.float32, jnp.bfloat16, jnp.int32)
VMEM_LIMIT = 48 * 2**20
LAYERS, CELLS, LANES, SLOTS, BLOCKS, PLANTS = (32, 256, 128, 72, 128, 16)


def split(x):
    hi = x.astype(BF16)
    return (hi, (x - hi.astype(F32)).astype(BF16))


def inverted(x):
    near = pltpu.reciprocal(x, approx=True)
    near = near * (2.0 - x * near)
    return near * (2.0 - x * near)


def conduct(head, sat_conduct, alpha):
    power = jnp.exp(PORE_INDEX * jnp.log(alpha * jnp.abs(head)))
    root = jnp.exp((-0.5 * PORE_POWER) * jnp.log(1.0 + power))
    inner = 1.0 - jnp.exp(-PORE_POWER * jnp.log(1.0 + 1.0 / power))
    return sat_conduct * root * inner * inner


def capacity(head, alpha_dry, wetting, reversal_head):
    alpha = alpha_dry * (1.0 + wetting)
    log_scaled = jnp.log(alpha * jnp.abs(head))
    log_term = jnp.log(1.0 + jnp.exp(PORE_INDEX * log_scaled))
    slope = (
        (PORE_POWER * PORE_INDEX)
        * alpha
        * jnp.exp((PORE_INDEX - 1.0) * log_scaled + (-PORE_POWER - 1.0) * log_term)
    )
    turned = jnp.exp(PORE_INDEX * jnp.log(alpha_dry * jnp.abs(reversal_head)))
    ratio = jnp.exp(PORE_POWER * (jnp.log(1.0 + 2.0**PORE_INDEX * turned) - jnp.log(1.0 + turned)))
    factor = wetting * ratio + (1.0 - wetting)
    return SPAN_THETA * factor * slope + STORAGE


def x_places():
    odd = lax.rem(lax.axis_index("gx"), 2)
    return (2 - 2 * odd, 2 * odd)


def lay_cells(head, cond, weight, chip_edge, cross, edge_minus, edge_plus):
    even = x_places()[0] == 2
    for field, ref in enumerate((head, cond)):
        for half in range(2):
            turned = ref[half * 128 : half * 128 + 128, :].T
            edge_minus[field * 2 + half : field * 2 + half + 1, :] = turned[0:1]
            edge_plus[field * 2 + half : field * 2 + half + 1, :] = turned[127:128]
            hi, lo = split(turned)
            weight[field * 128 : field * 128 + 128, half * 128 : half * 128 + 128] = hi
            weight[field * 128 : field * 128 + 128, 256 + half * 128 : 384 + half * 128] = lo
        first = ref[pl.ds(0, LAYERS, stride=8), :]
        last = ref[pl.ds(7, LAYERS, stride=8), :]
        chip_edge[32 * field : 32 * field + 32, :] = jnp.where(even, last, first)
        at = cross.shape[0] - 64 + 32 * field
        cross[at : at + 32, :] = jnp.where(even, first, last)
    edge_minus[4:8, :] = jnp.zeros((4, LANES), F32)
    edge_plus[4:8, :] = jnp.zeros((4, LANES), F32)


def eight(ref, at):
    return ref[pl.ds(pl.multiple_of(at, 8), 8), :]


def gather_cells(row, col, weight, outs):
    cells = lax.broadcasted_iota(I32, (CELLS, LANES), 0).astype(F32).astype(BF16)
    columns = lax.broadcasted_iota(I32, (LANES, LANES), 0)
    one, zero = (jnp.ones((), BF16), jnp.zeros((), BF16))
    for out, place in outs:
        for dy in range(3):
            rows8, cols8 = (eight(x, (place * 3 + dy) * 8) for x in (row, col))
            for chunk in range(0, 8, 2):
                picks = []
                for i in (chunk, chunk + 1):
                    wanted = rows8[i : i + 1].astype(F32).astype(BF16)
                    wanted = jnp.broadcast_to(wanted, (CELLS, LANES))
                    picks.append(jnp.where(cells == wanted, one, zero))
                pick = jnp.concatenate(picks, 1)
                got = lax.dot_general(
                    weight[...],
                    jnp.concatenate([pick, pick], 0),
                    (((1,), (0,)), ((), ())),
                    preferred_element_type=F32,
                )
                for n, i in enumerate((chunk, chunk + 1)):
                    mask = columns == cols8[i : i + 1]
                    for field in range(2):
                        part = got[field * 128 : field * 128 + 128, n * 128 : n * 128 + 128]
                        at = dy * 16 + field * 8 + i
                        out[at : at + 1, :] = jnp.sum(jnp.where(mask, part, 0.0), 0, keepdims=True)


def leads():
    return lax.axis_index("gx") == 0


def start_kernel(
    head, cond, row, col, chip_edge, cross, edge_minus, edge_plus, weight, chip
):
    lay_cells(head, cond, weight, chip_edge, cross, edge_minus, edge_plus)
    gather_cells(row, col, weight, ((cross, x_places()[1]),))

    @pl.when(leads())
    def _():
        gather_cells(row, col, weight, ((chip, x_places()[0]),))


def first_rest_kernel(row, col, weight, _, chip_in, chip, here):
    @pl.when(leads())
    def _():
        chip[...] = chip_in[...]
        gather_cells(row, col, weight, ((here, 1),))

    @pl.when(jnp.logical_not(leads()))
    def _():
        gather_cells(row, col, weight, ((chip, x_places()[0]), (here, 1)))


def cross_kernel(row, col, weight, cross_edge, cross):
    gather_cells(row, col, weight, ((cross, x_places()[1]),))
    cross[48:112, :] = cross_edge[...]


def rest_kernel(row, col, weight, _, chip, here):
    gather_cells(row, col, weight, ((chip, x_places()[0]), (here, 1)))


def collar_kernel(stem, entry, demand, second, need):
    sub = lax.broadcasted_iota(I32, (BLOCKS, LANES), 0)
    lane = lax.broadcasted_iota(I32, (BLOCKS, LANES), 1)
    own = sub == lane
    stem_col = jnp.sum(jnp.where(own, stem[...], 0.0), 1, keepdims=True)
    entry_col = jnp.sum(jnp.where(own, entry[...].astype(F32), 0.0), 1, keepdims=True)
    second[...] = jnp.where(lane.astype(F32) == entry_col, stem_col, 0.0)
    need[...] = jnp.zeros((1, LANES), F32)
    need[:, 0:PLANTS] = demand[...]


def terms_kernel(
    head, cond, head_old, alpha_dry, wet, reversal, chip_edges, cross, side_minus, side_plus,
    back_minus, back_here, back_plus, back_chip, row, col,
    numerator, denominator, halo,
):
    pieces = [(x, 8, 3 + dy) for dy, x in enumerate((back_minus, back_here, back_plus))]
    pieces += [(back_chip, dy * 8, x_places()[0] * 3 + dy) for dy in range(3)]
    sink = SINK_GAIN * sink_of(pieces, row, col)
    even = x_places()[0] == 2
    from_plus = jnp.where(even, chip_edges[...], cross[48:112, :])
    from_minus = jnp.where(even, cross[48:112, :], chip_edges[...])
    halo[...] = jnp.zeros_like(halo)
    turned = []
    for i in range(4):
        halo[0:1, :] = side_minus[48 + i : 49 + i, :]
        halo[127:128, :] = side_plus[48 + i : 49 + i, :]
        turned.append(halo[...].T)
    sub = lax.broadcasted_iota(I32, (8, LANES), 0)
    lane = lax.broadcasted_iota(I32, (8, LANES), 1)
    for layer in range(LAYERS):
        at = slice(layer * 8, layer * 8 + 8)
        h, c = (head[at, :], cond[at, :])
        cap = capacity(h, alpha_dry[at, :], wet[at, :].astype(F32), reversal[at, :])
        num, den = (cap * head_old[at, :], cap)
        local = slice(layer % 16 * 8, layer % 16 * 8 + 8)
        halo_h, halo_c = (turned[layer // 16][local], turned[2 + layer // 16][local])

        def add(num, den, near_h, near_c):
            face = 0.5 * (c + near_c)
            return (num + face * near_h, den + face)

        def beside(x, line, spot):
            return jnp.where(sub == spot, jnp.broadcast_to(line, (8, LANES)), x)

        num, den = add(
            num, den,
            beside(pltpu.roll(h, 7, 0), from_plus[layer : layer + 1], 7),
            beside(pltpu.roll(c, 7, 0), from_plus[32 + layer : 33 + layer], 7),
        )
        num, den = add(
            num, den,
            beside(pltpu.roll(h, 1, 0), from_minus[layer : layer + 1], 0),
            beside(pltpu.roll(c, 1, 0), from_minus[32 + layer : 33 + layer], 0),
        )
        num, den = add(
            num, den,
            jnp.where(lane == 127, halo_h, pltpu.roll(h, 127, 1)),
            jnp.where(lane == 127, halo_c, pltpu.roll(c, 127, 1)),
        )
        num, den = add(
            num, den,
            jnp.where(lane == 0, halo_h, pltpu.roll(h, 1, 1)),
            jnp.where(lane == 0, halo_c, pltpu.roll(c, 1, 1)),
        )
        if layer > 0:
            above = slice(layer * 8 - 8, layer * 8)
            num, den = add(num, den, head[above, :] + 1.0, cond[above, :])
        if layer < LAYERS - 1:
            below = slice(layer * 8 + 8, layer * 8 + 16)
            num, den = add(num, den, head[below, :] - 1.0, cond[below, :])
        else:
            num = num - c
        half = layer // 16
        numerator[at, :] = num - sink[local, half * 128 : half * 128 + 128]
        denominator[at, :] = den


def root_kernel(
    chip, here, cross, side_minus, side_plus, code, radial_in, axial, collar_link, demand,
    out_minus, out_here, out_plus, collar_out, weight, table, seg_head, seg_cond, uptake, summed,
):
    cross_place, chip_place = x_places()
    places = (chip_place, 1, cross_place)
    for n, place in enumerate(places):
        for dy in range(3):
            if dy == 1:
                source, at = ((chip, here, cross)[n], 16)
            else:
                source, at = ((side_plus, None, side_minus)[dy], n * 16)
            for field in range(2):
                to = pl.multiple_of(field * 72 + (place * 3 + dy) * 8, 8)
                table[pl.ds(to, 8), :] = source[at + field * 8 : at + field * 8 + 8, :]
    weight[:, 0:128], weight[:, 128:256] = split(table[...])
    columns = lax.broadcasted_iota(I32, (128, LANES), 0).astype(F32).astype(BF16)
    rows = lax.broadcasted_iota(I32, (SLOTS, LANES), 0)
    one, zero = (jnp.ones((), BF16), jnp.zeros((), BF16))
    for j in range(0, BLOCKS, 8):
        picks = []
        for i in range(j, j + 8):
            wanted = jnp.broadcast_to((code[i : i + 1, :] & 127).astype(F32).astype(BF16), (128, LANES))
            picks.append(jnp.where(columns == wanted, one, zero))
        pick = jnp.concatenate(picks, 1)
        got = lax.dot_general(
            weight[...],
            jnp.concatenate([pick, pick], 0),
            (((1,), (0,)), ((), ())),
            preferred_element_type=F32,
        )
        for n, i in enumerate(range(j, j + 8)):
            mask = rows == (code[i : i + 1, :] >> 7)
            for field, ref in enumerate((seg_head, seg_cond)):
                part = got[field * 72 : field * 72 + 72, n * 128 : n * 128 + 128]
                ref[i : i + 1, :] = jnp.sum(jnp.where(mask, part, 0.0), 0, keepdims=True)
    group = 32
    lane = lax.broadcasted_iota(I32, (group, LANES), 1)
    plant_row = lax.broadcasted_iota(I32, (group // 8, 1), 0)
    collar_line = jnp.zeros((1, LANES), F32)
    for g in range(BLOCKS // group):
        at = slice(g * group, g * group + group)
        hs, ks, rr = (seg_head[at, :], seg_cond[at, :], radial_in[at, :])
        radial = rr * ks / (rr + ks)
        right = jnp.where(lane == 127, 0.0, axial[at, :])
        left = pltpu.roll(right, 1, 1)
        second = collar_link[at, :]
        first = radial * hs
        diagonal = radial + second + left + right
        lower, upper = (-left, -right)
        for step in range(7):
            stride = 2**step
            inverse = inverted(diagonal)
            low = -lower * pltpu.roll(inverse, stride, 1)
            high = -upper * pltpu.roll(inverse, 128 - stride, 1)
            first, second = (
                x + low * pltpu.roll(x, stride, 1) + high * pltpu.roll(x, 128 - stride, 1)
                for x in (first, second)
            )
            diagonal = diagonal + low * lower + high * upper
            if step < 6:
                lower = low * pltpu.roll(lower, stride, 1)
                upper = high * pltpu.roll(upper, 128 - stride, 1)
        inverse = inverted(diagonal)
        free, collar = (first * inverse, second * inverse)

        def per_plant(x):
            return jnp.sum(jnp.sum(x.reshape(group // 8, 8, LANES), 1), 1, keepdims=True)

        mine = lax.broadcasted_iota(I32, (group // 8, LANES), 1) == plant_row + g * (group // 8)
        need = jnp.sum(jnp.where(mine, demand[...], 0.0), 1, keepdims=True)
        head = (per_plant(radial * (hs - free)) - need) / per_plant(radial * collar)
        spread = jnp.broadcast_to(head[:, None, :], (group // 8, 8, LANES)).reshape(group, LANES)
        uptake[at, :] = radial * (hs - (free + spread * collar))
        collar_line = collar_line + jnp.sum(jnp.where(mine, head, 0.0), 0, keepdims=True)
    collar_out[...] = collar_line[:, 0:PLANTS]
    slot_rows = lax.broadcasted_iota(I32, (80, LANES), 0).astype(F32).astype(BF16)
    slot_cols = columns
    total = jnp.zeros((160, LANES), F32)
    for start in range(0, BLOCKS, 8):
        values, spots = ([], [])
        for i in range(start, start + 8):
            where = code[i : i + 1, :]
            hi, lo = split(uptake[i : i + 1, :])
            mask = slot_rows == jnp.broadcast_to((where >> 7).astype(F32).astype(BF16), (80, LANES))
            values.append(
                jnp.concatenate(
                    [jnp.where(mask, jnp.broadcast_to(v, (80, LANES)), zero) for v in (hi, lo)], 0
                )
            )
            wanted = jnp.broadcast_to((where & 127).astype(F32).astype(BF16), (128, LANES))
            spots.append(jnp.where(slot_cols == wanted, one, zero))
        total = total + lax.dot_general(
            jnp.concatenate(values, 1),
            jnp.concatenate(spots, 1),
            (((1,), (1,)), ((), ())),
            preferred_element_type=F32,
        )
    summed[...] = total[0:72] + total[80:152]
    for n, place in enumerate(places):
        for dy, out in enumerate((out_minus, out_here, out_plus)):
            out[n * 8 : n * 8 + 8, :] = eight(summed, (place * 3 + dy) * 8)


def sink_of(pieces, row, col):
    low_rows = lax.broadcasted_iota(I32, (128, LANES), 0).astype(F32).astype(BF16)
    places_of = lax.broadcasted_iota(I32, (256, LANES), 0).astype(F32).astype(BF16)
    one, zero = (jnp.ones((), BF16), jnp.zeros((), BF16))
    total = jnp.zeros((256, 256), F32)
    for source, base, k in pieces:
        values, places = ([], [])
        rows8, cols8 = (eight(x, k * 8) for x in (row, col))
        for chunk in range(8):
            r, c = (rows8[chunk : chunk + 1], cols8[chunk : chunk + 1])
            hi, lo = split(source[base + chunk : base + chunk + 1, :])
            mask = low_rows == jnp.broadcast_to((r & 127).astype(F32).astype(BF16), (128, LANES))
            values.append(
                jnp.concatenate(
                    [jnp.where(mask, jnp.broadcast_to(v, (128, LANES)), zero) for v in (hi, lo)], 0
                )
            )
            wanted = ((r >> 7) * 128 + c).astype(F32).astype(BF16)
            places.append(jnp.where(places_of == jnp.broadcast_to(wanted, (256, LANES)), one, zero))
        total = total + lax.dot_general(
            jnp.concatenate(values, 1),
            jnp.concatenate(places, 1),
            (((1,), (1,)), ((), ())),
            preferred_element_type=F32,
        )
    return total[0:128] + total[128:256]


def new_head(cross, row, col, numerator, denominator, head_new):
    place = x_places()[1]
    sink = sink_of([(cross, dy * 8, place * 3 + dy) for dy in range(3)], row, col)
    for half in range(2):
        at = slice(half * 128, half * 128 + 128)
        head_new[at, :] = (numerator[at, :] - SINK_GAIN * sink[:, at]) / denominator[at, :]


def next_kernel(
    cross, row, col, numerator, denominator, sat, alpha_dry, wet,
    head, cond, chip_edge, cross_edge, edge_minus, edge_plus, weight,
):
    new_head(cross, row, col, numerator, denominator, head)
    for layer in range(LAYERS):
        at = slice(layer * 8, layer * 8 + 8)
        cond[at, :] = conduct(head[at, :], sat[at, :], alpha_dry[at, :] * (1.0 + wet[at, :].astype(F32)))
    lay_cells(head, cond, weight, chip_edge, cross_edge, edge_minus, edge_plus)


def last_kernel(cross, row, col, numerator, denominator, head):
    new_head(cross, row, col, numerator, denominator, head)


def call(kernel, outs, scratch=(), specs=None, micros=1):
    shapes = [jax.ShapeDtypeStruct(shape, dtype) for shape, dtype in outs]
    return pl.pallas_call(
        kernel,
        out_shape=shapes,
        scratch_shapes=[pltpu.VMEM(*x) if isinstance(x, tuple) else x for x in scratch],
        compiler_params=pltpu.CompilerParams(vmem_limit_bytes=VMEM_LIMIT),
        cost_estimate=pl.CostEstimate(
            flops=micros * 10**9, bytes_accessed=micros * 3 * 10**6, transcendentals=0
        ),
        **({} if specs is None else {"in_specs": specs}),
    )


MESSAGE = ((112, 128), F32)
EDGE = ((64, 128), F32)
SLOT = ((48, 128), F32)
SIDES = [((8, 128), F32)] * 2 + [((256, 512), BF16)]


def up(x, axis):
    size = lax.axis_size(axis)
    return lax.ppermute(x, axis, [(i, (i + 1) % size) for i in range(size)])


def down(x, axis):
    size = lax.axis_size(axis)
    return lax.ppermute(x, axis, [((i + 1) % size, i) for i in range(size)])


def swap(x, axis, first):
    size = lax.axis_size(axis)
    pairs = [((first + i) % size, (first + i + 1) % size) for i in range(0, size, 2)]
    return lax.ppermute(x, axis, [p for i, j in pairs for p in ((i, j), (j, i))])


def spread(row, col, chip_edge, cross, edge_minus, edge_plus, weight, *early):
    from_cross = swap(cross, "gx", 1)
    chip_edges = swap(chip_edge, "gx", 0)
    chip, here = call(first_rest_kernel if early else rest_kernel, [SLOT] * 2, micros=2)(
        row, col, weight, chip_edges, *early
    )
    from_chip = swap(chip, "gx", 0)
    parts = (from_chip, here, from_cross)
    side_minus = up(jnp.concatenate([x[32:48] for x in parts] + [edge_plus], 0), "gy")
    side_plus = down(jnp.concatenate([x[0:16] for x in parts] + [edge_minus], 0), "gy")
    return (*parts, side_minus, side_plus), chip_edges


def give_back(minus, here, plus):
    back = (up(minus, "gy"), here, down(plus, "gy"))
    from_cross = swap(jnp.concatenate([x[16:24] for x in back], 0), "gx", 1)
    from_chip = swap(jnp.concatenate([x[0:8] for x in back], 0), "gx", 0)
    return (back, (from_chip, from_cross))


def on_device(
    head_start,
    sat_conduct,
    alpha_dry,
    wet_flag,
    reversal_head,
    send_row,
    send_col,
    root_radial,
    root_axial,
    stem_link,
    entry_seg,
    source_dev,
    source_slot,
    demand,
):
    tile = head_start.shape
    head, sat, alpha, wet, reversal = (
        x.reshape(CELLS, LANES) for x in (head_start, sat_conduct, alpha_dry, wet_flag, reversal_head)
    )
    rows_gx = lax.axis_size("gx")
    cols_gy = lax.axis_size("gy")
    offset_k = (lax.axis_index("gx") - source_dev // cols_gy + 1) % rows_gx * 3 + (
        lax.axis_index("gy") - source_dev % cols_gy + 1
    ) % cols_gy
    code = offset_k * send_row.shape[2] + source_slot
    row, col = (x.reshape(SLOTS, LANES) for x in (send_row, send_col))
    head_old = head
    cond = conduct(head, sat, alpha * (1.0 + wet.astype(F32)))
    messages = call(start_kernel, [EDGE, MESSAGE] + SIDES + [SLOT], micros=2)(head, cond, row, col)
    collar_link, need = call(collar_kernel, [((BLOCKS, LANES), F32), ((1, LANES), F32)])(
        stem_link.reshape(1, BLOCKS), entry_seg.reshape(1, BLOCKS), demand.reshape(1, PLANTS)
    )
    for iteration in range(PICARD):
        got, chip_edges = spread(row, col, *messages)
        *sums, collar = call(
            root_kernel,
            [((24, 128), F32)] * 3 + [((1, PLANTS), F32)],
            [((144, 256), BF16), ((144, 128), F32)] + [((128, 128), F32)] * 3 + [((72, 128), F32)],
            micros=6,
        )(*got, code, root_radial, root_axial, collar_link, need)
        near, (from_chip, from_cross) = give_back(*sums)
        numerator, denominator = call(
            terms_kernel,
            [((CELLS, LANES), F32)] * 2,
            [((128, 128), F32)],
        )(
            head, cond, head_old, alpha, wet, reversal, chip_edges, got[2], got[3], got[4],
            *near, from_chip, row, col,
        )
        if iteration < PICARD - 1:
            head, cond, chip_edge, cross_edge, *sides, weight = call(
                next_kernel, [((CELLS, LANES), F32)] * 2 + [EDGE] * 2 + SIDES, micros=2
            )(from_cross, row, col, numerator, denominator, sat, alpha, wet)
            (cross,) = call(cross_kernel, [MESSAGE])(row, col, weight, cross_edge)
            messages = (chip_edge, cross, *sides, weight)
        else:
            (head,) = call(last_kernel, [((CELLS, LANES), F32)])(
                from_cross, row, col, numerator, denominator
            )
    return (head.reshape(tile), collar.reshape(-1))


def solution(mesh):
    tile, lists, blocks, line = (
        P(None, "gx", "gy"),
        P(("gx", "gy"), None, None),
        P(("gx", "gy"), None),
        P(("gx", "gy")),
    )
    return jax.shard_map(
        on_device,
        mesh=mesh,
        in_specs=(tile,) * 5 + (lists,) * 2 + (blocks,) * 2 + (line,) * 2 + (blocks,) * 2 + (line,),
        out_specs=(tile, line),
        check_vma=False,
    )
```
